256 devices in a mesh: ctx: 128 (over x, y, z_lo, core), mp: 2 (over z_hi).
Axes of the slice: x: 4, y: 4, z: 8 (z_hi: 2, z_lo: 4; z = z_hi * 4 + z_lo), core: 2. Of those that a mesh axis runs over, the one named last changes fastest.
Arguments:
- fine_q: bfloat16 [65536, 2048], P('ctx', 'mp'), may hold values from -10 to 10
- fine_k: bfloat16 [65536, 2048], P('ctx', 'mp'), may hold values from -10 to 10
- fine_v: bfloat16 [65536, 2048], P('ctx', 'mp'), may hold values from -6 to 6
- norm_gain: float32 [2048], P('mp'), may hold values from 0.1 to 1.9
- short_weight: bfloat16 [2048, 4096], P('mp'), may hold values from -0.15467961 to 0.15467961
Outputs:
- final: bfloat16 [65536, 2048], P('ctx', 'mp')
The draws below stay inside these ranges and needn't reach their ends.
All inputs are finite; a program needn't handle non-finite values.
Results may differ from the reference program's by a relative error of at most 0.015.
The reference program's roundings to bfloat16 on the way count: a program that leaves them out, or rounds other values in their place, can miss the bound.
Values may be sent and summed in bfloat16 or wider, within the bound.
No kernel may reach another device: no remote copies, remote signals or barrier semaphores. Data moves between devices by JAX's collectives and lax.ppermute only.
A program may use at most 128 MiB of HBM per device.

```python
import math
import jax
import jax.numpy as jnp
from jax import lax

D_FINE = 2048
HEADS = 16
C_HEADS = 8
C_HEAD = 256
WINDOW = 1024
SHORT = 16
TOKENS = 65536
COARSE = 4096


def draw_fine_q(key, part):
    key = jax.random.fold_in(key, 1)
    return jnp.clip(jax.random.normal(key, (TOKENS, D_FINE), jnp.float32), -6.0, 6.0).astype(jnp.bfloat16)


def draw_fine_k(key, part):
    key = jax.random.fold_in(key, 2)
    return jnp.clip(jax.random.normal(key, (TOKENS, D_FINE), jnp.float32), -6.0, 6.0).astype(jnp.bfloat16)


def draw_short_weight(key, part):
    key = jax.random.fold_in(key, 3)
    columns = 2 * C_HEADS * C_HEAD
    noise = jnp.clip(jax.random.normal(jax.random.fold_in(key, 1), (D_FINE, columns), jnp.float32), -4.0, 4.0)
    row_sign = (2 * jax.random.randint(jax.random.fold_in(key, 2), (D_FINE, 1), 0, 2) - 1).astype(jnp.float32)
    col_sign = (2 * jax.random.randint(jax.random.fold_in(key, 3), (1, columns), 0, 2) - 1).astype(jnp.float32)
    column = jnp.arange(columns, dtype=jnp.int32)
    marked = (column // (2 * C_HEAD) % 4 == 0) & (column % (2 * C_HEAD) < C_HEAD)
    strong = 2.0 * row_sign * col_sign * marked.astype(jnp.float32)[None, :]
    return ((noise + strong) / math.sqrt(D_FINE)).astype(jnp.bfloat16)


def levels(stream_key, extent, pieces, least, largest):
    factor_of = 1.0
    for position, blocks in pieces:
        steps = jax.random.uniform(jax.random.fold_in(jax.random.fold_in(stream_key, 6), position), (blocks,), jnp.float32, least / len(pieces), largest / len(pieces))
        factor_of = factor_of * jnp.repeat(jnp.exp(steps), extent[position] // blocks).reshape((-1,) + (1,) * (len(extent) - 1 - position))
    return factor_of


def scatter_about(key, dims, scale, limit, cuts=(), kind=jnp.bfloat16):
    factor_of = levels(key, dims, cuts, -0.22, 0.18) if cuts else 1.0
    drawn = jax.random.normal(key, dims, jnp.float32) * scale * factor_of
    return jnp.minimum(jnp.maximum(drawn, -limit), limit).astype(kind)


def setup_inputs(seed: int = 0) -> dict:
    key_list = jax.random.split(jax.random.key(seed), 6)
    return {
        "fine_q": draw_fine_q(jax.random.fold_in(key_list[5], 71), 0),
        "fine_k": draw_fine_k(jax.random.fold_in(key_list[5], 71), 0),
        "fine_v": scatter_about(key_list[2], (TOKENS, D_FINE), 1.0, 6.0, ((0, 128), (1, 2))),
        "norm_gain": jnp.clip(1.0 + 0.18 * jax.random.normal(key_list[3], (D_FINE,), jnp.float32), 0.1, 1.9),
        "short_weight": draw_short_weight(jax.random.fold_in(key_list[5], 71), 0),
    }


NEG_FILL = -1e+30

def attend(queries, keys, values, allowed, scale):
    scores = jnp.einsum('qhd,khd->hqk', queries, keys) * scale
    scores = jnp.where(allowed[None], scores, NEG_FILL)
    top = lax.optimization_barrier(jnp.max(scores, -1, keepdims=True))
    probs = jnp.where(allowed[None], jnp.exp(scores - top), 0.0)
    total = lax.optimization_barrier(jnp.sum(probs, -1))
    rounded = lax.optimization_barrier(probs.astype(jnp.bfloat16)).astype(jnp.float32)
    mixed = jnp.einsum('hqk,khd->qhd', rounded, values)
    return mixed / jnp.transpose(total)[:, :, None]

def reference(fine_q, fine_k, fine_v, norm_gain, short_weight):
    head_size = D_FINE // HEADS
    queries = fine_q.astype(jnp.float32).reshape(TOKENS, HEADS, head_size)
    keys = fine_k.astype(jnp.float32).reshape(TOKENS, HEADS, head_size)
    values = fine_v.astype(jnp.float32).reshape(TOKENS, HEADS, head_size)
    front = jnp.zeros((WINDOW, HEADS, head_size), jnp.float32)
    keys_pad = jnp.concatenate([front, keys], 0)
    values_pad = jnp.concatenate([front, values], 0)
    block_rows = min(512, TOKENS)

    def fine_block(block_index):
        first = block_index * block_rows
        q_block = lax.dynamic_slice_in_dim(queries, first, block_rows, 0)
        k_block = lax.dynamic_slice_in_dim(keys_pad, first, block_rows + WINDOW, 0)
        v_block = lax.dynamic_slice_in_dim(values_pad, first, block_rows + WINDOW, 0)
        q_pos = first + jnp.arange(block_rows, dtype=jnp.int32)
        k_pos = first - WINDOW + jnp.arange(block_rows + WINDOW, dtype=jnp.int32)
        allowed = (k_pos[None, :] <= q_pos[:, None]) & (k_pos[None, :] > q_pos[:, None] - WINDOW) & (k_pos[None, :] >= 0)
        return attend(q_block, k_block, v_block, allowed, 1.0 / math.sqrt(head_size)).reshape(block_rows, D_FINE)
    fine_out = lax.map(fine_block, jnp.arange(TOKENS // block_rows, dtype=jnp.int32))
    fine_out = fine_out.reshape(TOKENS, D_FINE).astype(jnp.bfloat16)
    shifted = jnp.concatenate([jnp.zeros((SHORT - 1, D_FINE), jnp.bfloat16), fine_out[:TOKENS - SHORT + 1]], 0)
    pooled = lax.optimization_barrier(jnp.sum(shifted.astype(jnp.float32).reshape(COARSE, SHORT, D_FINE), 1)) / SHORT
    spread = lax.optimization_barrier(jnp.sum(pooled * pooled, -1, keepdims=True)) / D_FINE
    normed = (pooled * lax.rsqrt(spread + 1e-05) * norm_gain.astype(jnp.float32)).astype(jnp.bfloat16)
    coarse_kv = jnp.dot(normed, short_weight, preferred_element_type=jnp.float32).astype(jnp.bfloat16)
    coarse_kv = coarse_kv.reshape(COARSE, C_HEADS, 2, C_HEAD)
    coarse_keys = coarse_kv[:, :, 0, :].astype(jnp.float32)
    coarse_values = coarse_kv[:, :, 1, :].astype(jnp.float32)
    coarse_rows = min(512, COARSE)
    k_pos = jnp.arange(COARSE, dtype=jnp.int32)

    def coarse_block(block_index):
        first = block_index * coarse_rows
        q_block = lax.dynamic_slice_in_dim(coarse_keys, first, coarse_rows, 0)
        q_pos = first + jnp.arange(coarse_rows, dtype=jnp.int32)
        allowed = k_pos[None, :] < jnp.maximum(q_pos, 1)[:, None]
        return attend(q_block, coarse_keys, coarse_values, allowed, 1.0 / math.sqrt(C_HEAD)).reshape(coarse_rows, D_FINE)
    coarse_out = lax.map(coarse_block, jnp.arange(COARSE // coarse_rows, dtype=jnp.int32))
    coarse_out = coarse_out.reshape(COARSE, D_FINE).astype(jnp.bfloat16)
    final = fine_out.astype(jnp.float32).reshape(COARSE, SHORT, D_FINE) + coarse_out.astype(jnp.float32)[:, None, :]
    return final.reshape(TOKENS, D_FINE).astype(jnp.bfloat16)
```

```python
import functools
import math

import jax
import jax.numpy as jnp
from jax import lax
from jax.experimental import pallas as pl
from jax.experimental.pallas import tpu as pltpu
from jax.sharding import Mesh
from jax.sharding import PartitionSpec as P

D_FINE = 2048
HEADS = 16
HEAD = 128
C_HEADS = 8
C_HEAD = 256
WINDOW = 1024
SHORT = 16
EPS = 1e-05
NEG = -1e30
LOG2E = 1.4426950408889634

ROWS = 512
HALF = 1024
LOCAL_HEADS = HALF // HEAD
TILE = 256
BAND = WINDOW + TILE
CROWS = ROWS // SHORT
GROUP = 4 * CROWS
CTX = ("x", "y", "z", "c")
MIB = 1 << 20


def shifted(value, steps):
    count = 128
    return lax.ppermute(
        value, CTX, [(s, s + steps) for s in range(max(0, -steps), min(count, count - steps))]
    )


def rolled(value, axis, steps):
    count = lax.axis_size(axis)
    return lax.ppermute(value, axis, [(s, (s + steps) % count) for s in range(count)])


def probs_kernel(info, q_ref, ka_ref, ks_ref, ko_ref, kc_ref, p_ref, l_ref):
    head = pl.program_id(0)
    index = info[0]
    core = info[1]
    scale = LOG2E / math.sqrt(HEAD)
    kb = jnp.where(core == 0, ks_ref[...], ko_ref[...])
    chunks = [
        ka_ref[0:TILE, :],
        ka_ref[TILE : 2 * TILE, :],
        kb[0:TILE, :],
        kb[TILE : 2 * TILE, :],
        kc_ref[0:TILE, :],
        kc_ref[TILE : 2 * TILE, :],
    ]
    valid = [index >= 2, index >= 2, index >= 1, index >= 1, None, None]
    row = lax.broadcasted_iota(jnp.int32, (TILE, TILE), 0)
    col = lax.broadcasted_iota(jnp.int32, (TILE, TILE), 1)
    lane = lax.broadcasted_iota(jnp.int32, (TILE, 128), 1)
    for tile in range(ROWS // TILE):
        q = q_ref[tile * TILE : (tile + 1) * TILE, :]
        scores = []
        top = None
        for step in range(5):
            chunk = tile + step
            s = lax.dot_general(
                q, chunks[chunk], (((1,), (1,)), ((), ())), preferred_element_type=jnp.float32
            )
            if step == 0:
                s = jnp.where(col > row, s, NEG)
            if step == 4:
                s = jnp.where(col <= row, s, NEG)
            scores.append(s)
            high = jnp.max(s, -1, keepdims=True)
            if valid[chunk] is not None:
                high = jnp.where(valid[chunk], high, NEG)
            top = high if top is None else jnp.maximum(top, high)
        total = jnp.zeros((TILE, 1), jnp.float32)
        for step in range(5):
            chunk = tile + step
            base = top
            if valid[chunk] is not None:
                base = jnp.where(valid[chunk], top, -NEG)
            p = jnp.exp2((scores[step] - base) * scale)
            total = total + jnp.sum(p, -1, keepdims=True)
            p_ref[0, tile, :, step * TILE : (step + 1) * TILE] = p.astype(jnp.bfloat16)
        rows = slice(tile * TILE, (tile + 1) * TILE)
        l_ref[rows, :] = jnp.where(lane == head, total, l_ref[rows, :])


def fine_probs(info, q, ka, ks, ko, kc):
    column = pl.BlockSpec((ROWS, HEAD), lambda h, info: (0, h))
    return pl.pallas_call(
        probs_kernel,
        grid_spec=pltpu.PrefetchScalarGridSpec(
            num_scalar_prefetch=1,
            grid=(LOCAL_HEADS,),
            in_specs=[column] * 5,
            out_specs=[
                pl.BlockSpec((1, 2, TILE, BAND), lambda h, info: (h, 0, 0, 0)),
                pl.BlockSpec((ROWS, 128), lambda h, info: (0, 0)),
            ],
        ),
        out_shape=[
            jax.ShapeDtypeStruct((LOCAL_HEADS, 2, TILE, BAND), jnp.bfloat16),
            jax.ShapeDtypeStruct((ROWS, 128), jnp.float32),
        ],
        compiler_params=pltpu.CompilerParams(vmem_limit_bytes=32 * MIB),
        cost_estimate=pl.CostEstimate(
            flops=2 * LOCAL_HEADS * ROWS * BAND * HEAD,
            bytes_accessed=16 * MIB,
            transcendentals=LOCAL_HEADS * ROWS * BAND,
        ),
        name="fine_probs",
    )(info, q, ka, ks, ko, kc)


def mix_kernel(info, p_ref, l_ref, va_ref, vs_ref, vo_ref, vc_ref, out_ref, pool_ref, v_ref):
    head = pl.program_id(0)
    core = info[1]
    v_ref[0:ROWS, :] = va_ref[...]
    v_ref[ROWS : 2 * ROWS, :] = jnp.where(core == 0, vs_ref[...], vo_ref[...])
    v_ref[2 * ROWS : 3 * ROWS, :] = vc_ref[...]
    lane = lax.broadcasted_iota(jnp.int32, (TILE, 128), 1)
    pooled = jnp.zeros((40, HEAD), jnp.float32)
    for tile in range(ROWS // TILE):
        rows = slice(tile * TILE, (tile + 1) * TILE)
        total = jnp.sum(jnp.where(lane == head, l_ref[rows, :], 0.0), -1, keepdims=True)
        mixed = jnp.dot(
            p_ref[0, tile], v_ref[tile * TILE : tile * TILE + BAND, :],
            preferred_element_type=jnp.float32,
        )
        out = (mixed / total).astype(jnp.bfloat16)
        out_ref[rows, :] = out
        j = lax.broadcasted_iota(jnp.int32, (40, TILE), 0)
        r = lax.broadcasted_iota(jnp.int32, (40, TILE), 1) + tile * TILE
        pick = jnp.where((r > SHORT * j - SHORT) & (r <= SHORT * j), 1.0, 0.0)
        pooled = pooled + jnp.dot(
            pick.astype(jnp.bfloat16), out, preferred_element_type=jnp.float32
        )
    pool_ref[...] = pooled


def fine_mix(info, p, l, va, vs, vo, vc):
    column = pl.BlockSpec((ROWS, HEAD), lambda h, info: (0, h))
    return pl.pallas_call(
        mix_kernel,
        grid_spec=pltpu.PrefetchScalarGridSpec(
            num_scalar_prefetch=1,
            grid=(LOCAL_HEADS,),
            in_specs=[
                pl.BlockSpec((1, 2, TILE, BAND), lambda h, info: (h, 0, 0, 0)),
                pl.BlockSpec((ROWS, 128), lambda h, info: (0, 0)),
            ]
            + [column] * 4,
            out_specs=[column, pl.BlockSpec((40, HEAD), lambda h, info: (0, h))],
            scratch_shapes=[pltpu.VMEM((3 * ROWS, HEAD), jnp.bfloat16)],
        ),
        out_shape=[
            jax.ShapeDtypeStruct((ROWS, HALF), jnp.bfloat16),
            jax.ShapeDtypeStruct((40, HALF), jnp.float32),
        ],
        compiler_params=pltpu.CompilerParams(vmem_limit_bytes=32 * MIB),
        cost_estimate=pl.CostEstimate(
            flops=2 * LOCAL_HEADS * ROWS * BAND * HEAD,
            bytes_accessed=16 * MIB,
            transcendentals=0,
        ),
        name="fine_mix",
    )(info, p, l, va, vs, vo, vc)


def short_kernel(pooled_ref, spread_ref, gain_ref, w_ref, out_ref):
    factor = lax.rsqrt(spread_ref[...] / D_FINE + EPS)
    normed = (pooled_ref[...] * factor[:, 0:1] * gain_ref[...]).astype(jnp.bfloat16)
    out_ref[0] = jnp.dot(normed, w_ref[...], preferred_element_type=jnp.float32)


def shorten(pooled, spread, gain, weight):
    return pl.pallas_call(
        short_kernel,
        grid=(C_HEADS,),
        in_specs=[
            pl.BlockSpec((CROWS, HALF), lambda j: (0, 0)),
            pl.BlockSpec((CROWS, 128), lambda j: (0, 0)),
            pl.BlockSpec((1, HALF), lambda j: (0, 0)),
            pl.BlockSpec((HALF, 2 * C_HEAD), lambda j: (0, (j % 2) * 4 + j // 2)),
        ],
        out_specs=pl.BlockSpec((1, CROWS, 2 * C_HEAD), lambda j: (j, 0, 0)),
        out_shape=jax.ShapeDtypeStruct((C_HEADS, CROWS, 2 * C_HEAD), jnp.float32),
        compiler_params=pltpu.CompilerParams(vmem_limit_bytes=32 * MIB),
        cost_estimate=pl.CostEstimate(
            flops=2 * CROWS * HALF * 4096, bytes_accessed=9 * MIB, transcendentals=0
        ),
        name="shorten",
    )(pooled, spread, gain, weight)


def split3(value):
    first = value.astype(jnp.bfloat16).astype(jnp.float32)
    rest = value - first
    second = rest.astype(jnp.bfloat16).astype(jnp.float32)
    return first, second, rest - second


def coarse_kernel(info, *refs):
    q_refs, kv_refs, out_ref, kv_all = refs[0:4], refs[4:12], refs[12], refs[13]
    x, z, c = info[2], info[4], info[1]
    scale = 1.0 / math.sqrt(C_HEAD)
    keys = 8 * GROUP
    for piece in range(8):
        kv_all[piece * GROUP : (piece + 1) * GROUP, :] = kv_refs[piece][...]
    slot = lax.broadcasted_iota(jnp.int32, (1, keys), 1)
    piece = slot // GROUP
    inside = slot % GROUP
    from_x = (x - piece // 2 + 4) % 4
    from_c = jnp.where(piece % 2 == 0, c, 1 - c)
    key_pos = (
        from_x * 1024 + (inside // CROWS) * 256 + z * 64 + from_c * 32 + inside % CROWS
    )
    inner = lax.broadcasted_iota(jnp.int32, (GROUP, 1), 0)
    lane = lax.broadcasted_iota(jnp.int32, (GROUP, 128), 1)
    for k in range(4):
        from_z = (z - k + 4) % 4
        pos = x * 1024 + (inner // CROWS) * 256 + from_z * 64 + c * 32 + inner % CROWS
        allowed = key_pos < jnp.maximum(pos, 1)
        s = lax.dot_general(
            q_refs[k][...], kv_all[:, 0:C_HEAD], (((1,), (1,)), ((), ())),
            preferred_element_type=jnp.float32,
        ) * scale
        s = jnp.where(allowed, s, NEG)
        top = jnp.max(s, -1, keepdims=True)
        p = jnp.where(allowed, jnp.exp(s - top), 0.0)
        total = jnp.sum(p, -1, keepdims=True)
        mixed = jnp.dot(
            p.astype(jnp.bfloat16), kv_all[:, C_HEAD : 2 * C_HEAD],
            preferred_element_type=jnp.float32,
        )
        some = total > 0.0
        safe = jnp.where(some, total, 1.0)
        mixed = jnp.where(some, mixed / safe, 0.0)
        level = jnp.where(some, top + jnp.log(safe), NEG)
        a, b, d = split3(level)
        extra = jnp.where(lane == 0, a, jnp.where(lane == 1, b, jnp.where(lane == 2, d, 0.0)))
        for y in range(4):
            rows = slice(y * CROWS, (y + 1) * CROWS)
            out_ref[y * 4 + from_z, :, 0:C_HEAD] = mixed[rows, :].astype(jnp.bfloat16)
            out_ref[y * 4 + from_z, :, C_HEAD : C_HEAD + 128] = extra[rows, :].astype(
                jnp.bfloat16
            )


def coarse_attend(info, queries, pairs):
    whole = pl.BlockSpec(memory_space=pltpu.VMEM)
    return pl.pallas_call(
        coarse_kernel,
        in_specs=[pl.BlockSpec(memory_space=pltpu.SMEM)] + [whole] * 12,
        out_specs=whole,
        out_shape=jax.ShapeDtypeStruct((16, CROWS, C_HEAD + 128), jnp.bfloat16),
        scratch_shapes=[pltpu.VMEM((8 * GROUP, 2 * C_HEAD), jnp.bfloat16)],
        compiler_params=pltpu.CompilerParams(vmem_limit_bytes=32 * MIB),
        cost_estimate=pl.CostEstimate(
            flops=4 * 4 * GROUP * 8 * GROUP * C_HEAD,
            bytes_accessed=2 * MIB,
            transcendentals=4 * GROUP * 8 * GROUP,
        ),
        name="coarse_attend",
    )(info, *queries, *pairs)


def final_kernel(part_ref, fine_ref, out_ref):
    parts = part_ref[...].astype(jnp.float32)
    levels = jnp.sum(parts[:, :, C_HEAD : C_HEAD + 128], -1, keepdims=True)
    top = jnp.max(levels, 0, keepdims=True)
    weights = jnp.exp(levels - top)
    total = jnp.sum(weights, 0)
    mixed = jnp.sum(parts[:, :, 0:C_HEAD] * weights, 0) / total
    coarse = mixed.astype(jnp.bfloat16)
    r = lax.broadcasted_iota(jnp.int32, (ROWS, CROWS), 0)
    j = lax.broadcasted_iota(jnp.int32, (ROWS, CROWS), 1)
    spread = jnp.where(r // SHORT == j, 1.0, 0.0).astype(jnp.bfloat16)
    up = jnp.dot(spread, coarse, preferred_element_type=jnp.float32)
    out_ref[...] = (fine_ref[...].astype(jnp.float32) + up).astype(jnp.bfloat16)


def finish(parts, fine):
    column = pl.BlockSpec((ROWS, C_HEAD), lambda h: (0, h))
    return pl.pallas_call(
        final_kernel,
        grid=(4,),
        in_specs=[pl.BlockSpec((4, CROWS, C_HEAD + 128), lambda h: (h, 0, 0)), column],
        out_specs=column,
        out_shape=jax.ShapeDtypeStruct((ROWS, HALF), jnp.bfloat16),
        compiler_params=pltpu.CompilerParams(vmem_limit_bytes=32 * MIB),
        name="finish",
    )(parts, fine)


def per_device(fine_q, fine_k, fine_v, norm_gain, short_weight):
    x, y, z, c = (lax.axis_index(a) for a in CTX)
    index = ((x * 4 + y) * 4 + z) * 2 + c
    info = jnp.stack([index, c, x, y, z]).astype(jnp.int32)

    k2 = shifted(fine_k, 2)
    v2 = shifted(fine_v, 2)
    ko = rolled(fine_k, "c", 1)
    vo = rolled(fine_v, "c", 1)
    ks = rolled(k2, "c", 1)
    vs = rolled(v2, "c", 1)
    p, l = fine_probs(info, fine_q, k2, ks, ko, fine_k)
    fine_out, sums = fine_mix(info, p, l, v2, vs, vo, fine_v)

    tail = shifted(sums[CROWS : CROWS + 8], 1)
    pooled = (sums[:CROWS] + jnp.pad(tail[0:1], ((0, CROWS - 1), (0, 0)))) / SHORT
    spread = lax.psum(jnp.sum(pooled * pooled, -1), "m")
    spread = jnp.broadcast_to(spread[:, None], (CROWS, 128))
    partial_kv = shorten(pooled, spread, norm_gain[None], short_weight)
    swapped = lax.all_to_all(partial_kv, ("y", "m"), split_axis=0, concat_axis=0, tiled=True)
    swapped = swapped.reshape(4, 2, CROWS, 2 * C_HEAD)
    kv = (swapped[:, 0] + swapped[:, 1]).astype(jnp.bfloat16).reshape(GROUP, 2 * C_HEAD)

    own_keys = kv[:, :C_HEAD]
    queries = [own_keys] + [rolled(own_keys, "z", k) for k in (1, 2, 3)]
    along = [kv] + [rolled(kv, "x", k) for k in (1, 2, 3)]
    pairs = []
    for piece in along:
        pairs += [piece, rolled(piece, "c", 1)]
    parts = coarse_attend(info, queries, pairs)
    parts = lax.all_to_all(parts, ("y", "z"), split_axis=0, concat_axis=0, tiled=True)
    return finish(parts, fine_out)


def solution(mesh):
    grid = Mesh(mesh.devices.reshape(4, 4, 4, 2, 2), ("x", "y", "z", "c", "m"))
    rows = P(CTX, "m")
    return jax.shard_map(
        per_device,
        mesh=grid,
        in_specs=(rows, rows, rows, P("m"), P("m", None)),
        out_specs=rows,
        check_vma=False,
    )
```

```python
import functools
import math

import jax
import jax.numpy as jnp
from jax import lax
from jax.experimental import pallas as pl
from jax.experimental.pallas import tpu as pltpu
from jax.sharding import Mesh
from jax.sharding import PartitionSpec as P

D_FINE = 2048
HEADS = 16
HEAD = 128
C_HEADS = 8
C_HEAD = 256
WINDOW = 1024
SHORT = 16
EPS = 1e-05
NEG = -1e30
LOG2E = 1.4426950408889634

ROWS = 512
HALF = 1024
LOCAL_HEADS = HALF // HEAD
TILE = 256
BAND = WINDOW + TILE
CROWS = ROWS // SHORT
GROUP = 4 * CROWS
SMALL = pl.CostEstimate(flops=1, bytes_accessed=1, transcendentals=0)
CTX = ("x", "y", "z", "c")
MIB = 1 << 20
LIMIT = 44 * MIB
FIRST_HEADS = 6
TAIL = 128 + 2 * ROWS
SENT = 3 * C_HEAD


def shifted(value, steps):
    count = 128
    return lax.ppermute(
        value, CTX, [(s, s + steps) for s in range(max(0, -steps), min(count, count - steps))]
    )


def rolled(value, axis, steps):
    count = lax.axis_size(axis)
    return lax.ppermute(value, axis, [(s, (s + steps) % count) for s in range(count)])


def swapped(value, count):
    size = value.shape[0] // count
    return [rolled(value[i * size : (i + 1) * size], "c", 1) for i in range(count)]


def across(value, steps, other):
    pairs = [(x * 2 + c, (x + steps) % 4 * 2 + (c + other) % 2) for x in range(4) for c in (0, 1)]
    return lax.ppermute(value, ("x", "c"), pairs)


def attend(q, pieces, store):
    scale = LOG2E / math.sqrt(HEAD)
    scores = []
    top = None
    for keys, okay, mask in pieces:
        s = lax.dot_general(
            q, keys, (((1,), (1,)), ((), ())), preferred_element_type=jnp.float32
        )
        if mask is not None:
            s = jnp.where(mask, s, NEG)
        scores.append(s)
        high = jnp.max(s, -1, keepdims=True)
        if okay is not None:
            high = jnp.where(okay, high, NEG)
        top = high if top is None else jnp.maximum(top, high)
    total = jnp.zeros((q.shape[0], 1), jnp.float32)
    for step, (keys, okay, mask) in enumerate(pieces):
        base = top if okay is None else jnp.where(okay, top, -NEG)
        p = jnp.exp2((scores[step] - base) * scale)
        total = total + jnp.sum(p, -1, keepdims=True)
        store(step, p.astype(jnp.bfloat16))
    return total


def probs_kernel(info, q_ref, ka_ref, ko_ref, kc_ref, *refs):
    ks_refs, (p_ref, l_ref) = refs[:-2], refs[-2:]
    head = pl.program_id(0)
    index = info[0]
    core = info[1]
    kb = jnp.where(core == 0, jnp.concatenate([r[...] for r in ks_refs], 0), ko_ref[...])
    chunks = [
        ka_ref[0:TILE, :],
        ka_ref[TILE : 2 * TILE, :],
        kb[0:TILE, :],
        kb[TILE : 2 * TILE, :],
        kc_ref[0:TILE, :],
        kc_ref[TILE : 2 * TILE, :],
    ]
    valid = [index >= 2, index >= 2, index >= 1, index >= 1, None, None]
    row = lax.broadcasted_iota(jnp.int32, (TILE, TILE), 0)
    col = lax.broadcasted_iota(jnp.int32, (TILE, TILE), 1)
    lane = lax.broadcasted_iota(jnp.int32, (TILE, 128), 1)

    for tile in range(ROWS // TILE):
        masks = [col > row, None, None, None, col <= row]
        pieces = [(chunks[tile + j], valid[tile + j], masks[j]) for j in range(5)]

        def store(step, p, tile=tile):
            p_ref[0, tile, :, step * TILE : (step + 1) * TILE] = p

        rows = slice(tile * TILE, (tile + 1) * TILE)
        total = attend(q_ref[rows, :], pieces, store)
        l_ref[rows, :] = jnp.where(lane == head, total, l_ref[rows, :])


def tail_kernel(info, _, ka_ref, ko_ref, qt_ref, kt_ref, *refs):
    ks_refs, (pt_ref, lt_ref) = refs[:-2], refs[-2:]
    head = pl.program_id(0)
    index = info[0]
    core = info[1]
    kb = jnp.where(core == 0, jnp.concatenate([r[...] for r in ks_refs], 0), ko_ref[...])
    r16 = lax.broadcasted_iota(jnp.int32, (SHORT, 128), 0)
    c16 = lax.broadcasted_iota(jnp.int32, (SHORT, 128), 1)
    r512 = lax.broadcasted_iota(jnp.int32, (SHORT, ROWS), 0)
    c512 = lax.broadcasted_iota(jnp.int32, (SHORT, ROWS), 1)
    first = jnp.concatenate([kt_ref[...], jnp.zeros((128 - SHORT, HEAD), jnp.bfloat16)], 0)
    pieces = [
        (first, index >= 3, (c16 > r16) & (c16 < SHORT)),
        (ka_ref[...], index >= 2, None),
        (kb, index >= 1, c512 <= r512 + (ROWS - SHORT)),
    ]
    places = [(0, 128), (128, 128 + ROWS), (128 + ROWS, 128 + 2 * ROWS)]

    def store_tail(step, p):
        pt_ref[0, :, places[step][0] : places[step][1]] = p

    total = attend(qt_ref[...], pieces, store_tail)
    lt_ref[...] = jnp.where(c16 == head, total, lt_ref[...])


def fine_probs(info, q, ka, ks, ko, kc):
    column = pl.BlockSpec((ROWS, HEAD), lambda h, info: (0, h))
    piece = pl.BlockSpec((ROWS // len(ks), HEAD), lambda h, info: (0, h))
    return pl.pallas_call(
        probs_kernel,
        grid_spec=pltpu.PrefetchScalarGridSpec(
            num_scalar_prefetch=1,
            grid=(LOCAL_HEADS,),
            in_specs=[column] * 4 + [piece] * len(ks),
            out_specs=[
                pl.BlockSpec((1, 2, TILE, BAND), lambda h, info: (h, 0, 0, 0)),
                pl.BlockSpec((ROWS, 128), lambda h, info: (0, 0)),
            ],
        ),
        out_shape=[
            jax.ShapeDtypeStruct((LOCAL_HEADS, 2, TILE, BAND), jnp.bfloat16),
            jax.ShapeDtypeStruct((ROWS, 128), jnp.float32),
        ],
        compiler_params=pltpu.CompilerParams(vmem_limit_bytes=LIMIT),
        cost_estimate=SMALL,
        name="fine_probs",
    )(info, q, ka, ko, kc, *ks)


def tail_probs(info, after, ka, ks, ko, qt, kvt):
    column = pl.BlockSpec((ROWS, HEAD), lambda h, info: (0, h))
    small = pl.BlockSpec((SHORT, HEAD), lambda h, info: (0, h))
    piece = pl.BlockSpec((ROWS // len(ks), HEAD), lambda h, info: (0, h))
    return pl.pallas_call(
        tail_kernel,
        grid_spec=pltpu.PrefetchScalarGridSpec(
            num_scalar_prefetch=1,
            grid=(LOCAL_HEADS,),
            in_specs=[pl.BlockSpec(memory_space=pl.ANY)]
            + [column] * 2
            + [small] * 2
            + [piece] * len(ks),
            out_specs=[
                pl.BlockSpec((1, SHORT, TAIL), lambda h, info: (h, 0, 0)),
                pl.BlockSpec((SHORT, 128), lambda h, info: (0, 0)),
            ],
        ),
        out_shape=[
            jax.ShapeDtypeStruct((LOCAL_HEADS, SHORT, TAIL), jnp.bfloat16),
            jax.ShapeDtypeStruct((SHORT, 128), jnp.float32),
        ],
        compiler_params=pltpu.CompilerParams(vmem_limit_bytes=LIMIT),
        cost_estimate=SMALL,
        name="tail_probs",
    )(info, after, ka, ko, qt, kvt, *ks)


def mix_kernel(
    second, pieces, info, p_ref, l_ref, pt_ref, lt_ref, va_ref, vo_ref, vc_ref, vt_ref, *refs
):
    vs_refs, refs = refs[:pieces], refs[pieces:]
    if second:
        before_ref, _, _, out_ref, pool_ref, square_ref, v_ref, s_ref = refs
    else:
        out_ref, pool_ref, square_ref, v_ref, s_ref = refs
    step = pl.program_id(0)
    head = step + (FIRST_HEADS if second else 0)
    core = info[1]

    @pl.when(step == 0)
    def _():
        s_ref[...] = before_ref[...] if second else jnp.zeros_like(s_ref)

    v_ref[0:SHORT, :] = vt_ref[...]
    v_ref[SHORT:128, :] = jnp.zeros((128 - SHORT, HEAD), jnp.bfloat16)
    v_ref[128 : 128 + ROWS, :] = va_ref[...]
    v_ref[128 + ROWS : 128 + 2 * ROWS, :] = jnp.where(
        core == 0, jnp.concatenate([r[...] for r in vs_refs], 0), vo_ref[...]
    )
    v_ref[128 + 2 * ROWS : 128 + 3 * ROWS, :] = vc_ref[...]

    lane = lax.broadcasted_iota(jnp.int32, (TILE, 128), 1)
    lane16 = lax.broadcasted_iota(jnp.int32, (SHORT, 128), 1)
    total = jnp.sum(jnp.where(lane16 == head, lt_ref[...], 0.0), -1, keepdims=True)
    mixed = jnp.dot(pt_ref[0], v_ref[0:TAIL, :], preferred_element_type=jnp.float32)
    some = total > 0.0
    tail = jnp.where(some, mixed / jnp.where(some, total, 1.0), 0.0).astype(jnp.bfloat16)
    j = lax.broadcasted_iota(jnp.int32, (CROWS, SHORT), 0)
    r = lax.broadcasted_iota(jnp.int32, (CROWS, SHORT), 1)
    pick = jnp.where((j == 0) & (r > 0), 1.0, 0.0).astype(jnp.bfloat16)
    pooled = jnp.dot(pick, tail, preferred_element_type=jnp.float32)
    for tile in range(ROWS // TILE):
        rows = slice(tile * TILE, (tile + 1) * TILE)
        total = jnp.sum(jnp.where(lane == head, l_ref[rows, :], 0.0), -1, keepdims=True)
        mixed = jnp.dot(
            p_ref[0, tile],
            v_ref[128 + tile * TILE : 128 + tile * TILE + BAND, :],
            preferred_element_type=jnp.float32,
        )
        out = (mixed / total).astype(jnp.bfloat16)
        out_ref[rows, :] = out
        j = lax.broadcasted_iota(jnp.int32, (CROWS, TILE), 0)
        r = lax.broadcasted_iota(jnp.int32, (CROWS, TILE), 1) + tile * TILE
        pick = jnp.where((r > SHORT * j - SHORT) & (r <= SHORT * j), 1.0, 0.0)
        pooled = pooled + jnp.dot(
            pick.astype(jnp.bfloat16), out, preferred_element_type=jnp.float32
        )
    pooled = pooled * (1.0 / SHORT)
    pool_ref[...] = pooled
    s_ref[...] = s_ref[...] + pooled * pooled

    @pl.when(step == pl.num_programs(0) - 1)
    def _():
        if second:
            square_ref[...] = jnp.broadcast_to(
                jnp.sum(s_ref[...], -1, keepdims=True), (CROWS, 128)
            )
        else:
            square_ref[...] = s_ref[...]


def fine_mix(second, info, p, l, pt, lt, va, vs, vo, vc, kvt, *before):
    off = FIRST_HEADS if second else 0
    near = pl.BlockSpec((ROWS, HEAD), lambda h, info: (0, h))
    far = pl.BlockSpec((ROWS, HEAD), lambda h, info: (0, h + off))
    whole = lambda *shape: pl.BlockSpec(shape, lambda h, info: (0,) * len(shape))
    anywhere = pl.BlockSpec(memory_space=pl.ANY)
    in_specs = [
        pl.BlockSpec((1, 2, TILE, BAND), lambda h, info: (h + off, 0, 0, 0)),
        whole(ROWS, 128),
        pl.BlockSpec((1, SHORT, TAIL), lambda h, info: (h + off, 0, 0)),
        whole(SHORT, 128),
        near,
        far,
        far,
        pl.BlockSpec((SHORT, HEAD), lambda h, info: (1, h + off)),
    ]
    in_specs += [pl.BlockSpec((ROWS // len(vs), HEAD), lambda h, info: (0, h))] * len(vs)
    aliases = {}
    if second:
        in_specs += [whole(CROWS, 128), anywhere, anywhere]
        aliases = {len(in_specs) - 1: 0, len(in_specs): 1}
    return pl.pallas_call(
        functools.partial(mix_kernel, second, len(vs)),
        grid_spec=pltpu.PrefetchScalarGridSpec(
            num_scalar_prefetch=1,
            grid=(LOCAL_HEADS - FIRST_HEADS if second else FIRST_HEADS,),
            in_specs=in_specs,
            out_specs=[
                far,
                pl.BlockSpec((CROWS, HEAD), lambda h, info: (0, h + off)),
                whole(CROWS, 128),
            ],
            scratch_shapes=[
                pltpu.VMEM((128 + 3 * ROWS, HEAD), jnp.bfloat16),
                pltpu.VMEM((CROWS, 128), jnp.float32),
            ],
        ),
        out_shape=[
            jax.ShapeDtypeStruct((ROWS, HALF), jnp.bfloat16),
            jax.ShapeDtypeStruct((CROWS, HALF), jnp.float32),
            jax.ShapeDtypeStruct((CROWS, 128), jnp.float32),
        ],
        input_output_aliases=aliases,
        compiler_params=pltpu.CompilerParams(vmem_limit_bytes=LIMIT),
        cost_estimate=SMALL,
        name="fine_mix",
    )(info, p, l, pt, lt, va, vo, vc, kvt, *vs, *before)


def short_kernel(pooled_ref, own_ref, other_ref, gain_ref, w_ref, out_ref):
    factor = lax.rsqrt((own_ref[:, 0:1] + other_ref[:, 0:1]) / D_FINE + EPS)
    normed = (pooled_ref[...] * factor * gain_ref[...]).astype(jnp.bfloat16)
    part = jnp.dot(normed, w_ref[...], preferred_element_type=jnp.float32)
    keys = part[:, 0:C_HEAD]
    high = keys.astype(jnp.bfloat16)
    out_ref[0, :, 0:C_HEAD] = high
    out_ref[0, :, C_HEAD : 2 * C_HEAD] = (keys - high.astype(jnp.float32)).astype(jnp.bfloat16)
    out_ref[0, :, 2 * C_HEAD : SENT] = part[:, C_HEAD : 2 * C_HEAD].astype(jnp.bfloat16)


def shorten(pooled, own, other, gain, weight):
    return pl.pallas_call(
        short_kernel,
        grid=(C_HEADS,),
        in_specs=[
            pl.BlockSpec((CROWS, HALF), lambda j: (0, 0)),
            pl.BlockSpec((CROWS, 128), lambda j: (0, 0)),
            pl.BlockSpec((CROWS, 128), lambda j: (0, 0)),
            pl.BlockSpec((1, HALF), lambda j: (0, 0)),
            pl.BlockSpec((HALF, 2 * C_HEAD), lambda j: (0, (j % 2) * 4 + j // 2)),
        ],
        out_specs=pl.BlockSpec((1, CROWS, SENT), lambda j: (j, 0, 0)),
        out_shape=jax.ShapeDtypeStruct((C_HEADS, CROWS, SENT), jnp.bfloat16),
        compiler_params=pltpu.CompilerParams(vmem_limit_bytes=LIMIT),
        cost_estimate=SMALL,
        name="shorten",
    )(pooled, own, other, gain, weight)


def join_kernel(got_ref, kv_ref, key_ref):
    for y in range(4):
        one = got_ref[2 * y].astype(jnp.float32)
        two = got_ref[2 * y + 1].astype(jnp.float32)
        both = one + two
        keys = both[:, 0:C_HEAD] + both[:, C_HEAD : 2 * C_HEAD]
        values = both[:, 2 * C_HEAD : SENT]
        rows = slice(y * CROWS, (y + 1) * CROWS)
        kv_ref[rows, 0:C_HEAD] = keys.astype(jnp.bfloat16)
        kv_ref[rows, C_HEAD : 2 * C_HEAD] = values.astype(jnp.bfloat16)
        key_ref[rows, :] = keys.astype(jnp.bfloat16)


def join(got):
    whole = pl.BlockSpec(memory_space=pltpu.VMEM)
    return pl.pallas_call(
        join_kernel,
        in_specs=[whole],
        out_specs=[whole, whole],
        out_shape=[
            jax.ShapeDtypeStruct((GROUP, 2 * C_HEAD), jnp.bfloat16),
            jax.ShapeDtypeStruct((GROUP, C_HEAD), jnp.bfloat16),
        ],
        name="join",
    )(got)


def split3(value):
    first = value.astype(jnp.bfloat16).astype(jnp.float32)
    rest = value - first
    second = rest.astype(jnp.bfloat16).astype(jnp.float32)
    return first, second, rest - second


def coarse_kernel(info, *refs):
    q_refs, kv_refs, out_ref, kv_all = refs[0:4], refs[4:12], refs[12], refs[13]
    x, z, c = info[2], info[4], info[1]
    scale = 1.0 / math.sqrt(C_HEAD)
    keys = 8 * GROUP
    for piece in range(8):
        kv_all[piece * GROUP : (piece + 1) * GROUP, :] = kv_refs[piece][...]
    slot = lax.broadcasted_iota(jnp.int32, (1, keys), 1)
    piece = slot // GROUP
    inside = slot % GROUP
    from_x = (x - piece // 2 + 4) % 4
    from_c = jnp.where(piece % 2 == 0, c, 1 - c)
    key_pos = (
        from_x * 1024 + (inside // CROWS) * 256 + z * 64 + from_c * 32 + inside % CROWS
    )
    inner = lax.broadcasted_iota(jnp.int32, (GROUP, 1), 0)
    lane = lax.broadcasted_iota(jnp.int32, (GROUP, 128), 1)
    for k in range(4):
        from_z = (z - k + 4) % 4
        pos = x * 1024 + (inner // CROWS) * 256 + from_z * 64 + c * 32 + inner % CROWS
        allowed = key_pos < jnp.maximum(pos, 1)
        s = lax.dot_general(
            q_refs[k][...], kv_all[:, 0:C_HEAD], (((1,), (1,)), ((), ())),
            preferred_element_type=jnp.float32,
        ) * scale
        s = jnp.where(allowed, s, NEG)
        top = jnp.max(s, -1, keepdims=True)
        p = jnp.where(allowed, jnp.exp(s - top), 0.0)
        total = jnp.sum(p, -1, keepdims=True)
        mixed = jnp.dot(
            p.astype(jnp.bfloat16), kv_all[:, C_HEAD : 2 * C_HEAD],
            preferred_element_type=jnp.float32,
        )
        some = total > 0.0
        safe = jnp.where(some, total, 1.0)
        mixed = jnp.where(some, mixed / safe, 0.0)
        level = jnp.where(some, top + jnp.log(safe), NEG)
        a, b, d = split3(level)
        extra = jnp.where(lane == 0, a, jnp.where(lane == 1, b, jnp.where(lane == 2, d, 0.0)))
        for y in range(4):
            rows = slice(y * CROWS, (y + 1) * CROWS)
            out_ref[y * 4 + from_z, :, 0:C_HEAD] = mixed[rows, :].astype(jnp.bfloat16)
            out_ref[y * 4 + from_z, :, C_HEAD : C_HEAD + 128] = extra[rows, :].astype(
                jnp.bfloat16
            )


def coarse_attend(info, queries, pairs):
    whole = pl.BlockSpec(memory_space=pltpu.VMEM)
    return pl.pallas_call(
        coarse_kernel,
        in_specs=[pl.BlockSpec(memory_space=pltpu.SMEM)] + [whole] * 12,
        out_specs=whole,
        out_shape=jax.ShapeDtypeStruct((16, CROWS, C_HEAD + 128), jnp.bfloat16),
        scratch_shapes=[pltpu.VMEM((8 * GROUP, 2 * C_HEAD), jnp.bfloat16)],
        compiler_params=pltpu.CompilerParams(vmem_limit_bytes=32 * MIB),
        cost_estimate=pl.CostEstimate(
            flops=4 * 4 * GROUP * 8 * GROUP * C_HEAD,
            bytes_accessed=2 * MIB,
            transcendentals=4 * GROUP * 8 * GROUP,
        ),
        name="coarse_attend",
    )(info, *queries, *pairs)


def final_kernel(part_ref, fine_ref, out_ref):
    parts = part_ref[...].astype(jnp.float32)
    levels = jnp.sum(parts[:, :, C_HEAD : C_HEAD + 128], -1, keepdims=True)
    top = jnp.max(levels, 0, keepdims=True)
    weights = jnp.exp(levels - top)
    total = jnp.sum(weights, 0)
    mixed = jnp.sum(parts[:, :, 0:C_HEAD] * weights, 0) / total
    coarse = mixed.astype(jnp.bfloat16)
    r = lax.broadcasted_iota(jnp.int32, (ROWS, CROWS), 0)
    j = lax.broadcasted_iota(jnp.int32, (ROWS, CROWS), 1)
    spread = jnp.where(r // SHORT == j, 1.0, 0.0).astype(jnp.bfloat16)
    up = jnp.dot(spread, coarse, preferred_element_type=jnp.float32)
    out_ref[...] = (fine_ref[...].astype(jnp.float32) + up).astype(jnp.bfloat16)


def finish(parts, fine):
    column = pl.BlockSpec((ROWS, C_HEAD), lambda h: (0, h))
    return pl.pallas_call(
        final_kernel,
        grid=(4,),
        in_specs=[pl.BlockSpec((4, CROWS, C_HEAD + 128), lambda h: (h, 0, 0)), column],
        out_specs=column,
        out_shape=jax.ShapeDtypeStruct((ROWS, HALF), jnp.bfloat16),
        compiler_params=pltpu.CompilerParams(vmem_limit_bytes=32 * MIB),
        name="finish",
    )(parts, fine)


def per_device(fine_q, fine_k, fine_v, norm_gain, short_weight):
    x, y, z, c = (lax.axis_index(a) for a in CTX)
    index = ((x * 4 + y) * 4 + z) * 2 + c
    info = jnp.stack([index, c, x, y, z]).astype(jnp.int32)

    k2 = shifted(fine_k, 2)
    ko = rolled(fine_k, "c", 1)
    ks = swapped(k2, 4)
    qt = shifted(fine_q[ROWS - SHORT :], 1)
    kvt = shifted(jnp.concatenate([fine_k[ROWS - SHORT :], fine_v[ROWS - SHORT :]], 0), 3)
    v2a = shifted(fine_v[:, : FIRST_HEADS * HEAD], 2)
    v2b = shifted(fine_v[:, FIRST_HEADS * HEAD :], 2)
    vo = rolled(fine_v, "c", 1)
    p, l = fine_probs(info, fine_q, k2, ks, ko, fine_k)
    pt, lt = tail_probs(info, l, k2, ks, ko, qt, kvt)
    v2a, lt = lax.optimization_barrier((v2a, lt))
    vsa = swapped(v2a, 2)
    fine_out, pooled, squares = fine_mix(
        False, info, p, l, pt, lt, v2a, vsa, vo, fine_v, kvt
    )
    v2b, squares = lax.optimization_barrier((v2b, squares))
    vsb = swapped(v2b, 1)
    fine_out, pooled, squares = fine_mix(
        True, info, p, l, pt, lt, v2b, vsb, vo, fine_v, kvt, squares, fine_out, pooled
    )
    other = rolled(squares, "m", 1)
    sent = shorten(pooled, squares, other, norm_gain[None], short_weight)

    got = lax.all_to_all(sent, ("y", "m"), split_axis=0, concat_axis=0, tiled=True)
    kv, own_keys = join(got)
    pairs = [kv, rolled(kv, "c", 1)]
    for k in (1, 2, 3):
        pairs += [across(kv, k, 0), across(kv, k, 1)]
    queries = [own_keys] + [rolled(own_keys, "z", k) for k in (1, 2, 3)]
    parts = coarse_attend(info, queries, pairs)
    parts = lax.all_to_all(parts, ("y", "z"), split_axis=0, concat_axis=0, tiled=True)
    return finish(parts, fine_out)


def solution(mesh):
    grid = Mesh(mesh.devices.reshape(4, 4, 4, 2, 2), ("x", "y", "z", "c", "m"))
    rows = P(CTX, "m")
    return jax.shard_map(
        per_device,
        mesh=grid,
        in_specs=(rows, rows, rows, P("m"), P("m", None)),
        out_specs=rows,
        check_vma=False,
    )
```

```python
import functools
import math

import jax
import jax.numpy as jnp
from jax import lax
from jax.experimental import pallas as pl
from jax.experimental.pallas import tpu as pltpu
from jax.sharding import Mesh
from jax.sharding import PartitionSpec as P

D_FINE = 2048
HEADS = 16
HEAD = 128
C_HEADS = 8
C_HEAD = 256
WINDOW = 1024
SHORT = 16
EPS = 1e-05
NEG = -1e30
LOG2E = 1.4426950408889634

ROWS = 512
HALF = 1024
LOCAL_HEADS = HALF // HEAD
TILE = 256
CROWS = ROWS // SHORT
GROUP = 4 * CROWS
SMALL = pl.CostEstimate(flops=1, bytes_accessed=1, transcendentals=0)
CTX = ("x", "y", "z", "c")
MIB = 1 << 20
LIMIT = 32 * MIB
SENT = 3 * C_HEAD


def shifted(value, steps):
    count = 128
    return lax.ppermute(
        value, CTX, [(s, s + steps) for s in range(max(0, -steps), min(count, count - steps))]
    )


def rolled(value, axis, steps):
    count = lax.axis_size(axis)
    return lax.ppermute(value, axis, [(s, (s + steps) % count) for s in range(count)])


def swapped(value, count):
    size = value.shape[0] // count
    return [rolled(value[i * size : (i + 1) * size], "c", 1) for i in range(count)]


def attend(q, pieces, store):
    scale = LOG2E / math.sqrt(HEAD)
    scores = []
    top = None
    for keys, okay, mask in pieces:
        s = lax.dot_general(
            q, keys, (((1,), (1,)), ((), ())), preferred_element_type=jnp.float32
        )
        if mask is not None:
            s = jnp.where(mask, s, NEG)
        scores.append(s)
        high = jnp.max(s, -1, keepdims=True)
        if okay is not None:
            high = jnp.where(okay, high, NEG)
        top = high if top is None else jnp.maximum(top, high)
    total = jnp.zeros((q.shape[0], 1), jnp.float32)
    for step, (keys, okay, mask) in enumerate(pieces):
        base = top if okay is None else jnp.where(okay, top, -NEG)
        p = jnp.exp2((scores[step] - base) * scale)
        total = total + jnp.sum(p, -1, keepdims=True)
        store(step, p.astype(jnp.bfloat16))
    return total


def probs_kernel(
    pieces, info, q_ref, ka_ref, ko_ref, kc_ref, vo_ref, vc_ref, *refs
):
    ks_refs, (far_ref, mid_ref, near_ref, l_ref, acc_ref) = refs[:pieces], refs[pieces:]
    head = pl.program_id(0)
    index = info[0]
    core = info[1]
    kb = jnp.where(core == 0, jnp.concatenate([r[...] for r in ks_refs], 0), ko_ref[...])
    chunks = [
        ka_ref[0:TILE, :],
        ka_ref[TILE : 2 * TILE, :],
        kb[0:TILE, :],
        kb[TILE : 2 * TILE, :],
        kc_ref[0:TILE, :],
        kc_ref[TILE : 2 * TILE, :],
    ]
    valid = [index >= 2, index >= 2, index >= 1, index >= 1, None, None]
    row = lax.broadcasted_iota(jnp.int32, (TILE, TILE), 0)
    col = lax.broadcasted_iota(jnp.int32, (TILE, TILE), 1)
    lane = lax.broadcasted_iota(jnp.int32, (TILE, 128), 1)
    for tile in range(ROWS // TILE):
        masks = [col > row, None, None, None, col <= row]
        keys = [(chunks[tile + j], valid[tile + j], masks[j]) for j in range(5)]
        rows = slice(tile * TILE, (tile + 1) * TILE)

        def store(step, p, tile=tile, rows=rows):
            chunk = tile + step
            if chunk == 0:
                far_ref[0] = p
            elif chunk == 1:
                mid_ref[0, rows, :] = p
            elif chunk < 4:
                near_ref[0, rows, (chunk - 2) * TILE : (chunk - 1) * TILE] = p
            else:
                values = vc_ref[(chunk - 4) * TILE : (chunk - 3) * TILE, :]
                part = jnp.dot(p, values, preferred_element_type=jnp.float32)
                if chunk == 5:
                    part = part + acc_ref[rows, :]
                acc_ref[rows, :] = part

        total = attend(q_ref[rows, :], keys, store)
        l_ref[rows, :] = jnp.where(lane == head, total, l_ref[rows, :])

    @pl.when(core == 1)
    def _():
        acc_ref[...] = acc_ref[...] + jnp.dot(
            near_ref[0], vo_ref[...], preferred_element_type=jnp.float32
        )


def fine_probs(info, q, ka, ks, ko, kc, vo, vc):
    column = pl.BlockSpec((ROWS, HEAD), lambda h, info: (0, h))
    piece = pl.BlockSpec((ROWS // len(ks), HEAD), lambda h, info: (0, h))
    return pl.pallas_call(
        functools.partial(probs_kernel, len(ks)),
        grid_spec=pltpu.PrefetchScalarGridSpec(
            num_scalar_prefetch=1,
            grid=(LOCAL_HEADS,),
            in_specs=[column] * 6 + [piece] * len(ks),
            out_specs=[
                pl.BlockSpec((1, TILE, TILE), lambda h, info: (h, 0, 0)),
                pl.BlockSpec((1, ROWS, TILE), lambda h, info: (h, 0, 0)),
                pl.BlockSpec((1, ROWS, ROWS), lambda h, info: (h, 0, 0)),
                pl.BlockSpec((ROWS, 128), lambda h, info: (0, 0)),
                column,
            ],
        ),
        out_shape=[
            jax.ShapeDtypeStruct((LOCAL_HEADS, TILE, TILE), jnp.bfloat16),
            jax.ShapeDtypeStruct((LOCAL_HEADS, ROWS, TILE), jnp.bfloat16),
            jax.ShapeDtypeStruct((LOCAL_HEADS, ROWS, ROWS), jnp.bfloat16),
            jax.ShapeDtypeStruct((ROWS, 128), jnp.float32),
            jax.ShapeDtypeStruct((ROWS, HALF), jnp.float32),
        ],
        compiler_params=pltpu.CompilerParams(vmem_limit_bytes=LIMIT),
        cost_estimate=SMALL,
        name="fine_probs",
    )(info, q, ka, ko, kc, vo, vc, *ks)


def mix_kernel(
    info, far_ref, mid_ref, near_ref, l_ref, acc_ref, va_ref, vs_ref, out_ref, pool_ref, sum_ref
):
    head = pl.program_id(0)
    core = info[1]
    mixed = acc_ref[...] + jnp.dot(
        mid_ref[0], va_ref[TILE : 2 * TILE, :], preferred_element_type=jnp.float32
    )
    far = jnp.dot(far_ref[0], va_ref[0:TILE, :], preferred_element_type=jnp.float32)
    sum_ref[0:TILE, :] = mixed[0:TILE, :] + far
    sum_ref[TILE : 2 * TILE, :] = mixed[TILE : 2 * TILE, :]

    @pl.when(core == 0)
    def _():
        sum_ref[...] = sum_ref[...] + jnp.dot(
            near_ref[0], vs_ref[...], preferred_element_type=jnp.float32
        )

    lane = lax.broadcasted_iota(jnp.int32, (ROWS, 128), 1)
    total = jnp.sum(jnp.where(lane == head, l_ref[...], 0.0), -1, keepdims=True)
    out = (sum_ref[...] / total).astype(jnp.bfloat16)
    out_ref[...] = out
    j = lax.broadcasted_iota(jnp.int32, (40, ROWS), 0)
    r = lax.broadcasted_iota(jnp.int32, (40, ROWS), 1)
    pick = jnp.where((r > SHORT * j - SHORT) & (r <= SHORT * j), 1.0, 0.0)
    pool_ref[...] = jnp.dot(pick.astype(jnp.bfloat16), out, preferred_element_type=jnp.float32)


def fine_mix(info, far, mid, near, l, acc, va, vs):
    column = pl.BlockSpec((ROWS, HEAD), lambda h, info: (0, h))
    return pl.pallas_call(
        mix_kernel,
        grid_spec=pltpu.PrefetchScalarGridSpec(
            num_scalar_prefetch=1,
            grid=(LOCAL_HEADS,),
            in_specs=[
                pl.BlockSpec((1, TILE, TILE), lambda h, info: (h, 0, 0)),
                pl.BlockSpec((1, ROWS, TILE), lambda h, info: (h, 0, 0)),
                pl.BlockSpec((1, ROWS, ROWS), lambda h, info: (h, 0, 0)),
                pl.BlockSpec((ROWS, 128), lambda h, info: (0, 0)),
                column,
                column,
                column,
            ],
            out_specs=[column, pl.BlockSpec((40, HEAD), lambda h, info: (0, h))],
            scratch_shapes=[pltpu.VMEM((ROWS, HEAD), jnp.float32)],
        ),
        out_shape=[
            jax.ShapeDtypeStruct((ROWS, HALF), jnp.bfloat16),
            jax.ShapeDtypeStruct((40, HALF), jnp.float32),
        ],
        compiler_params=pltpu.CompilerParams(vmem_limit_bytes=LIMIT),
        cost_estimate=SMALL,
        name="fine_mix",
    )(info, far, mid, near, l, acc, va, vs)


def short_kernel(pooled_ref, own_ref, other_ref, gain_ref, w_ref, out_ref):
    factor = lax.rsqrt((own_ref[:, 0:1] + other_ref[:, 0:1]) / D_FINE + EPS)
    normed = (pooled_ref[...] * factor * gain_ref[...]).astype(jnp.bfloat16)
    part = jnp.dot(normed, w_ref[...], preferred_element_type=jnp.float32)
    keys = part[:, 0:C_HEAD]
    high = keys.astype(jnp.bfloat16)
    out_ref[0, :, 0:C_HEAD] = high
    out_ref[0, :, C_HEAD : 2 * C_HEAD] = (keys - high.astype(jnp.float32)).astype(jnp.bfloat16)
    out_ref[0, :, 2 * C_HEAD : SENT] = part[:, C_HEAD : 2 * C_HEAD].astype(jnp.bfloat16)


def shorten(pooled, own, other, gain, weight):
    return pl.pallas_call(
        short_kernel,
        grid=(C_HEADS,),
        in_specs=[
            pl.BlockSpec((CROWS, HALF), lambda j: (0, 0)),
            pl.BlockSpec((CROWS, 128), lambda j: (0, 0)),
            pl.BlockSpec((CROWS, 128), lambda j: (0, 0)),
            pl.BlockSpec((1, HALF), lambda j: (0, 0)),
            pl.BlockSpec((HALF, 2 * C_HEAD), lambda j: (0, (j % 2) * 4 + j // 2)),
        ],
        out_specs=pl.BlockSpec((1, CROWS, SENT), lambda j: (j, 0, 0)),
        out_shape=jax.ShapeDtypeStruct((C_HEADS, CROWS, SENT), jnp.bfloat16),
        compiler_params=pltpu.CompilerParams(vmem_limit_bytes=60 * MIB),
        cost_estimate=SMALL,
        name="shorten",
    )(pooled, own, other, gain, weight)


def join_kernel(got_ref, kv_ref, key_ref):
    for y in range(4):
        one = got_ref[2 * y].astype(jnp.float32)
        two = got_ref[2 * y + 1].astype(jnp.float32)
        both = one + two
        keys = both[:, 0:C_HEAD] + both[:, C_HEAD : 2 * C_HEAD]
        values = both[:, 2 * C_HEAD : SENT]
        rows = slice(y * CROWS, (y + 1) * CROWS)
        kv_ref[rows, 0:C_HEAD] = keys.astype(jnp.bfloat16)
        kv_ref[rows, C_HEAD : 2 * C_HEAD] = values.astype(jnp.bfloat16)
        key_ref[rows, :] = keys.astype(jnp.bfloat16)


def join(got):
    whole = pl.BlockSpec(memory_space=pltpu.VMEM)
    return pl.pallas_call(
        join_kernel,
        in_specs=[whole],
        out_specs=[whole, whole],
        out_shape=[
            jax.ShapeDtypeStruct((GROUP, 2 * C_HEAD), jnp.bfloat16),
            jax.ShapeDtypeStruct((GROUP, C_HEAD), jnp.bfloat16),
        ],
        name="join",
    )(got)


def split3(value):
    first = value.astype(jnp.bfloat16).astype(jnp.float32)
    rest = value - first
    second = rest.astype(jnp.bfloat16).astype(jnp.float32)
    return first, second, rest - second


def coarse_kernel(info, *refs):
    q_refs, kv_refs, out_ref, kv_all = refs[0:4], refs[4:12], refs[12], refs[13]
    x, z, c = info[2], info[4], info[1]
    scale = 1.0 / math.sqrt(C_HEAD)
    keys = 8 * GROUP
    for piece in range(8):
        kv_all[piece * GROUP : (piece + 1) * GROUP, :] = kv_refs[piece][...]
    slot = lax.broadcasted_iota(jnp.int32, (1, keys), 1)
    piece = slot // GROUP
    inside = slot % GROUP
    from_x = (x - piece // 2 + 4) % 4
    from_c = jnp.where(piece % 2 == 0, c, 1 - c)
    key_pos = (
        from_x * 1024 + (inside // CROWS) * 256 + z * 64 + from_c * 32 + inside % CROWS
    )
    inner = lax.broadcasted_iota(jnp.int32, (GROUP, 1), 0)
    lane = lax.broadcasted_iota(jnp.int32, (GROUP, 128), 1)
    for k in range(4):
        from_z = (z - k + 4) % 4
        pos = x * 1024 + (inner // CROWS) * 256 + from_z * 64 + c * 32 + inner % CROWS
        allowed = key_pos < jnp.maximum(pos, 1)
        s = lax.dot_general(
            q_refs[k][...], kv_all[:, 0:C_HEAD], (((1,), (1,)), ((), ())),
            preferred_element_type=jnp.float32,
        ) * scale
        s = jnp.where(allowed, s, NEG)
        top = jnp.max(s, -1, keepdims=True)
        p = jnp.where(allowed, jnp.exp(s - top), 0.0)
        total = jnp.sum(p, -1, keepdims=True)
        mixed = jnp.dot(
            p.astype(jnp.bfloat16), kv_all[:, C_HEAD : 2 * C_HEAD],
            preferred_element_type=jnp.float32,
        )
        some = total > 0.0
        safe = jnp.where(some, total, 1.0)
        mixed = jnp.where(some, mixed / safe, 0.0)
        level = jnp.where(some, top + jnp.log(safe), NEG)
        a, b, d = split3(level)
        extra = jnp.where(lane == 0, a, jnp.where(lane == 1, b, jnp.where(lane == 2, d, 0.0)))
        for y in range(4):
            rows = slice(y * CROWS, (y + 1) * CROWS)
            out_ref[y * 4 + from_z, :, 0:C_HEAD] = mixed[rows, :].astype(jnp.bfloat16)
            out_ref[y * 4 + from_z, :, C_HEAD : C_HEAD + 128] = extra[rows, :].astype(
                jnp.bfloat16
            )


def coarse_attend(info, queries, pairs):
    whole = pl.BlockSpec(memory_space=pltpu.VMEM)
    return pl.pallas_call(
        coarse_kernel,
        in_specs=[pl.BlockSpec(memory_space=pltpu.SMEM)] + [whole] * 12,
        out_specs=whole,
        out_shape=jax.ShapeDtypeStruct((16, CROWS, C_HEAD + 128), jnp.bfloat16),
        scratch_shapes=[pltpu.VMEM((8 * GROUP, 2 * C_HEAD), jnp.bfloat16)],
        compiler_params=pltpu.CompilerParams(vmem_limit_bytes=32 * MIB),
        cost_estimate=pl.CostEstimate(
            flops=4 * 4 * GROUP * 8 * GROUP * C_HEAD,
            bytes_accessed=2 * MIB,
            transcendentals=4 * GROUP * 8 * GROUP,
        ),
        name="coarse_attend",
    )(info, *queries, *pairs)


def final_kernel(part_ref, fine_ref, out_ref):
    parts = part_ref[...].astype(jnp.float32)
    levels = jnp.sum(parts[:, :, C_HEAD : C_HEAD + 128], -1, keepdims=True)
    top = jnp.max(levels, 0, keepdims=True)
    weights = jnp.exp(levels - top)
    total = jnp.sum(weights, 0)
    mixed = jnp.sum(parts[:, :, 0:C_HEAD] * weights, 0) / total
    coarse = mixed.astype(jnp.bfloat16)
    r = lax.broadcasted_iota(jnp.int32, (ROWS, CROWS), 0)
    j = lax.broadcasted_iota(jnp.int32, (ROWS, CROWS), 1)
    spread = jnp.where(r // SHORT == j, 1.0, 0.0).astype(jnp.bfloat16)
    up = jnp.dot(spread, coarse, preferred_element_type=jnp.float32)
    out_ref[...] = (fine_ref[...].astype(jnp.float32) + up).astype(jnp.bfloat16)


def finish(parts, fine):
    column = pl.BlockSpec((ROWS, C_HEAD), lambda h: (0, h))
    return pl.pallas_call(
        final_kernel,
        grid=(4,),
        in_specs=[pl.BlockSpec((4, CROWS, C_HEAD + 128), lambda h: (h, 0, 0)), column],
        out_specs=column,
        out_shape=jax.ShapeDtypeStruct((ROWS, HALF), jnp.bfloat16),
        compiler_params=pltpu.CompilerParams(vmem_limit_bytes=32 * MIB),
        name="finish",
    )(parts, fine)


def per_device(fine_q, fine_k, fine_v, norm_gain, short_weight):
    x, y, z, c = (lax.axis_index(a) for a in CTX)
    index = ((x * 4 + y) * 4 + z) * 2 + c
    info = jnp.stack([index, c, x, y, z]).astype(jnp.int32)

    k2 = shifted(fine_k, 2)
    v2 = shifted(fine_v, 2)
    ko = rolled(fine_k, "c", 1)
    vo = rolled(fine_v, "c", 1)
    ks = swapped(k2, 4)
    far, mid, near, l, acc = fine_probs(info, fine_q, k2, ks, ko, fine_k, vo, fine_v)
    v2, l = lax.optimization_barrier((v2, l))
    vs = rolled(v2, "c", 1)
    fine_out, sums = fine_mix(info, far, mid, near, l, acc, v2, vs)

    tail = shifted(sums[CROWS : CROWS + 8], 1)
    pooled = (sums[:CROWS] + jnp.pad(tail[0:1], ((0, CROWS - 1), (0, 0)))) / SHORT
    squares = jnp.sum(pooled * pooled, -1, keepdims=True)
    squares = jnp.broadcast_to(squares, (CROWS, 128))
    other = rolled(squares, "m", 1)
    sent = shorten(pooled, squares, other, norm_gain[None], short_weight)

    got = lax.all_to_all(sent, ("y", "m"), split_axis=0, concat_axis=0, tiled=True)
    kv, own_keys = join(got)
    along = [rolled(kv, "x", k) for k in (1, 2, 3)]
    queries = [own_keys] + [rolled(own_keys, "z", k) for k in (1, 2)]
    along[0], kv, own_keys = lax.optimization_barrier((along[0], kv, own_keys))
    queries.append(rolled(own_keys, "z", 3))
    pairs = []
    for piece in [kv] + along:
        pairs += [piece, rolled(piece, "c", 1)]
    parts = coarse_attend(info, queries, pairs)
    parts = lax.all_to_all(parts, ("y", "z"), split_axis=0, concat_axis=0, tiled=True)
    return finish(parts, fine_out)


def solution(mesh):
    grid = Mesh(mesh.devices.reshape(4, 4, 4, 2, 2), ("x", "y", "z", "c", "m"))
    rows = P(CTX, "m")
    return jax.shard_map(
        per_device,
        mesh=grid,
        in_specs=(rows, rows, rows, P("m"), P("m", None)),
        out_specs=rows,
        check_vma=False,
    )
```

```python
import functools
import math

import jax
import jax.numpy as jnp
from jax import lax
from jax.experimental import pallas as pl
from jax.experimental.pallas import tpu as pltpu
from jax.sharding import Mesh
from jax.sharding import PartitionSpec as P

D_FINE = 2048
HEADS = 16
HEAD = 128
C_HEADS = 8
C_HEAD = 256
WINDOW = 1024
SHORT = 16
EPS = 1e-05
NEG = -1e30
LOG2E = 1.4426950408889634

ROWS = 512
HALF = 1024
LOCAL_HEADS = HALF // HEAD
TILE = 256
CROWS = ROWS // SHORT
GROUP = 4 * CROWS
SMALL = pl.CostEstimate(flops=1, bytes_accessed=1, transcendentals=0)
CTX = ("x", "y", "z", "c")
MIB = 1 << 20
LIMIT = 32 * MIB
SENT = 3 * C_HEAD


def shifted(value, steps):
    count = 128
    return lax.ppermute(
        value, CTX, [(s, s + steps) for s in range(max(0, -steps), min(count, count - steps))]
    )


def rolled(value, axis, steps):
    count = lax.axis_size(axis)
    return lax.ppermute(value, axis, [(s, (s + steps) % count) for s in range(count)])


def paired(value, axis, distance):
    count = lax.axis_size(axis)
    return lax.ppermute(value, axis, [(s, s ^ distance) for s in range(count)])


def swapped(value, count):
    size = value.shape[0] // count
    return [rolled(value[i * size : (i + 1) * size], "c", 1) for i in range(count)]


def attend(q, pieces, store):
    scale = LOG2E / math.sqrt(HEAD)
    scores = []
    top = None
    for keys, okay, mask in pieces:
        s = lax.dot_general(
            q, keys, (((1,), (1,)), ((), ())), preferred_element_type=jnp.float32
        )
        if mask is not None:
            s = jnp.where(mask, s, NEG)
        scores.append(s)
        high = jnp.max(s, -1, keepdims=True)
        if okay is not None:
            high = jnp.where(okay, high, NEG)
        top = high if top is None else jnp.maximum(top, high)
    total = jnp.zeros((q.shape[0], 1), jnp.float32)
    for step, (keys, okay, mask) in enumerate(pieces):
        base = top if okay is None else jnp.where(okay, top, -NEG)
        p = jnp.exp2((scores[step] - base) * scale)
        total = total + jnp.sum(p, -1, keepdims=True)
        store(step, p.astype(jnp.bfloat16))
    return total


def near_kernel(q_ref, k_ref, v_ref, q_out, k_out, v_out):
    q_out[...] = q_ref[...]
    k_out[...] = k_ref[...]
    v_out[...] = v_ref[...]


def bring_near(q, k, v):
    column = pl.BlockSpec((ROWS, 2 * HEAD), lambda h: (0, h))
    return pl.pallas_call(
        near_kernel,
        grid=(LOCAL_HEADS // 2,),
        in_specs=[column] * 3,
        out_specs=[column] * 3,
        out_shape=[jax.ShapeDtypeStruct((ROWS, HALF), jnp.bfloat16)] * 3,
        compiler_params=pltpu.CompilerParams(vmem_limit_bytes=LIMIT),
        cost_estimate=pl.CostEstimate(flops=1 << 30, bytes_accessed=6 * MIB, transcendentals=0),
        name="bring_near",
    )(q, k, v)


def probs_kernel(
    pieces, info, q_ref, ka_ref, ko_ref, kc_ref, vo_ref, vc_ref, *refs
):
    ks_refs, (far_ref, mid_ref, near_ref, l_ref, acc_ref) = refs[:pieces], refs[pieces:]
    head = pl.program_id(0)
    index = info[0]
    core = info[1]
    kb = jnp.where(core == 0, jnp.concatenate([r[...] for r in ks_refs], 0), ko_ref[...])
    chunks = [
        ka_ref[0:TILE, :],
        ka_ref[TILE : 2 * TILE, :],
        kb[0:TILE, :],
        kb[TILE : 2 * TILE, :],
        kc_ref[0:TILE, :],
        kc_ref[TILE : 2 * TILE, :],
    ]
    valid = [index >= 2, index >= 2, index >= 1, index >= 1, None, None]
    row = lax.broadcasted_iota(jnp.int32, (TILE, TILE), 0)
    col = lax.broadcasted_iota(jnp.int32, (TILE, TILE), 1)
    lane = lax.broadcasted_iota(jnp.int32, (TILE, 128), 1)
    for tile in range(ROWS // TILE):
        masks = [col > row, None, None, None, col <= row]
        keys = [(chunks[tile + j], valid[tile + j], masks[j]) for j in range(5)]
        rows = slice(tile * TILE, (tile + 1) * TILE)

        def store(step, p, tile=tile, rows=rows):
            chunk = tile + step
            if chunk == 0:
                far_ref[0] = p
            elif chunk == 1:
                mid_ref[0, rows, :] = p
            elif chunk < 4:
                near_ref[0, rows, (chunk - 2) * TILE : (chunk - 1) * TILE] = p
            else:
                values = vc_ref[(chunk - 4) * TILE : (chunk - 3) * TILE, :]
                part = jnp.dot(p, values, preferred_element_type=jnp.float32)
                if chunk == 5:
                    part = part + acc_ref[rows, :]
                acc_ref[rows, :] = part

        total = attend(q_ref[rows, :], keys, store)
        l_ref[rows, :] = jnp.where(lane == head, total, l_ref[rows, :])

    @pl.when(core == 1)
    def _():
        acc_ref[...] = acc_ref[...] + jnp.dot(
            near_ref[0], vo_ref[...], preferred_element_type=jnp.float32
        )


def fine_probs(info, q, ka, ks, ko, kc, vo, vc):
    column = pl.BlockSpec((ROWS, HEAD), lambda h, info: (0, h))
    piece = pl.BlockSpec((ROWS // len(ks), HEAD), lambda h, info: (0, h))
    return pl.pallas_call(
        functools.partial(probs_kernel, len(ks)),
        grid_spec=pltpu.PrefetchScalarGridSpec(
            num_scalar_prefetch=1,
            grid=(LOCAL_HEADS,),
            in_specs=[column] * 6 + [piece] * len(ks),
            out_specs=[
                pl.BlockSpec((1, TILE, TILE), lambda h, info: (h, 0, 0)),
                pl.BlockSpec((1, ROWS, TILE), lambda h, info: (h, 0, 0)),
                pl.BlockSpec((1, ROWS, ROWS), lambda h, info: (h, 0, 0)),
                pl.BlockSpec((ROWS, 128), lambda h, info: (0, 0)),
                column,
            ],
        ),
        out_shape=[
            jax.ShapeDtypeStruct((LOCAL_HEADS, TILE, TILE), jnp.bfloat16),
            jax.ShapeDtypeStruct((LOCAL_HEADS, ROWS, TILE), jnp.bfloat16),
            jax.ShapeDtypeStruct((LOCAL_HEADS, ROWS, ROWS), jnp.bfloat16),
            jax.ShapeDtypeStruct((ROWS, 128), jnp.float32),
            jax.ShapeDtypeStruct((ROWS, HALF), jnp.float32),
        ],
        compiler_params=pltpu.CompilerParams(vmem_limit_bytes=LIMIT),
        cost_estimate=SMALL,
        name="fine_probs",
    )(info, q, ka, ko, kc, vo, vc, *ks)


def mix_kernel(
    info, far_ref, mid_ref, near_ref, l_ref, acc_ref, va_ref, vs_ref,
    out_ref, pool_ref, pack_ref, tail_ref,
):
    core = info[1]

    def mix(with_near):
        j = lax.broadcasted_iota(jnp.int32, (40, ROWS), 0)
        r = lax.broadcasted_iota(jnp.int32, (40, ROWS), 1)
        pick = jnp.where((r > SHORT * j - SHORT) & (r <= SHORT * j), 1.0, 0.0)
        pick = pick.astype(jnp.bfloat16)
        squares = jnp.zeros((CROWS, HEAD), jnp.float32)
        for head in range(LOCAL_HEADS):
            columns = slice(head * HEAD, (head + 1) * HEAD)
            mixed = acc_ref[:, columns] + jnp.dot(
                mid_ref[head], va_ref[TILE : 2 * TILE, columns],
                preferred_element_type=jnp.float32,
            )
            if with_near:
                mixed = mixed + jnp.dot(
                    near_ref[head], vs_ref[:, columns], preferred_element_type=jnp.float32
                )
            first = mixed[0:TILE, :] + jnp.dot(
                far_ref[head], va_ref[0:TILE, columns], preferred_element_type=jnp.float32
            )
            mixed = jnp.concatenate([first, mixed[TILE : 2 * TILE, :]], 0)
            out = (mixed / l_ref[:, head : head + 1]).astype(jnp.bfloat16)
            out_ref[:, columns] = out
            sums = jnp.dot(pick, out, preferred_element_type=jnp.float32)
            pooled = sums[0:CROWS, :] * (1.0 / SHORT)
            pool_ref[:, columns] = pooled
            squares = squares + pooled * pooled
            pack_ref[CROWS + head : CROWS + head + 1, :] = pooled[0:1, :]
            tail_ref[head : head + 1, :] = sums[CROWS : CROWS + 1, :] * (1.0 / SHORT)
        pack_ref[0:CROWS, :] = jnp.broadcast_to(
            jnp.sum(squares, -1, keepdims=True), (CROWS, HEAD)
        )

    @pl.when(core == 0)
    def _():
        mix(True)

    @pl.when(core == 1)
    def _():
        mix(False)


def fine_mix(info, far, mid, near, l, acc, va, vs):
    whole = pl.BlockSpec(memory_space=pltpu.VMEM)
    return pl.pallas_call(
        mix_kernel,
        in_specs=[pl.BlockSpec(memory_space=pltpu.SMEM)] + [whole] * 7,
        out_specs=[whole] * 4,
        out_shape=[
            jax.ShapeDtypeStruct((ROWS, HALF), jnp.bfloat16),
            jax.ShapeDtypeStruct((CROWS, HALF), jnp.float32),
            jax.ShapeDtypeStruct((CROWS + LOCAL_HEADS, HEAD), jnp.float32),
            jax.ShapeDtypeStruct((LOCAL_HEADS, HEAD), jnp.float32),
        ],
        compiler_params=pltpu.CompilerParams(vmem_limit_bytes=LIMIT),
        cost_estimate=SMALL,
        name="fine_mix",
    )(info, far, mid, near, l, acc, va, vs)


def short_kernel(
    pool_ref, own_ref, other_ref, tail_ref, other_tail_ref, gain_ref, w_ref,
    out_ref, held, acc, sems,
):
    depth = HALF // 4
    loads = [
        pltpu.make_async_copy(
            w_ref.at[pl.ds(i * depth, depth), :], held.at[pl.ds(i * depth, depth), :], sems.at[i]
        )
        for i in range(4)
    ]
    for load in loads:
        load.start()
    first = own_ref[CROWS : CROWS + LOCAL_HEADS, :] + tail_ref[...]
    second = other_ref[CROWS : CROWS + LOCAL_HEADS, :] + other_tail_ref[...]
    both = jnp.sum(first * first + second * second, 0, keepdims=True)
    both = jnp.sum(both, -1, keepdims=True)
    row = lax.broadcasted_iota(jnp.int32, (CROWS, 1), 0)
    squares = jnp.where(row == 0, both, own_ref[0:CROWS, 0:1] + other_ref[0:CROWS, 0:1])
    factor = lax.rsqrt(squares / D_FINE + EPS)
    start = jnp.concatenate([first[h : h + 1, :] for h in range(LOCAL_HEADS)], 1)
    pooled = jnp.where(row == 0, start, pool_ref[...])
    normed = (pooled * factor * gain_ref[...]).astype(jnp.bfloat16)
    for i, load in enumerate(loads):
        load.wait()
        for part in range(4):
            columns = slice(part * 1024, (part + 1) * 1024)
            added = jnp.dot(
                normed[:, i * depth : (i + 1) * depth],
                held[i * depth : (i + 1) * depth, columns],
                preferred_element_type=jnp.float32,
            )
            acc[:, columns] = added if i == 0 else acc[:, columns] + added
    for piece in range(C_HEADS):
        begin = ((piece % 2) * 4 + piece // 2) * 2 * C_HEAD
        keys = acc[:, begin : begin + C_HEAD]
        high = keys.astype(jnp.bfloat16)
        out_ref[piece, :, 0:C_HEAD] = high
        out_ref[piece, :, C_HEAD : 2 * C_HEAD] = (keys - high.astype(jnp.float32)).astype(
            jnp.bfloat16
        )
        out_ref[piece, :, 2 * C_HEAD : SENT] = acc[
            :, begin + C_HEAD : begin + 2 * C_HEAD
        ].astype(jnp.bfloat16)


def shorten(pooled, own, other, tail, other_tail, gain, weight):
    whole = pl.BlockSpec(memory_space=pltpu.VMEM)
    return pl.pallas_call(
        short_kernel,
        in_specs=[whole] * 6 + [pl.BlockSpec(memory_space=pl.ANY)],
        out_specs=whole,
        out_shape=jax.ShapeDtypeStruct((C_HEADS, CROWS, SENT), jnp.bfloat16),
        scratch_shapes=[
            pltpu.VMEM((HALF, 4096), jnp.bfloat16),
            pltpu.VMEM((CROWS, 4096), jnp.float32),
            pltpu.SemaphoreType.DMA((4,)),
        ],
        compiler_params=pltpu.CompilerParams(vmem_limit_bytes=56 * MIB),
        cost_estimate=SMALL,
        name="shorten",
    )(pooled, own, other, tail, other_tail, gain, weight)


def join_kernel(got_ref, kv_ref, key_ref):
    for y in range(4):
        one = got_ref[2 * y].astype(jnp.float32)
        two = got_ref[2 * y + 1].astype(jnp.float32)
        both = one + two
        keys = both[:, 0:C_HEAD] + both[:, C_HEAD : 2 * C_HEAD]
        values = both[:, 2 * C_HEAD : SENT]
        rows = slice(y * CROWS, (y + 1) * CROWS)
        kv_ref[rows, 0:C_HEAD] = keys.astype(jnp.bfloat16)
        kv_ref[rows, C_HEAD : 2 * C_HEAD] = values.astype(jnp.bfloat16)
        key_ref[rows, :] = keys.astype(jnp.bfloat16)


def join(got):
    whole = pl.BlockSpec(memory_space=pltpu.VMEM)
    return pl.pallas_call(
        join_kernel,
        in_specs=[whole],
        out_specs=[whole, whole],
        out_shape=[
            jax.ShapeDtypeStruct((GROUP, 2 * C_HEAD), jnp.bfloat16),
            jax.ShapeDtypeStruct((GROUP, C_HEAD), jnp.bfloat16),
        ],
        name="join",
    )(got)


def split3(value):
    first = value.astype(jnp.bfloat16).astype(jnp.float32)
    rest = value - first
    second = rest.astype(jnp.bfloat16).astype(jnp.float32)
    return first, second, rest - second


def coarse_kernel(info, *refs):
    q_refs, kv_refs, out_ref, kv_all = refs[0:3], refs[3:11], refs[11], refs[12]
    x, z, c = info[2], info[4], info[1]
    scale = 1.0 / math.sqrt(C_HEAD)
    keys = 8 * GROUP
    for piece in range(8):
        kv_all[piece * GROUP : (piece + 1) * GROUP, :] = kv_refs[piece][...]
    slot = lax.broadcasted_iota(jnp.int32, (1, keys), 1)
    piece = slot // GROUP
    inside = slot % GROUP
    from_x = (x - piece // 2 + 4) % 4
    from_c = jnp.where(piece % 2 == 0, c, 1 - c)
    key_pos = (
        from_x * 1024 + (inside // CROWS) * 256 + z * 64 + from_c * 32 + inside % CROWS
    )
    inner = lax.broadcasted_iota(jnp.int32, (GROUP, 1), 0)
    lane = lax.broadcasted_iota(jnp.int32, (GROUP, 128), 1)
    for k in range(4):
        from_z = jnp.bitwise_xor(z, k)
        if k < 2:
            query = q_refs[k][...]
        else:
            query = q_refs[2][(k - 2) * GROUP : (k - 1) * GROUP, :]
        pos = x * 1024 + (inner // CROWS) * 256 + from_z * 64 + c * 32 + inner % CROWS
        allowed = key_pos < jnp.maximum(pos, 1)
        s = lax.dot_general(
            query, kv_all[:, 0:C_HEAD], (((1,), (1,)), ((), ())),
            preferred_element_type=jnp.float32,
        ) * scale
        s = jnp.where(allowed, s, NEG)
        top = jnp.max(s, -1, keepdims=True)
        p = jnp.where(allowed, jnp.exp(s - top), 0.0)
        total = jnp.sum(p, -1, keepdims=True)
        mixed = jnp.dot(
            p.astype(jnp.bfloat16), kv_all[:, C_HEAD : 2 * C_HEAD],
            preferred_element_type=jnp.float32,
        )
        some = total > 0.0
        safe = jnp.where(some, total, 1.0)
        mixed = jnp.where(some, mixed / safe, 0.0)
        level = jnp.where(some, top + jnp.log(safe), NEG)
        a, b, d = split3(level)
        extra = jnp.where(lane == 0, a, jnp.where(lane == 1, b, jnp.where(lane == 2, d, 0.0)))
        for y in range(4):
            rows = slice(y * CROWS, (y + 1) * CROWS)
            out_ref[y * 4 + from_z, :, 0:C_HEAD] = mixed[rows, :].astype(jnp.bfloat16)
            out_ref[y * 4 + from_z, :, C_HEAD : C_HEAD + 128] = extra[rows, :].astype(
                jnp.bfloat16
            )


def coarse_attend(info, queries, pairs):
    whole = pl.BlockSpec(memory_space=pltpu.VMEM)
    return pl.pallas_call(
        coarse_kernel,
        grid=(1,),
        in_specs=[pl.BlockSpec(memory_space=pltpu.SMEM)]
        + [pl.BlockSpec((GROUP, C_HEAD), lambda i: (0, 0))]
        + [whole] * 2
        + [pl.BlockSpec((GROUP, 2 * C_HEAD), lambda i: (0, 0))]
        + [whole] * 7,
        out_specs=whole,
        out_shape=jax.ShapeDtypeStruct((16, CROWS, C_HEAD + 128), jnp.bfloat16),
        scratch_shapes=[pltpu.VMEM((8 * GROUP, 2 * C_HEAD), jnp.bfloat16)],
        compiler_params=pltpu.CompilerParams(vmem_limit_bytes=32 * MIB),
        cost_estimate=pl.CostEstimate(
            flops=4 * 4 * GROUP * 8 * GROUP * C_HEAD,
            bytes_accessed=2 * MIB,
            transcendentals=4 * GROUP * 8 * GROUP,
        ),
        name="coarse_attend",
    )(info, *queries, *pairs)


def final_kernel(part_ref, fine_ref, out_ref):
    parts = part_ref[...].astype(jnp.float32)
    levels = jnp.sum(parts[:, :, C_HEAD : C_HEAD + 128], -1, keepdims=True)
    top = jnp.max(levels, 0, keepdims=True)
    weights = jnp.exp(levels - top)
    total = jnp.sum(weights, 0)
    mixed = jnp.sum(parts[:, :, 0:C_HEAD] * weights, 0) / total
    coarse = mixed.astype(jnp.bfloat16)
    r = lax.broadcasted_iota(jnp.int32, (ROWS, CROWS), 0)
    j = lax.broadcasted_iota(jnp.int32, (ROWS, CROWS), 1)
    spread = jnp.where(r // SHORT == j, 1.0, 0.0).astype(jnp.bfloat16)
    up = jnp.dot(spread, coarse, preferred_element_type=jnp.float32)
    out_ref[...] = (fine_ref[...].astype(jnp.float32) + up).astype(jnp.bfloat16)


def finish(parts, fine):
    column = pl.BlockSpec((ROWS, C_HEAD), lambda h: (0, h))
    return pl.pallas_call(
        final_kernel,
        grid=(4,),
        in_specs=[pl.BlockSpec((4, CROWS, C_HEAD + 128), lambda h: (h, 0, 0)), column],
        out_specs=column,
        out_shape=jax.ShapeDtypeStruct((ROWS, HALF), jnp.bfloat16),
        compiler_params=pltpu.CompilerParams(vmem_limit_bytes=32 * MIB),
        name="finish",
    )(parts, fine)


def per_device(fine_q, fine_k, fine_v, norm_gain, short_weight):
    x, y, z, c = (lax.axis_index(a) for a in CTX)
    index = ((x * 4 + y) * 4 + z) * 2 + c
    info = jnp.stack([index, c, x, y, z]).astype(jnp.int32)

    k2 = shifted(fine_k, 2)
    v2 = shifted(fine_v, 2)
    ko = rolled(fine_k, "c", 1)
    vo = rolled(fine_v, "c", 1)
    own_q, own_k, own_v = bring_near(fine_q, fine_k, fine_v)
    k2, own_q, own_k, own_v = lax.optimization_barrier((k2, own_q, own_k, own_v))
    ks = swapped(k2, 4)
    far, mid, near, l, acc = fine_probs(info, own_q, k2, ks, ko, own_k, vo, own_v)
    v2, l = lax.optimization_barrier((v2, l))
    vs = rolled(v2, "c", 1)
    fine_out, pooled, pack, tail = fine_mix(info, far, mid, near, l, acc, v2, vs)

    last = shifted(tail, 1)
    last_other = lax.ppermute(
        tail, CTX + ("m",), [(2 * i + m, 2 * i + 3 - m) for i in range(127) for m in (0, 1)]
    )
    other = rolled(pack, "m", 1)
    sent = shorten(pooled, pack, other, last, last_other, norm_gain[None], short_weight)

    got = lax.all_to_all(sent, ("y", "m"), split_axis=0, concat_axis=0, tiled=True)
    kv, own_keys = join(got)
    next_keys = paired(own_keys, "z", 1)
    along = [rolled(kv, "x", k) for k in (1, 2, 3)]
    far_keys = paired(jnp.concatenate([own_keys, next_keys], 0), "z", 2)
    queries = [own_keys, next_keys, far_keys]
    pairs = []
    for piece in [kv] + along:
        pairs += [piece, rolled(piece, "c", 1)]
    parts = coarse_attend(info, queries, pairs)
    parts = lax.all_to_all(parts, ("y", "z"), split_axis=0, concat_axis=0, tiled=True)
    return finish(parts, fine_out)


def solution(mesh):
    grid = Mesh(mesh.devices.reshape(4, 4, 4, 2, 2), ("x", "y", "z", "c", "m"))
    rows = P(CTX, "m")
    return jax.shard_map(
        per_device,
        mesh=grid,
        in_specs=(rows, rows, rows, P("m"), P("m", None)),
        out_specs=rows,
        check_vma=False,
    )
```

```python
import functools
import math

import jax
import jax.numpy as jnp
from jax import lax
from jax.experimental import pallas as pl
from jax.experimental.pallas import tpu as pltpu
from jax.sharding import Mesh
from jax.sharding import PartitionSpec as P

D_FINE = 2048
HEADS = 16
HEAD = 128
C_HEADS = 8
C_HEAD = 256
WINDOW = 1024
SHORT = 16
EPS = 1e-05
NEG = -1e30
LOG2E = 1.4426950408889634

ROWS = 512
HALF = 1024
LOCAL_HEADS = HALF // HEAD
TILE = 256
CROWS = ROWS // SHORT
GROUP = 4 * CROWS
SMALL = pl.CostEstimate(flops=1, bytes_accessed=1, transcendentals=0)
CTX = ("x", "y", "z", "c")
MIB = 1 << 20


def shifted(value, steps):
    count = 128
    return lax.ppermute(
        value, CTX, [(s, s + steps) for s in range(max(0, -steps), min(count, count - steps))]
    )


def rolled(value, axis, steps):
    count = lax.axis_size(axis)
    return lax.ppermute(value, axis, [(s, (s + steps) % count) for s in range(count)])


def paired(value, axis, distance):
    count = lax.axis_size(axis)
    return lax.ppermute(value, axis, [(s, s ^ distance) for s in range(count)])


def limit(mib):
    return pltpu.CompilerParams(vmem_limit_bytes=mib * MIB)


def halves_kernel(in_ref, low_ref, high_ref):
    low_ref[...] = in_ref[0:TILE, :]
    high_ref[...] = in_ref[TILE : 2 * TILE, :]


def halves(value):
    half = pl.BlockSpec((TILE, 512), lambda i: (0, i))
    return pl.pallas_call(
        halves_kernel,
        grid=(2,),
        in_specs=[pl.BlockSpec((ROWS, 512), lambda i: (0, i))],
        out_specs=[half] * 2,
        out_shape=[jax.ShapeDtypeStruct((TILE, HALF), jnp.bfloat16)] * 2,
        compiler_params=limit(8),
        cost_estimate=SMALL,
        name="halves",
    )(value)


def pick_kernel(info, part_ref, own_ref, part_out, own_out):
    part_out[...] = part_ref[...]
    own_out[...] = own_ref[...]


def pick_columns(info, weight):
    wide = 2 * C_HEAD
    size = HALF // 8
    part = pl.BlockSpec(
        (size, wide), lambda i, info: (info[2] * 2 + info[1], (1 - info[5]) * 4 + info[3])
    )
    own = pl.BlockSpec((HALF // 4, wide), lambda i, info: (i, info[5] * 4 + info[3]))
    return pl.pallas_call(
        pick_kernel,
        grid_spec=pltpu.PrefetchScalarGridSpec(
            num_scalar_prefetch=1,
            grid=(4,),
            in_specs=[part, own],
            out_specs=[
                pl.BlockSpec((size, wide), lambda i, info: (0, 0)),
                pl.BlockSpec((HALF // 4, wide), lambda i, info: (i, 0)),
            ],
        ),
        out_shape=[
            jax.ShapeDtypeStruct((size, wide), jnp.bfloat16),
            jax.ShapeDtypeStruct((HALF, wide), jnp.bfloat16),
        ],
        compiler_params=limit(8),
        cost_estimate=pl.CostEstimate(flops=1 << 30, bytes_accessed=2 * MIB, transcendentals=0),
        name="pick_columns",
    )(info, weight, weight)


def start_kernel(pool_ref, tail_ref, out_ref):
    row = lax.broadcasted_iota(jnp.int32, (CROWS, 1), 0)
    out_ref[...] = pool_ref[...] + jnp.where(row == 0, tail_ref[0:1, :], 0.0)


def add_tail(pooled, tail):
    whole = pl.BlockSpec(memory_space=pltpu.VMEM)
    return pl.pallas_call(
        start_kernel,
        in_specs=[whole] * 2,
        out_specs=whole,
        out_shape=jax.ShapeDtypeStruct((CROWS, HALF), jnp.float32),
        compiler_params=limit(4),
        cost_estimate=SMALL,
        name="add_tail",
    )(pooled, tail)


def both_kernel(one_ref, two_ref, out_ref):
    out_ref[0:GROUP, :] = one_ref[...]
    out_ref[GROUP : 2 * GROUP, :] = two_ref[...]


def stacked(one, two):
    whole = pl.BlockSpec(memory_space=pltpu.VMEM)
    return pl.pallas_call(
        both_kernel,
        in_specs=[whole] * 2,
        out_specs=whole,
        out_shape=jax.ShapeDtypeStruct((2 * GROUP, C_HEAD), jnp.bfloat16),
        compiler_params=limit(4),
        cost_estimate=SMALL,
        name="stacked",
    )(one, two)


def attend(q, pieces, store):
    scale = LOG2E / math.sqrt(HEAD)
    scores = []
    top = None
    for keys, okay, mask in pieces:
        s = lax.dot_general(
            q, keys, (((1,), (1,)), ((), ())), preferred_element_type=jnp.float32
        )
        if mask is not None:
            s = jnp.where(mask, s, NEG)
        scores.append(s)
        high = jnp.max(s, -1, keepdims=True)
        if okay is not None:
            high = jnp.where(okay, high, NEG)
        top = high if top is None else jnp.maximum(top, high)
    total = jnp.zeros((q.shape[0], 1), jnp.float32)
    for step, (keys, okay, mask) in enumerate(pieces):
        base = top if okay is None else jnp.where(okay, top, -NEG)
        p = jnp.exp2((scores[step] - base) * scale)
        total = total + jnp.sum(p, -1, keepdims=True)
        store(step, p.astype(jnp.bfloat16))
    return total


def probs_kernel(
    pieces, info, q_ref, ka_ref, ko_ref, kc_ref, vo_ref, vc_ref, *refs
):
    ks_refs, (far_ref, mid_ref, near_ref, l_ref, acc_ref) = refs[:pieces], refs[pieces:]
    head = pl.program_id(0)
    index = info[0]
    core = info[1]
    kb = jnp.where(core == 0, jnp.concatenate([r[...] for r in ks_refs], 0), ko_ref[...])
    chunks = [
        ka_ref[0:TILE, :],
        ka_ref[TILE : 2 * TILE, :],
        kb[0:TILE, :],
        kb[TILE : 2 * TILE, :],
        kc_ref[0:TILE, :],
        kc_ref[TILE : 2 * TILE, :],
    ]
    valid = [index >= 2, index >= 2, index >= 1, index >= 1, None, None]
    row = lax.broadcasted_iota(jnp.int32, (TILE, TILE), 0)
    col = lax.broadcasted_iota(jnp.int32, (TILE, TILE), 1)
    lane = lax.broadcasted_iota(jnp.int32, (TILE, 128), 1)
    for tile in range(ROWS // TILE):
        masks = [col > row, None, None, None, col <= row]
        keys = [(chunks[tile + j], valid[tile + j], masks[j]) for j in range(5)]
        rows = slice(tile * TILE, (tile + 1) * TILE)

        def store(step, p, tile=tile, rows=rows):
            chunk = tile + step
            if chunk == 0:
                far_ref[0] = p
            elif chunk == 1:
                mid_ref[0, rows, :] = p
            elif chunk < 4:
                near_ref[0, rows, (chunk - 2) * TILE : (chunk - 1) * TILE] = p
            else:
                values = vc_ref[(chunk - 4) * TILE : (chunk - 3) * TILE, :]
                part = jnp.dot(p, values, preferred_element_type=jnp.float32)
                if chunk == 5:
                    part = part + acc_ref[rows, :]
                acc_ref[rows, :] = part

        total = attend(q_ref[rows, :], keys, store)
        l_ref[rows, :] = jnp.where(lane == head, total, l_ref[rows, :])

    @pl.when(core == 1)
    def _():
        acc_ref[...] = acc_ref[...] + jnp.dot(
            near_ref[0], vo_ref[...], preferred_element_type=jnp.float32
        )


def fine_probs(info, q, ka, ks, ko, kc, vo, vc):
    column = pl.BlockSpec((ROWS, HEAD), lambda h, info: (0, h))
    piece = pl.BlockSpec((ROWS // len(ks), HEAD), lambda h, info: (0, h))
    return pl.pallas_call(
        functools.partial(probs_kernel, len(ks)),
        grid_spec=pltpu.PrefetchScalarGridSpec(
            num_scalar_prefetch=1,
            grid=(LOCAL_HEADS,),
            in_specs=[column] * 6 + [piece] * len(ks),
            out_specs=[
                pl.BlockSpec((1, TILE, TILE), lambda h, info: (h, 0, 0)),
                pl.BlockSpec((1, ROWS, TILE), lambda h, info: (h, 0, 0)),
                pl.BlockSpec((1, ROWS, ROWS), lambda h, info: (h, 0, 0)),
                pl.BlockSpec((ROWS, 128), lambda h, info: (0, 0)),
                column,
            ],
        ),
        out_shape=[
            jax.ShapeDtypeStruct((LOCAL_HEADS, TILE, TILE), jnp.bfloat16),
            jax.ShapeDtypeStruct((LOCAL_HEADS, ROWS, TILE), jnp.bfloat16),
            jax.ShapeDtypeStruct((LOCAL_HEADS, ROWS, ROWS), jnp.bfloat16),
            jax.ShapeDtypeStruct((ROWS, 128), jnp.float32),
            jax.ShapeDtypeStruct((ROWS, HALF), jnp.float32),
        ],
        compiler_params=limit(20),
        cost_estimate=SMALL,
        name="fine_probs",
    )(info, q, ka, ko, kc, vo, vc, *ks)


def mix_kernel(
    info, far_ref, mid_ref, near_ref, l_ref, acc_ref, va_ref, vs_ref,
    out_ref, pool_ref, tail_ref,
):
    core = info[1]

    def mix(with_near):
        j = lax.broadcasted_iota(jnp.int32, (40, ROWS), 0)
        r = lax.broadcasted_iota(jnp.int32, (40, ROWS), 1)
        pick = jnp.where((r > SHORT * j - SHORT) & (r <= SHORT * j), 1.0, 0.0)
        pick = pick.astype(jnp.bfloat16)
        for head in range(LOCAL_HEADS):
            columns = slice(head * HEAD, (head + 1) * HEAD)
            mixed = acc_ref[:, columns] + jnp.dot(
                mid_ref[head], va_ref[TILE : 2 * TILE, columns],
                preferred_element_type=jnp.float32,
            )
            if with_near:
                mixed = mixed + jnp.dot(
                    near_ref[head], vs_ref[:, columns], preferred_element_type=jnp.float32
                )
            first = mixed[0:TILE, :] + jnp.dot(
                far_ref[head], va_ref[0:TILE, columns], preferred_element_type=jnp.float32
            )
            mixed = jnp.concatenate([first, mixed[TILE : 2 * TILE, :]], 0)
            out = (mixed / l_ref[:, head : head + 1]).astype(jnp.bfloat16)
            out_ref[:, columns] = out
            sums = jnp.dot(pick, out, preferred_element_type=jnp.float32)
            sums = sums * (1.0 / SHORT)
            pool_ref[:, columns] = sums[0:CROWS, :]
            tail_ref[:, columns] = sums[CROWS : CROWS + 8, :]

    @pl.when(core == 0)
    def _():
        mix(True)

    @pl.when(core == 1)
    def _():
        mix(False)


def fine_mix(info, far, mid, near, l, acc, va, vs):
    whole = pl.BlockSpec(memory_space=pltpu.VMEM)
    return pl.pallas_call(
        mix_kernel,
        in_specs=[pl.BlockSpec(memory_space=pltpu.SMEM)] + [whole] * 7,
        out_specs=[whole] * 3,
        out_shape=[
            jax.ShapeDtypeStruct((ROWS, HALF), jnp.bfloat16),
            jax.ShapeDtypeStruct((CROWS, HALF), jnp.float32),
            jax.ShapeDtypeStruct((8, HALF), jnp.float32),
        ],
        compiler_params=limit(20),
        cost_estimate=SMALL,
        name="fine_mix",
    )(info, far, mid, near, l, acc, va, vs)


def norm_kernel(own_ref, other_ref, gain_ref, other_gain_ref, out_ref):
    own = own_ref[...]
    other = other_ref[...]
    squares = jnp.sum(own * own, -1, keepdims=True) + jnp.sum(other * other, -1, keepdims=True)
    factor = lax.rsqrt(squares / D_FINE + EPS)
    out_ref[:, 0:HALF] = (own * factor * gain_ref[...]).astype(jnp.bfloat16)
    out_ref[:, HALF : 2 * HALF] = (other * factor * other_gain_ref[...]).astype(jnp.bfloat16)


def normalise(own, other, gain, other_gain):
    whole = pl.BlockSpec(memory_space=pltpu.VMEM)
    return pl.pallas_call(
        norm_kernel,
        in_specs=[whole] * 4,
        out_specs=whole,
        out_shape=jax.ShapeDtypeStruct((CROWS, 2 * HALF), jnp.bfloat16),
        compiler_params=limit(4),
        cost_estimate=SMALL,
        name="normalise",
    )(own, other, gain, other_gain)


def project_kernel(info, *refs):
    row_refs, own_ref, far_refs, (kv_ref, key_ref, rows_ref, w_ref) = (
        refs[0:4], refs[4], refs[5:13], refs[13:],
    )
    c, x, y = info[1], info[2], info[3]
    for k in range(4):
        begin = pl.multiple_of((y - k + 4) % 4 * CROWS, CROWS)
        rows_ref[pl.ds(begin, CROWS), :] = row_refs[k][...]
    size = HALF // 8
    for piece in range(8):
        from_x = (x - piece // 2 + 4) % 4
        from_c = c if piece % 2 == 0 else 1 - c
        begin = pl.multiple_of((from_x * 2 + from_c) * size, size)
        w_ref[pl.ds(begin, size), :] = far_refs[piece][...]
    kv = jnp.dot(rows_ref[:, 0:HALF], own_ref[...], preferred_element_type=jnp.float32)
    kv = kv + jnp.dot(
        rows_ref[:, HALF : 2 * HALF], w_ref[...], preferred_element_type=jnp.float32
    )
    kv = kv.astype(jnp.bfloat16)
    kv_ref[...] = kv
    key_ref[...] = kv[:, 0:C_HEAD]


def project(info, rows, own, far):
    whole = pl.BlockSpec(memory_space=pltpu.VMEM)
    return pl.pallas_call(
        project_kernel,
        in_specs=[pl.BlockSpec(memory_space=pltpu.SMEM)] + [whole] * 13,
        out_specs=[whole, whole],
        out_shape=[
            jax.ShapeDtypeStruct((GROUP, 2 * C_HEAD), jnp.bfloat16),
            jax.ShapeDtypeStruct((GROUP, C_HEAD), jnp.bfloat16),
        ],
        scratch_shapes=[
            pltpu.VMEM((GROUP, 2 * HALF), jnp.bfloat16),
            pltpu.VMEM((HALF, 2 * C_HEAD), jnp.bfloat16),
        ],
        compiler_params=limit(20),
        cost_estimate=SMALL,
        name="project",
    )(info, *rows, own, *far)


def split3(value):
    first = value.astype(jnp.bfloat16).astype(jnp.float32)
    rest = value - first
    second = rest.astype(jnp.bfloat16).astype(jnp.float32)
    return first, second, rest - second


def coarse_kernel(info, *refs):
    q_refs, kv_refs, out_ref, kv_all = refs[0:3], refs[3:11], refs[11], refs[12]
    x, z, c = info[2], info[4], info[1]
    scale = 1.0 / math.sqrt(C_HEAD)
    keys = 8 * GROUP
    for piece in range(8):
        kv_all[piece * GROUP : (piece + 1) * GROUP, :] = kv_refs[piece][...]
    slot = lax.broadcasted_iota(jnp.int32, (1, keys), 1)
    piece = slot // GROUP
    inside = slot % GROUP
    from_x = (x - piece // 2 + 4) % 4
    from_c = jnp.where(piece % 2 == 0, c, 1 - c)
    key_pos = (
        from_x * 1024 + (inside // CROWS) * 256 + z * 64 + from_c * 32 + inside % CROWS
    )
    inner = lax.broadcasted_iota(jnp.int32, (GROUP, 1), 0)
    lane = lax.broadcasted_iota(jnp.int32, (GROUP, 128), 1)
    for k in range(4):
        from_z = jnp.bitwise_xor(z, k)
        if k < 2:
            query = q_refs[k][...]
        else:
            query = q_refs[2][(k - 2) * GROUP : (k - 1) * GROUP, :]
        pos = x * 1024 + (inner // CROWS) * 256 + from_z * 64 + c * 32 + inner % CROWS
        allowed = key_pos < jnp.maximum(pos, 1)
        s = lax.dot_general(
            query, kv_all[:, 0:C_HEAD], (((1,), (1,)), ((), ())),
            preferred_element_type=jnp.float32,
        ) * scale
        s = jnp.where(allowed, s, NEG)
        top = jnp.max(s, -1, keepdims=True)
        p = jnp.where(allowed, jnp.exp(s - top), 0.0)
        total = jnp.sum(p, -1, keepdims=True)
        mixed = jnp.dot(
            p.astype(jnp.bfloat16), kv_all[:, C_HEAD : 2 * C_HEAD],
            preferred_element_type=jnp.float32,
        )
        some = total > 0.0
        safe = jnp.where(some, total, 1.0)
        mixed = jnp.where(some, mixed / safe, 0.0)
        level = jnp.where(some, top + jnp.log(safe), NEG)
        a, b, d = split3(level)
        extra = jnp.where(lane == 0, a, jnp.where(lane == 1, b, jnp.where(lane == 2, d, 0.0)))
        for y in range(4):
            rows = slice(y * CROWS, (y + 1) * CROWS)
            out_ref[y * 4 + from_z, :, 0:C_HEAD] = mixed[rows, :].astype(jnp.bfloat16)
            out_ref[y * 4 + from_z, :, C_HEAD : C_HEAD + 128] = extra[rows, :].astype(
                jnp.bfloat16
            )


def coarse_attend(info, queries, pairs):
    whole = pl.BlockSpec(memory_space=pltpu.VMEM)
    return pl.pallas_call(
        coarse_kernel,
        grid=(1,),
        in_specs=[pl.BlockSpec(memory_space=pltpu.SMEM)]
        + [pl.BlockSpec((GROUP, C_HEAD), lambda i: (0, 0))]
        + [whole] * 2
        + [pl.BlockSpec((GROUP, 2 * C_HEAD), lambda i: (0, 0))]
        + [whole] * 7,
        out_specs=whole,
        out_shape=jax.ShapeDtypeStruct((16, CROWS, C_HEAD + 128), jnp.bfloat16),
        scratch_shapes=[pltpu.VMEM((8 * GROUP, 2 * C_HEAD), jnp.bfloat16)],
        compiler_params=limit(16),
        cost_estimate=pl.CostEstimate(
            flops=4 * 4 * GROUP * 8 * GROUP * C_HEAD,
            bytes_accessed=2 * MIB,
            transcendentals=4 * GROUP * 8 * GROUP,
        ),
        name="coarse_attend",
    )(info, *queries, *pairs)


def final_kernel(part_ref, fine_ref, out_ref):
    parts = part_ref[...].astype(jnp.float32)
    levels = jnp.sum(parts[:, :, C_HEAD : C_HEAD + 128], -1, keepdims=True)
    top = jnp.max(levels, 0, keepdims=True)
    weights = jnp.exp(levels - top)
    total = jnp.sum(weights, 0)
    mixed = jnp.sum(parts[:, :, 0:C_HEAD] * weights, 0) / total
    coarse = mixed.astype(jnp.bfloat16)
    r = lax.broadcasted_iota(jnp.int32, (ROWS, CROWS), 0)
    j = lax.broadcasted_iota(jnp.int32, (ROWS, CROWS), 1)
    spread = jnp.where(r // SHORT == j, 1.0, 0.0).astype(jnp.bfloat16)
    up = jnp.dot(spread, coarse, preferred_element_type=jnp.float32)
    out_ref[...] = (fine_ref[...].astype(jnp.float32) + up).astype(jnp.bfloat16)


def finish(parts, fine):
    column = pl.BlockSpec((ROWS, C_HEAD), lambda h: (0, h))
    return pl.pallas_call(
        final_kernel,
        grid=(4,),
        in_specs=[pl.BlockSpec((4, CROWS, C_HEAD + 128), lambda h: (h, 0, 0)), column],
        out_specs=column,
        out_shape=jax.ShapeDtypeStruct((ROWS, HALF), jnp.bfloat16),
        compiler_params=limit(16),
        name="finish",
    )(parts, fine)


def per_device(fine_q, fine_k, fine_v, norm_gain, short_weight):
    x, y, z, c, m = (lax.axis_index(a) for a in CTX + ("m",))
    index = ((x * 4 + y) * 4 + z) * 2 + c
    info = jnp.stack([index, c, x, y, z, m]).astype(jnp.int32)

    k2 = shifted(fine_k, 2)
    v2 = shifted(fine_v, 2)
    ko = rolled(fine_k, "c", 1)
    vo = rolled(fine_v, "c", 1)
    part, own_columns = pick_columns(info, short_weight)
    other_gain = rolled(norm_gain[None], "m", 1)
    k2, part = lax.optimization_barrier((k2, part))
    ks = [rolled(piece, "c", 1) for piece in halves(k2)]
    far, mid, near, l, acc = fine_probs(info, fine_q, k2, ks, ko, fine_k, vo, fine_v)
    v2, l = lax.optimization_barrier((v2, l))
    vs = rolled(v2, "c", 1)
    fine_out, pooled, tail = fine_mix(info, far, mid, near, l, acc, v2, vs)

    part = rolled(part, "m", 1)
    pooled = add_tail(pooled, shifted(tail, 1))
    part, pooled = lax.optimization_barrier((part, pooled))
    columns = []
    for piece in [part] + [rolled(part, "x", k) for k in (1, 2, 3)]:
        columns += [piece, rolled(piece, "c", 1)]

    other = rolled(pooled, "m", 1)
    normed = normalise(pooled, other, norm_gain[None], other_gain)
    rows = [normed] + [rolled(normed, "y", k) for k in (1, 2, 3)]
    kv, own_keys = project(info, rows, own_columns, columns)

    next_keys = paired(own_keys, "z", 1)
    along = [rolled(kv, "x", k) for k in (1, 2, 3)]
    far_keys = paired(stacked(own_keys, next_keys), "z", 2)
    queries = [own_keys, next_keys, far_keys]
    pairs = []
    for piece in [kv] + along:
        pairs += [piece, rolled(piece, "c", 1)]
    parts = coarse_attend(info, queries, pairs)
    parts = lax.all_to_all(parts, ("y", "z"), split_axis=0, concat_axis=0, tiled=True)
    return finish(parts, fine_out)


def solution(mesh):
    grid = Mesh(mesh.devices.reshape(4, 4, 4, 2, 2), ("x", "y", "z", "c", "m"))
    rows = P(CTX, "m")
    return jax.shard_map(
        per_device,
        mesh=grid,
        in_specs=(rows, rows, rows, P("m"), P("m", None)),
        out_specs=rows,
        check_vma=False,
    )
```

```python
import functools
import math

import jax
import jax.numpy as jnp
from jax import lax
from jax.experimental import pallas as pl
from jax.experimental.pallas import tpu as pltpu
from jax.sharding import Mesh
from jax.sharding import PartitionSpec as P

D_FINE = 2048
HEADS = 16
HEAD = 128
C_HEADS = 8
C_HEAD = 256
WINDOW = 1024
SHORT = 16
EPS = 1e-05
NEG = -1e30
LOG2E = 1.4426950408889634

ROWS = 512
HALF = 1024
LOCAL_HEADS = HALF // HEAD
TILE = 256
CROWS = ROWS // SHORT
GROUP = 4 * CROWS
SMALL = pl.CostEstimate(flops=1, bytes_accessed=1, transcendentals=0)
CTX = ("x", "y", "z", "c")
MIB = 1 << 20


def shifted(value, steps):
    count = 128
    return lax.ppermute(
        value, CTX, [(s, s + steps) for s in range(max(0, -steps), min(count, count - steps))]
    )


def rolled(value, axis, steps):
    count = lax.axis_size(axis)
    return lax.ppermute(value, axis, [(s, (s + steps) % count) for s in range(count)])


def paired(value, axis, distance):
    count = lax.axis_size(axis)
    return lax.ppermute(value, axis, [(s, s ^ distance) for s in range(count)])


def limit(mib):
    return pltpu.CompilerParams(vmem_limit_bytes=mib * MIB)


def halves_kernel(in_ref, low_ref, high_ref):
    low_ref[...] = in_ref[0:TILE, :]
    high_ref[...] = in_ref[TILE : 2 * TILE, :]


def halves(value):
    half = pl.BlockSpec((TILE, 512), lambda i: (0, i))
    return pl.pallas_call(
        halves_kernel,
        grid=(2,),
        in_specs=[pl.BlockSpec((ROWS, 512), lambda i: (0, i))],
        out_specs=[half] * 2,
        out_shape=[jax.ShapeDtypeStruct((TILE, HALF), jnp.bfloat16)] * 2,
        compiler_params=limit(8),
        cost_estimate=SMALL,
        name="halves",
    )(value)


def pick_kernel(info, part_ref, own_ref, part_out, own_out):
    part_out[...] = part_ref[...]
    own_out[...] = own_ref[...]


def pick_columns(info, weight):
    wide = 2 * C_HEAD
    size = HALF // 8
    part = pl.BlockSpec(
        (size, wide), lambda i, info: (info[2] * 2 + info[1], (1 - info[5]) * 4 + info[3])
    )
    own = pl.BlockSpec((HALF // 4, wide), lambda i, info: (i, info[5] * 4 + info[3]))
    return pl.pallas_call(
        pick_kernel,
        grid_spec=pltpu.PrefetchScalarGridSpec(
            num_scalar_prefetch=1,
            grid=(4,),
            in_specs=[part, own],
            out_specs=[
                pl.BlockSpec((size, wide), lambda i, info: (0, 0)),
                pl.BlockSpec((HALF // 4, wide), lambda i, info: (i, 0)),
            ],
        ),
        out_shape=[
            jax.ShapeDtypeStruct((size, wide), jnp.bfloat16),
            jax.ShapeDtypeStruct((HALF, wide), jnp.bfloat16),
        ],
        compiler_params=limit(8),
        cost_estimate=pl.CostEstimate(flops=1 << 30, bytes_accessed=2 * MIB, transcendentals=0),
        name="pick_columns",
    )(info, weight, weight)


def start_kernel(pool_ref, tail_ref, gain_ref, out_ref):
    row = lax.broadcasted_iota(jnp.int32, (CROWS, 1), 0)
    pooled = pool_ref[...] + jnp.where(row == 0, tail_ref[0:1, :], 0.0)
    out_ref[:, 0:HALF] = pooled * gain_ref[...]
    out_ref[:, HALF : HALF + 128] = jnp.broadcast_to(
        jnp.sum(pooled * pooled, -1, keepdims=True), (CROWS, 128)
    )


def add_tail(pooled, tail, gain):
    whole = pl.BlockSpec(memory_space=pltpu.VMEM)
    return pl.pallas_call(
        start_kernel,
        in_specs=[whole] * 3,
        out_specs=whole,
        out_shape=jax.ShapeDtypeStruct((CROWS, HALF + 128), jnp.float32),
        compiler_params=limit(4),
        cost_estimate=SMALL,
        name="add_tail",
    )(pooled, tail, gain)


def attend(q, pieces, store):
    scale = LOG2E / math.sqrt(HEAD)
    scores = []
    top = None
    for keys, okay, mask in pieces:
        s = lax.dot_general(
            q, keys, (((1,), (1,)), ((), ())), preferred_element_type=jnp.float32
        )
        if mask is not None:
            s = jnp.where(mask, s, NEG)
        scores.append(s)
        high = jnp.max(s, -1, keepdims=True)
        if okay is not None:
            high = jnp.where(okay, high, NEG)
        top = high if top is None else jnp.maximum(top, high)
    total = jnp.zeros((q.shape[0], 1), jnp.float32)
    for step, (keys, okay, mask) in enumerate(pieces):
        base = top if okay is None else jnp.where(okay, top, -NEG)
        p = jnp.exp2((scores[step] - base) * scale)
        total = total + jnp.sum(p, -1, keepdims=True)
        store(step, p.astype(jnp.bfloat16))
    return total


def probs_kernel(
    pieces, info, q_ref, ka_ref, ko_ref, kc_ref, vo_ref, vc_ref, *refs
):
    ks_refs, (far_ref, mid_ref, near_ref, l_ref, acc_ref) = refs[:pieces], refs[pieces:]
    head = pl.program_id(0)
    index = info[0]
    core = info[1]
    kb = jnp.where(core == 0, jnp.concatenate([r[...] for r in ks_refs], 0), ko_ref[...])
    chunks = [
        ka_ref[0:TILE, :],
        ka_ref[TILE : 2 * TILE, :],
        kb[0:TILE, :],
        kb[TILE : 2 * TILE, :],
        kc_ref[0:TILE, :],
        kc_ref[TILE : 2 * TILE, :],
    ]
    valid = [index >= 2, index >= 2, index >= 1, index >= 1, None, None]
    row = lax.broadcasted_iota(jnp.int32, (TILE, TILE), 0)
    col = lax.broadcasted_iota(jnp.int32, (TILE, TILE), 1)
    lane = lax.broadcasted_iota(jnp.int32, (TILE, 128), 1)
    for tile in range(ROWS // TILE):
        masks = [col > row, None, None, None, col <= row]
        keys = [(chunks[tile + j], valid[tile + j], masks[j]) for j in range(5)]
        rows = slice(tile * TILE, (tile + 1) * TILE)

        def store(step, p, tile=tile, rows=rows):
            chunk = tile + step
            if chunk == 0:
                far_ref[0] = p
            elif chunk == 1:
                mid_ref[0, rows, :] = p
            elif chunk < 4:
                near_ref[0, rows, (chunk - 2) * TILE : (chunk - 1) * TILE] = p
            else:
                values = vc_ref[(chunk - 4) * TILE : (chunk - 3) * TILE, :]
                part = jnp.dot(p, values, preferred_element_type=jnp.float32)
                if chunk == 5:
                    part = part + acc_ref[rows, :]
                acc_ref[rows, :] = part

        total = attend(q_ref[rows, :], keys, store)
        l_ref[rows, :] = jnp.where(lane == head, total, l_ref[rows, :])

    @pl.when(core == 1)
    def _():
        acc_ref[...] = acc_ref[...] + jnp.dot(
            near_ref[0], vo_ref[...], preferred_element_type=jnp.float32
        )


def fine_probs(info, q, ka, ks, ko, kc, vo, vc):
    column = pl.BlockSpec((ROWS, HEAD), lambda h, info: (0, h))
    piece = pl.BlockSpec((ROWS // len(ks), HEAD), lambda h, info: (0, h))
    return pl.pallas_call(
        functools.partial(probs_kernel, len(ks)),
        grid_spec=pltpu.PrefetchScalarGridSpec(
            num_scalar_prefetch=1,
            grid=(LOCAL_HEADS,),
            in_specs=[column] * 6 + [piece] * len(ks),
            out_specs=[
                pl.BlockSpec((1, TILE, TILE), lambda h, info: (h, 0, 0)),
                pl.BlockSpec((1, ROWS, TILE), lambda h, info: (h, 0, 0)),
                pl.BlockSpec((1, ROWS, ROWS), lambda h, info: (h, 0, 0)),
                pl.BlockSpec((ROWS, 128), lambda h, info: (0, 0)),
                column,
            ],
        ),
        out_shape=[
            jax.ShapeDtypeStruct((LOCAL_HEADS, TILE, TILE), jnp.bfloat16),
            jax.ShapeDtypeStruct((LOCAL_HEADS, ROWS, TILE), jnp.bfloat16),
            jax.ShapeDtypeStruct((LOCAL_HEADS, ROWS, ROWS), jnp.bfloat16),
            jax.ShapeDtypeStruct((ROWS, 128), jnp.float32),
            jax.ShapeDtypeStruct((ROWS, HALF), jnp.float32),
        ],
        compiler_params=limit(20),
        cost_estimate=SMALL,
        name="fine_probs",
    )(info, q, ka, ko, kc, vo, vc, *ks)


def last_kernel(info, mid_ref, near_ref, l_ref, acc_ref, va_ref, vs_ref, tail_ref):
    core = info[1]
    rows = slice(ROWS - SHORT, ROWS)

    def mix(with_near):
        j = lax.broadcasted_iota(jnp.int32, (8, SHORT), 0)
        r = lax.broadcasted_iota(jnp.int32, (8, SHORT), 1)
        pick = jnp.where((j == 0) & (r > 0), 1.0, 0.0).astype(jnp.bfloat16)
        for head in range(LOCAL_HEADS):
            columns = slice(head * HEAD, (head + 1) * HEAD)
            mixed = acc_ref[rows, columns] + jnp.dot(
                mid_ref[head, rows, :], va_ref[TILE : 2 * TILE, columns],
                preferred_element_type=jnp.float32,
            )
            if with_near:
                mixed = mixed + jnp.dot(
                    near_ref[head, rows, :], vs_ref[:, columns],
                    preferred_element_type=jnp.float32,
                )
            out = (mixed / l_ref[rows, head : head + 1]).astype(jnp.bfloat16)
            sums = jnp.dot(pick, out, preferred_element_type=jnp.float32)
            tail_ref[:, columns] = sums * (1.0 / SHORT)

    @pl.when(core == 0)
    def _():
        mix(True)

    @pl.when(core == 1)
    def _():
        mix(False)


def last_rows(info, mid, near, l, acc, va, vs):
    whole = pl.BlockSpec(memory_space=pltpu.VMEM)
    return pl.pallas_call(
        last_kernel,
        in_specs=[pl.BlockSpec(memory_space=pltpu.SMEM)] + [whole] * 6,
        out_specs=whole,
        out_shape=jax.ShapeDtypeStruct((8, HALF), jnp.float32),
        compiler_params=limit(16),
        cost_estimate=SMALL,
        name="last_rows",
    )(info, mid, near, l, acc, va, vs)


def mix_kernel(
    info, far_ref, mid_ref, near_ref, l_ref, acc_ref, va_ref, vs_ref, out_ref, pool_ref
):
    core = info[1]

    def mix(with_near):
        j = lax.broadcasted_iota(jnp.int32, (CROWS, ROWS), 0)
        r = lax.broadcasted_iota(jnp.int32, (CROWS, ROWS), 1)
        pick = jnp.where((r > SHORT * j - SHORT) & (r <= SHORT * j), 1.0, 0.0)
        pick = pick.astype(jnp.bfloat16)
        for head in range(LOCAL_HEADS):
            columns = slice(head * HEAD, (head + 1) * HEAD)
            mixed = acc_ref[:, columns] + jnp.dot(
                mid_ref[head], va_ref[TILE : 2 * TILE, columns],
                preferred_element_type=jnp.float32,
            )
            if with_near:
                mixed = mixed + jnp.dot(
                    near_ref[head], vs_ref[:, columns], preferred_element_type=jnp.float32
                )
            first = mixed[0:TILE, :] + jnp.dot(
                far_ref[head], va_ref[0:TILE, columns], preferred_element_type=jnp.float32
            )
            mixed = jnp.concatenate([first, mixed[TILE : 2 * TILE, :]], 0)
            out = (mixed / l_ref[:, head : head + 1]).astype(jnp.bfloat16)
            out_ref[:, columns] = out
            sums = jnp.dot(pick, out, preferred_element_type=jnp.float32)
            pool_ref[:, columns] = sums * (1.0 / SHORT)

    @pl.when(core == 0)
    def _():
        mix(True)

    @pl.when(core == 1)
    def _():
        mix(False)


def fine_mix(info, far, mid, near, l, acc, va, vs):
    whole = pl.BlockSpec(memory_space=pltpu.VMEM)
    return pl.pallas_call(
        mix_kernel,
        in_specs=[pl.BlockSpec(memory_space=pltpu.SMEM)] + [whole] * 7,
        out_specs=[whole] * 2,
        out_shape=[
            jax.ShapeDtypeStruct((ROWS, HALF), jnp.bfloat16),
            jax.ShapeDtypeStruct((CROWS, HALF), jnp.float32),
        ],
        compiler_params=limit(20),
        cost_estimate=pl.CostEstimate(flops=1 << 30, bytes_accessed=8 * MIB, transcendentals=0),
        name="fine_mix",
    )(info, far, mid, near, l, acc, va, vs)


def norm_kernel(own_ref, other_ref, out_ref):
    squares = own_ref[:, HALF : HALF + 1] + other_ref[:, HALF : HALF + 1]
    factor = lax.rsqrt(squares / D_FINE + EPS)
    out_ref[:, 0:HALF] = (own_ref[:, 0:HALF] * factor).astype(jnp.bfloat16)
    out_ref[:, HALF : 2 * HALF] = (other_ref[:, 0:HALF] * factor).astype(jnp.bfloat16)


def normalise(own, other):
    whole = pl.BlockSpec(memory_space=pltpu.VMEM)
    return pl.pallas_call(
        norm_kernel,
        in_specs=[whole] * 2,
        out_specs=whole,
        out_shape=jax.ShapeDtypeStruct((CROWS, 2 * HALF), jnp.bfloat16),
        compiler_params=limit(4),
        cost_estimate=SMALL,
        name="normalise",
    )(own, other)


def project_kernel(info, *refs):
    row_refs, own_ref, far_refs, (kv_ref, key_ref, rows_ref, w_ref) = (
        refs[0:4], refs[4], refs[5:13], refs[13:],
    )
    c, x, y = info[1], info[2], info[3]
    for k in range(4):
        begin = pl.multiple_of((y - k + 4) % 4 * CROWS, CROWS)
        rows_ref[pl.ds(begin, CROWS), :] = row_refs[k][...]
    size = HALF // 8
    for piece in range(8):
        from_x = (x - piece // 2 + 4) % 4
        from_c = c if piece % 2 == 0 else 1 - c
        begin = pl.multiple_of((from_x * 2 + from_c) * size, size)
        w_ref[pl.ds(begin, size), :] = far_refs[piece][...]
    kv = jnp.dot(rows_ref[:, 0:HALF], own_ref[...], preferred_element_type=jnp.float32)
    kv = kv + jnp.dot(
        rows_ref[:, HALF : 2 * HALF], w_ref[...], preferred_element_type=jnp.float32
    )
    kv = kv.astype(jnp.bfloat16)
    kv_ref[...] = kv
    key_ref[...] = kv[:, 0:C_HEAD]


def project(info, rows, own, far):
    whole = pl.BlockSpec(memory_space=pltpu.VMEM)
    return pl.pallas_call(
        project_kernel,
        in_specs=[pl.BlockSpec(memory_space=pltpu.SMEM)] + [whole] * 13,
        out_specs=[whole, whole],
        out_shape=[
            jax.ShapeDtypeStruct((GROUP, 2 * C_HEAD), jnp.bfloat16),
            jax.ShapeDtypeStruct((GROUP, C_HEAD), jnp.bfloat16),
        ],
        scratch_shapes=[
            pltpu.VMEM((GROUP, 2 * HALF), jnp.bfloat16),
            pltpu.VMEM((HALF, 2 * C_HEAD), jnp.bfloat16),
        ],
        compiler_params=limit(20),
        cost_estimate=SMALL,
        name="project",
    )(info, *rows, own, *far)


def split3(value):
    first = value.astype(jnp.bfloat16).astype(jnp.float32)
    rest = value - first
    second = rest.astype(jnp.bfloat16).astype(jnp.float32)
    return first, second, rest - second


def coarse_kernel(info, *refs):
    q_refs, kv_refs, (out_ref, kv_all, q_all) = refs[0:4], refs[4:12], refs[12:]
    x, z, c = info[2], info[4], info[1]
    scale = 1.0 / math.sqrt(C_HEAD)
    keys = 8 * GROUP
    for piece in range(8):
        kv_all[piece * GROUP : (piece + 1) * GROUP, :] = kv_refs[piece][...]
    for k in range(4):
        begin = pl.multiple_of(jnp.bitwise_xor(z, k) * GROUP, GROUP)
        q_all[pl.ds(begin, GROUP), :] = q_refs[k][...]
    slot = lax.broadcasted_iota(jnp.int32, (1, keys), 1)
    piece = slot // GROUP
    inside = slot % GROUP
    from_x = (x - piece // 2 + 4) % 4
    from_c = jnp.where(piece % 2 == 0, c, 1 - c)
    key_pos = (
        from_x * 1024 + (inside // CROWS) * 256 + z * 64 + from_c * 32 + inside % CROWS
    )
    place = lax.broadcasted_iota(jnp.int32, (4 * GROUP, 1), 0)
    inner = place % GROUP
    pos = x * 1024 + (inner // CROWS) * 256 + (place // GROUP) * 64 + c * 32 + inner % CROWS
    lane = lax.broadcasted_iota(jnp.int32, (4 * GROUP, 128), 1)
    allowed = key_pos < jnp.maximum(pos, 1)
    s = lax.dot_general(
        q_all[...], kv_all[:, 0:C_HEAD], (((1,), (1,)), ((), ())),
        preferred_element_type=jnp.float32,
    ) * scale
    s = jnp.where(allowed, s, NEG)
    top = jnp.max(s, -1, keepdims=True)
    p = jnp.where(allowed, jnp.exp(s - top), 0.0)
    total = jnp.sum(p, -1, keepdims=True)
    mixed = jnp.dot(
        p.astype(jnp.bfloat16), kv_all[:, C_HEAD : 2 * C_HEAD],
        preferred_element_type=jnp.float32,
    )
    some = total > 0.0
    safe = jnp.where(some, total, 1.0)
    mixed = jnp.where(some, mixed / safe, 0.0).astype(jnp.bfloat16)
    level = jnp.where(some, top + jnp.log(safe), NEG)
    a, b, d = split3(level)
    extra = jnp.where(lane == 0, a, jnp.where(lane == 1, b, jnp.where(lane == 2, d, 0.0)))
    extra = extra.astype(jnp.bfloat16)
    for from_z in range(4):
        for y in range(4):
            rows = slice(from_z * GROUP + y * CROWS, from_z * GROUP + (y + 1) * CROWS)
            out_ref[y * 4 + from_z, :, 0:C_HEAD] = mixed[rows, :]
            out_ref[y * 4 + from_z, :, C_HEAD : C_HEAD + 128] = extra[rows, :]


def coarse_attend(info, queries, pairs):
    whole = pl.BlockSpec(memory_space=pltpu.VMEM)
    return pl.pallas_call(
        coarse_kernel,
        grid=(1,),
        in_specs=[pl.BlockSpec(memory_space=pltpu.SMEM)]
        + [pl.BlockSpec((GROUP, C_HEAD), lambda i: (0, 0))]
        + [whole] * 3
        + [pl.BlockSpec((GROUP, 2 * C_HEAD), lambda i: (0, 0))]
        + [whole] * 7,
        out_specs=whole,
        out_shape=jax.ShapeDtypeStruct((16, CROWS, C_HEAD + 128), jnp.bfloat16),
        scratch_shapes=[
            pltpu.VMEM((8 * GROUP, 2 * C_HEAD), jnp.bfloat16),
            pltpu.VMEM((4 * GROUP, C_HEAD), jnp.bfloat16),
        ],
        compiler_params=limit(16),
        cost_estimate=pl.CostEstimate(
            flops=4 * 4 * GROUP * 8 * GROUP * C_HEAD,
            bytes_accessed=2 * MIB,
            transcendentals=4 * GROUP * 8 * GROUP,
        ),
        name="coarse_attend",
    )(info, *queries, *pairs)


def final_kernel(part_ref, fine_ref, out_ref):
    parts = part_ref[...].astype(jnp.float32)
    levels = jnp.sum(parts[:, :, C_HEAD : C_HEAD + 128], -1, keepdims=True)
    top = jnp.max(levels, 0, keepdims=True)
    weights = jnp.exp(levels - top)
    total = jnp.sum(weights, 0)
    mixed = jnp.sum(parts[:, :, 0:C_HEAD] * weights, 0) / total
    coarse = mixed.astype(jnp.bfloat16)
    r = lax.broadcasted_iota(jnp.int32, (ROWS, CROWS), 0)
    j = lax.broadcasted_iota(jnp.int32, (ROWS, CROWS), 1)
    spread = jnp.where(r // SHORT == j, 1.0, 0.0).astype(jnp.bfloat16)
    up = jnp.dot(spread, coarse, preferred_element_type=jnp.float32)
    out_ref[...] = (fine_ref[...].astype(jnp.float32) + up).astype(jnp.bfloat16)


def finish(parts, fine):
    column = pl.BlockSpec((ROWS, C_HEAD), lambda h: (0, h))
    return pl.pallas_call(
        final_kernel,
        grid=(4,),
        in_specs=[pl.BlockSpec((4, CROWS, C_HEAD + 128), lambda h: (h, 0, 0)), column],
        out_specs=column,
        out_shape=jax.ShapeDtypeStruct((ROWS, HALF), jnp.bfloat16),
        compiler_params=limit(16),
        name="finish",
    )(parts, fine)


def per_device(fine_q, fine_k, fine_v, norm_gain, short_weight):
    x, y, z, c, m = (lax.axis_index(a) for a in CTX + ("m",))
    index = ((x * 4 + y) * 4 + z) * 2 + c
    info = jnp.stack([index, c, x, y, z, m]).astype(jnp.int32)

    k2 = shifted(fine_k, 2)
    v2 = shifted(fine_v, 2)
    ko = rolled(fine_k, "c", 1)
    vo = rolled(fine_v, "c", 1)
    part, own_columns = pick_columns(info, short_weight)
    k2, part = lax.optimization_barrier((k2, part))
    ks = [rolled(piece, "c", 1) for piece in halves(k2)]
    far, mid, near, l, acc = fine_probs(info, fine_q, k2, ks, ko, fine_k, vo, fine_v)
    v2, l = lax.optimization_barrier((v2, l))
    vs = rolled(v2, "c", 1)
    tail = shifted(last_rows(info, mid, near, l, acc, v2, vs), 1)
    fine_out, pooled = fine_mix(info, far, mid, near, l, acc, v2, vs)

    part = rolled(part, "m", 1)
    pooled = add_tail(pooled, tail, norm_gain[None])
    part, pooled = lax.optimization_barrier((part, pooled))
    eighths = [part] + [rolled(part, "x", k) for k in (1, 2, 3)]

    other = rolled(pooled, "m", 1)
    normed = normalise(pooled, other)
    normed, *eighths = lax.optimization_barrier((normed, *eighths))
    columns = []
    for piece in eighths:
        columns += [piece, rolled(piece, "c", 1)]
    rows = [normed] + [rolled(normed, "y", k) for k in (1, 2, 3)]
    kv, own_keys = project(info, rows, own_columns, columns)

    queries = [own_keys] + [paired(own_keys, "z", k) for k in (1, 2, 3)]
    pieces = [kv] + [rolled(kv, "x", k) for k in (1, 2, 3)]
    held = lax.optimization_barrier((*queries, *pieces))
    queries, pieces = held[:4], held[4:]
    pairs = []
    for piece in pieces:
        pairs += [piece, rolled(piece, "c", 1)]
    parts = coarse_attend(info, queries, pairs)
    parts = lax.all_to_all(parts, ("y", "z"), split_axis=0, concat_axis=0, tiled=True)
    return finish(parts, fine_out)


def solution(mesh):
    grid = Mesh(mesh.devices.reshape(4, 4, 4, 2, 2), ("x", "y", "z", "c", "m"))
    rows = P(CTX, "m")
    return jax.shard_map(
        per_device,
        mesh=grid,
        in_specs=(rows, rows, rows, P("m"), P("m", None)),
        out_specs=rows,
        check_vma=False,
    )
```

```python
import functools
import math

import jax
import jax.numpy as jnp
from jax import lax
from jax.experimental import pallas as pl
from jax.experimental.pallas import tpu as pltpu
from jax.sharding import Mesh
from jax.sharding import PartitionSpec as P

D_FINE = 2048
HEADS = 16
HEAD = 128
C_HEADS = 8
C_HEAD = 256
WINDOW = 1024
SHORT = 16
EPS = 1e-05
NEG = -1e30
LOG2E = 1.4426950408889634

ROWS = 512
HALF = 1024
LOCAL_HEADS = HALF // HEAD
TILE = 256
CROWS = ROWS // SHORT
GROUP = 4 * CROWS
SMALL = pl.CostEstimate(flops=1, bytes_accessed=1, transcendentals=0)
CTX = ("x", "y", "z", "c")
MIB = 1 << 20


def shifted(value, steps):
    count = 128
    return lax.ppermute(
        value, CTX, [(s, s + steps) for s in range(max(0, -steps), min(count, count - steps))]
    )


def rolled(value, axis, steps):
    count = lax.axis_size(axis)
    return lax.ppermute(value, axis, [(s, (s + steps) % count) for s in range(count)])


def paired(value, axis, distance):
    count = lax.axis_size(axis)
    return lax.ppermute(value, axis, [(s, s ^ distance) for s in range(count)])


def limit(mib):
    return pltpu.CompilerParams(vmem_limit_bytes=mib * MIB)


def halves_kernel(in_ref, low_ref, high_ref):
    low_ref[...] = in_ref[0:TILE, :]
    high_ref[...] = in_ref[TILE : 2 * TILE, :]


def halves(value):
    half = pl.BlockSpec((TILE, 512), lambda i: (0, i))
    return pl.pallas_call(
        halves_kernel,
        grid=(2,),
        in_specs=[pl.BlockSpec((ROWS, 512), lambda i: (0, i))],
        out_specs=[half] * 2,
        out_shape=[jax.ShapeDtypeStruct((TILE, HALF), jnp.bfloat16)] * 2,
        compiler_params=limit(8),
        cost_estimate=SMALL,
        name="halves",
    )(value)


def pick_kernel(info, part_ref, own_ref, part_out, own_out):
    part_out[...] = part_ref[...]
    own_out[...] = own_ref[...]


def pick_columns(info, weight):
    wide = 2 * C_HEAD
    size = HALF // 8
    part = pl.BlockSpec(
        (size, wide), lambda i, info: (info[2] * 2 + info[1], (1 - info[5]) * 4 + info[3])
    )
    own = pl.BlockSpec((HALF // 4, wide), lambda i, info: (i, info[5] * 4 + info[3]))
    return pl.pallas_call(
        pick_kernel,
        grid_spec=pltpu.PrefetchScalarGridSpec(
            num_scalar_prefetch=1,
            grid=(4,),
            in_specs=[part, own],
            out_specs=[
                pl.BlockSpec((size, wide), lambda i, info: (0, 0)),
                pl.BlockSpec((HALF // 4, wide), lambda i, info: (i, 0)),
            ],
        ),
        out_shape=[
            jax.ShapeDtypeStruct((size, wide), jnp.bfloat16),
            jax.ShapeDtypeStruct((HALF, wide), jnp.bfloat16),
        ],
        compiler_params=limit(8),
        cost_estimate=pl.CostEstimate(flops=1 << 30, bytes_accessed=2 * MIB, transcendentals=0),
        name="pick_columns",
    )(info, weight, weight)


def start_kernel(pool_ref, tail_ref, gain_ref, out_ref):
    row = lax.broadcasted_iota(jnp.int32, (CROWS, 1), 0)
    pooled = pool_ref[...] + jnp.where(row == 0, tail_ref[0:1, :], 0.0)
    out_ref[:, 0:HALF] = pooled * gain_ref[...]
    out_ref[:, HALF : HALF + 128] = jnp.broadcast_to(
        jnp.sum(pooled * pooled, -1, keepdims=True), (CROWS, 128)
    )


def add_tail(pooled, tail, gain):
    whole = pl.BlockSpec(memory_space=pltpu.VMEM)
    return pl.pallas_call(
        start_kernel,
        in_specs=[whole] * 3,
        out_specs=whole,
        out_shape=jax.ShapeDtypeStruct((CROWS, HALF + 128), jnp.float32),
        compiler_params=limit(4),
        cost_estimate=SMALL,
        name="add_tail",
    )(pooled, tail, gain)


def attend(q, pieces, store):
    scale = LOG2E / math.sqrt(HEAD)
    scores = []
    top = None
    for keys, okay, mask in pieces:
        s = lax.dot_general(
            q, keys, (((1,), (1,)), ((), ())), preferred_element_type=jnp.float32
        )
        if mask is not None:
            s = jnp.where(mask, s, NEG)
        scores.append(s)
        high = jnp.max(s, -1, keepdims=True)
        if okay is not None:
            high = jnp.where(okay, high, NEG)
        top = high if top is None else jnp.maximum(top, high)
    total = jnp.zeros((q.shape[0], 1), jnp.float32)
    for step, (keys, okay, mask) in enumerate(pieces):
        base = top if okay is None else jnp.where(okay, top, -NEG)
        p = jnp.exp2((scores[step] - base) * scale)
        total = total + jnp.sum(p, -1, keepdims=True)
        store(step, p.astype(jnp.bfloat16))
    return total


def probs_kernel(
    pieces, info, q_ref, ka_ref, ko_ref, kc_ref, vo_ref, vc_ref, *refs
):
    ks_refs, (far_ref, mid_ref, near_ref, l_ref, acc_ref) = refs[:pieces], refs[pieces:]
    head = pl.program_id(0)
    index = info[0]
    core = info[1]
    kb = jnp.where(core == 0, jnp.concatenate([r[...] for r in ks_refs], 0), ko_ref[...])
    chunks = [
        ka_ref[0:TILE, :],
        ka_ref[TILE : 2 * TILE, :],
        kb[0:TILE, :],
        kb[TILE : 2 * TILE, :],
        kc_ref[0:TILE, :],
        kc_ref[TILE : 2 * TILE, :],
    ]
    valid = [index >= 2, index >= 2, index >= 1, index >= 1, None, None]
    row = lax.broadcasted_iota(jnp.int32, (TILE, TILE), 0)
    col = lax.broadcasted_iota(jnp.int32, (TILE, TILE), 1)
    lane = lax.broadcasted_iota(jnp.int32, (TILE, 128), 1)
    for tile in range(ROWS // TILE):
        masks = [col > row, None, None, None, col <= row]
        keys = [(chunks[tile + j], valid[tile + j], masks[j]) for j in range(5)]
        rows = slice(tile * TILE, (tile + 1) * TILE)

        def store(step, p, tile=tile, rows=rows):
            chunk = tile + step
            if chunk == 0:
                far_ref[0] = p
            elif chunk == 1:
                mid_ref[0, rows, :] = p
            elif chunk < 4:
                near_ref[0, rows, (chunk - 2) * TILE : (chunk - 1) * TILE] = p
            else:
                values = vc_ref[(chunk - 4) * TILE : (chunk - 3) * TILE, :]
                part = jnp.dot(p, values, preferred_element_type=jnp.float32)
                if chunk == 5:
                    part = part + acc_ref[rows, :]
                acc_ref[rows, :] = part

        total = attend(q_ref[rows, :], keys, store)
        before = jnp.where(head == 0, 1.0, l_ref[rows, :])
        l_ref[rows, :] = jnp.where(lane == head, total, before)

    @pl.when(core == 1)
    def _():
        acc_ref[...] = acc_ref[...] + jnp.dot(
            near_ref[0], vo_ref[...], preferred_element_type=jnp.float32
        )


def fine_probs(info, q, ka, ks, ko, kc, vo, vc):
    column = pl.BlockSpec((ROWS, HEAD), lambda h, info: (0, h))
    piece = pl.BlockSpec((ROWS // len(ks), HEAD), lambda h, info: (0, h))
    return pl.pallas_call(
        functools.partial(probs_kernel, len(ks)),
        grid_spec=pltpu.PrefetchScalarGridSpec(
            num_scalar_prefetch=1,
            grid=(LOCAL_HEADS,),
            in_specs=[column] * 6 + [piece] * len(ks),
            out_specs=[
                pl.BlockSpec((1, TILE, TILE), lambda h, info: (h, 0, 0)),
                pl.BlockSpec((1, ROWS, TILE), lambda h, info: (h, 0, 0)),
                pl.BlockSpec((1, ROWS, ROWS), lambda h, info: (h, 0, 0)),
                pl.BlockSpec((ROWS, 128), lambda h, info: (0, 0)),
                column,
            ],
        ),
        out_shape=[
            jax.ShapeDtypeStruct((LOCAL_HEADS, TILE, TILE), jnp.bfloat16),
            jax.ShapeDtypeStruct((LOCAL_HEADS, ROWS, TILE), jnp.bfloat16),
            jax.ShapeDtypeStruct((LOCAL_HEADS, ROWS, ROWS), jnp.bfloat16),
            jax.ShapeDtypeStruct((ROWS, 128), jnp.float32),
            jax.ShapeDtypeStruct((ROWS, HALF), jnp.float32),
        ],
        compiler_params=limit(20),
        cost_estimate=SMALL,
        name="fine_probs",
    )(info, q, ka, ko, kc, vo, vc, *ks)


def far_kernel(far_ref, mid_ref, acc_ref, va_ref, out_ref):
    for head in range(LOCAL_HEADS):
        columns = slice(head * HEAD, (head + 1) * HEAD)
        mixed = acc_ref[:, columns] + jnp.dot(
            mid_ref[head], va_ref[TILE : 2 * TILE, columns], preferred_element_type=jnp.float32
        )
        out_ref[0:TILE, columns] = mixed[0:TILE, :] + jnp.dot(
            far_ref[head], va_ref[0:TILE, columns], preferred_element_type=jnp.float32
        )
        out_ref[TILE : 2 * TILE, columns] = mixed[TILE : 2 * TILE, :]


def far_mix(far, mid, acc, va):
    whole = pl.BlockSpec(memory_space=pltpu.VMEM)
    return pl.pallas_call(
        far_kernel,
        in_specs=[whole] * 4,
        out_specs=whole,
        out_shape=jax.ShapeDtypeStruct((ROWS, HALF), jnp.float32),
        compiler_params=limit(16),
        cost_estimate=pl.CostEstimate(flops=1 << 30, bytes_accessed=8 * MIB, transcendentals=0),
        name="far_mix",
    )(far, mid, acc, va)


def last_kernel(info, near_ref, l_ref, acc_ref, vs_ref, tail_ref):
    core = info[1]
    rows = slice(ROWS - SHORT, ROWS)

    def mix(with_near):
        j = lax.broadcasted_iota(jnp.int32, (8, SHORT), 0)
        r = lax.broadcasted_iota(jnp.int32, (8, SHORT), 1)
        pick = jnp.where((j == 0) & (r > 0), 1.0, 0.0).astype(jnp.bfloat16)
        share = 1.0 / l_ref[rows, :]
        for head in range(LOCAL_HEADS):
            columns = slice(head * HEAD, (head + 1) * HEAD)
            mixed = acc_ref[rows, columns]
            if with_near:
                mixed = mixed + jnp.dot(
                    near_ref[head, rows, :], vs_ref[:, columns],
                    preferred_element_type=jnp.float32,
                )
            out = (mixed * share[:, head : head + 1]).astype(jnp.bfloat16)
            sums = jnp.dot(pick, out, preferred_element_type=jnp.float32)
            tail_ref[:, columns] = sums * (1.0 / SHORT)

    @pl.when(core == 0)
    def _():
        mix(True)

    @pl.when(core == 1)
    def _():
        mix(False)


def last_rows(info, near, l, acc, vs):
    whole = pl.BlockSpec(memory_space=pltpu.VMEM)
    return pl.pallas_call(
        last_kernel,
        in_specs=[pl.BlockSpec(memory_space=pltpu.SMEM)] + [whole] * 4,
        out_specs=whole,
        out_shape=jax.ShapeDtypeStruct((8, HALF), jnp.float32),
        compiler_params=limit(16),
        cost_estimate=SMALL,
        name="last_rows",
    )(info, near, l, acc, vs)


def mix_kernel(info, near_ref, l_ref, acc_ref, vs_ref, out_ref, pool_ref):
    core = info[1]

    def mix(with_near):
        j = lax.broadcasted_iota(jnp.int32, (CROWS, ROWS), 0)
        r = lax.broadcasted_iota(jnp.int32, (CROWS, ROWS), 1)
        pick = jnp.where((r > SHORT * j - SHORT) & (r <= SHORT * j), 1.0, 0.0)
        pick = pick.astype(jnp.bfloat16)
        share = 1.0 / l_ref[...]
        for head in range(LOCAL_HEADS):
            columns = slice(head * HEAD, (head + 1) * HEAD)
            mixed = acc_ref[:, columns]
            if with_near:
                mixed = mixed + jnp.dot(
                    near_ref[head], vs_ref[:, columns], preferred_element_type=jnp.float32
                )
            out = (mixed * share[:, head : head + 1]).astype(jnp.bfloat16)
            out_ref[:, columns] = out
            sums = jnp.dot(pick, out, preferred_element_type=jnp.float32)
            pool_ref[:, columns] = sums * (1.0 / SHORT)

    @pl.when(core == 0)
    def _():
        mix(True)

    @pl.when(core == 1)
    def _():
        mix(False)


def fine_mix(info, near, l, acc, vs):
    whole = pl.BlockSpec(memory_space=pltpu.VMEM)
    return pl.pallas_call(
        mix_kernel,
        in_specs=[pl.BlockSpec(memory_space=pltpu.SMEM)] + [whole] * 4,
        out_specs=[whole] * 2,
        out_shape=[
            jax.ShapeDtypeStruct((ROWS, HALF), jnp.bfloat16),
            jax.ShapeDtypeStruct((CROWS, HALF), jnp.float32),
        ],
        compiler_params=limit(20),
        cost_estimate=pl.CostEstimate(flops=1 << 30, bytes_accessed=8 * MIB, transcendentals=0),
        name="fine_mix",
    )(info, near, l, acc, vs)


def norm_kernel(own_ref, other_ref, out_ref):
    squares = own_ref[:, HALF : HALF + 1] + other_ref[:, HALF : HALF + 1]
    factor = lax.rsqrt(squares / D_FINE + EPS)
    out_ref[:, 0:HALF] = (own_ref[:, 0:HALF] * factor).astype(jnp.bfloat16)
    out_ref[:, HALF : 2 * HALF] = (other_ref[:, 0:HALF] * factor).astype(jnp.bfloat16)


def normalise(own, other):
    whole = pl.BlockSpec(memory_space=pltpu.VMEM)
    return pl.pallas_call(
        norm_kernel,
        in_specs=[whole] * 2,
        out_specs=whole,
        out_shape=jax.ShapeDtypeStruct((CROWS, 2 * HALF), jnp.bfloat16),
        compiler_params=limit(4),
        cost_estimate=SMALL,
        name="normalise",
    )(own, other)


def project_kernel(info, *refs):
    row_refs, own_ref, far_refs, (kv_ref, key_ref, rows_ref, w_ref) = (
        refs[0:4], refs[4], refs[5:13], refs[13:],
    )
    c, x, y = info[1], info[2], info[3]
    for k in range(4):
        begin = pl.multiple_of((y - k + 4) % 4 * CROWS, CROWS)
        rows_ref[pl.ds(begin, CROWS), :] = row_refs[k][...]
    size = HALF // 8
    for piece in range(8):
        from_x = (x - piece // 2 + 4) % 4
        from_c = c if piece % 2 == 0 else 1 - c
        begin = pl.multiple_of((from_x * 2 + from_c) * size, size)
        w_ref[pl.ds(begin, size), :] = far_refs[piece][...]
    kv = jnp.dot(rows_ref[:, 0:HALF], own_ref[...], preferred_element_type=jnp.float32)
    kv = kv + jnp.dot(
        rows_ref[:, HALF : 2 * HALF], w_ref[...], preferred_element_type=jnp.float32
    )
    kv = kv.astype(jnp.bfloat16)
    kv_ref[...] = kv
    key_ref[...] = kv[:, 0:C_HEAD]


def project(info, rows, own, far):
    whole = pl.BlockSpec(memory_space=pltpu.VMEM)
    return pl.pallas_call(
        project_kernel,
        in_specs=[pl.BlockSpec(memory_space=pltpu.SMEM)] + [whole] * 13,
        out_specs=[whole, whole],
        out_shape=[
            jax.ShapeDtypeStruct((GROUP, 2 * C_HEAD), jnp.bfloat16),
            jax.ShapeDtypeStruct((GROUP, C_HEAD), jnp.bfloat16),
        ],
        scratch_shapes=[
            pltpu.VMEM((GROUP, 2 * HALF), jnp.bfloat16),
            pltpu.VMEM((HALF, 2 * C_HEAD), jnp.bfloat16),
        ],
        compiler_params=limit(20),
        cost_estimate=SMALL,
        name="project",
    )(info, *rows, own, *far)


def split3(value):
    first = value.astype(jnp.bfloat16).astype(jnp.float32)
    rest = value - first
    second = rest.astype(jnp.bfloat16).astype(jnp.float32)
    return first, second, rest - second


def coarse_kernel(info, *refs):
    q_refs, kv_refs, (out_ref, kv_all, q_all) = refs[0:4], refs[4:12], refs[12:]
    x, z, c = info[2], info[4], info[1]
    scale = 1.0 / math.sqrt(C_HEAD)
    keys = 8 * GROUP
    for piece in range(8):
        kv_all[piece * GROUP : (piece + 1) * GROUP, :] = kv_refs[piece][...]
    for k in range(4):
        begin = pl.multiple_of(jnp.bitwise_xor(z, k) * GROUP, GROUP)
        q_all[pl.ds(begin, GROUP), :] = q_refs[k][...]
    slot = lax.broadcasted_iota(jnp.int32, (1, keys), 1)
    piece = slot // GROUP
    inside = slot % GROUP
    from_x = (x - piece // 2 + 4) % 4
    from_c = jnp.where(piece % 2 == 0, c, 1 - c)
    key_pos = (
        from_x * 1024 + (inside // CROWS) * 256 + z * 64 + from_c * 32 + inside % CROWS
    )
    place = lax.broadcasted_iota(jnp.int32, (4 * GROUP, 1), 0)
    inner = place % GROUP
    pos = x * 1024 + (inner // CROWS) * 256 + (place // GROUP) * 64 + c * 32 + inner % CROWS
    lane = lax.broadcasted_iota(jnp.int32, (4 * GROUP, 128), 1)
    allowed = key_pos < jnp.maximum(pos, 1)
    s = lax.dot_general(
        q_all[...], kv_all[:, 0:C_HEAD], (((1,), (1,)), ((), ())),
        preferred_element_type=jnp.float32,
    ) * scale
    s = jnp.where(allowed, s, NEG)
    top = jnp.max(s, -1, keepdims=True)
    p = jnp.where(allowed, jnp.exp(s - top), 0.0)
    total = jnp.sum(p, -1, keepdims=True)
    mixed = jnp.dot(
        p.astype(jnp.bfloat16), kv_all[:, C_HEAD : 2 * C_HEAD],
        preferred_element_type=jnp.float32,
    )
    some = total > 0.0
    safe = jnp.where(some, total, 1.0)
    mixed = jnp.where(some, mixed / safe, 0.0).astype(jnp.bfloat16)
    level = jnp.where(some, top + jnp.log(safe), NEG)
    a, b, d = split3(level)
    extra = jnp.where(lane == 0, a, jnp.where(lane == 1, b, jnp.where(lane == 2, d, 0.0)))
    extra = extra.astype(jnp.bfloat16)
    for from_z in range(4):
        for y in range(4):
            rows = slice(from_z * GROUP + y * CROWS, from_z * GROUP + (y + 1) * CROWS)
            out_ref[y * 4 + from_z, :, 0:C_HEAD] = mixed[rows, :]
            out_ref[y * 4 + from_z, :, C_HEAD : C_HEAD + 128] = extra[rows, :]


def coarse_attend(info, queries, pairs):
    whole = pl.BlockSpec(memory_space=pltpu.VMEM)
    return pl.pallas_call(
        coarse_kernel,
        grid=(1,),
        in_specs=[pl.BlockSpec(memory_space=pltpu.SMEM)]
        + [pl.BlockSpec((GROUP, C_HEAD), lambda i: (0, 0))]
        + [whole] * 3
        + [pl.BlockSpec((GROUP, 2 * C_HEAD), lambda i: (0, 0))]
        + [whole] * 7,
        out_specs=whole,
        out_shape=jax.ShapeDtypeStruct((16, CROWS, C_HEAD + 128), jnp.bfloat16),
        scratch_shapes=[
            pltpu.VMEM((8 * GROUP, 2 * C_HEAD), jnp.bfloat16),
            pltpu.VMEM((4 * GROUP, C_HEAD), jnp.bfloat16),
        ],
        compiler_params=limit(16),
        cost_estimate=pl.CostEstimate(
            flops=4 * 4 * GROUP * 8 * GROUP * C_HEAD,
            bytes_accessed=2 * MIB,
            transcendentals=4 * GROUP * 8 * GROUP,
        ),
        name="coarse_attend",
    )(info, *queries, *pairs)


def final_kernel(part_ref, fine_ref, out_ref, done_ref, sems):
    r = lax.broadcasted_iota(jnp.int32, (ROWS, CROWS), 0)
    j = lax.broadcasted_iota(jnp.int32, (ROWS, CROWS), 1)
    spread = jnp.where(r // SHORT == j, 1.0, 0.0).astype(jnp.bfloat16)
    coarse = []
    for head in range(4):
        parts = part_ref[4 * head : 4 * head + 4].astype(jnp.float32)
        levels = jnp.sum(parts[:, :, C_HEAD : C_HEAD + 128], -1, keepdims=True)
        top = jnp.max(levels, 0, keepdims=True)
        weights = jnp.exp(levels - top)
        total = jnp.sum(weights, 0)
        mixed = jnp.sum(parts[:, :, 0:C_HEAD] * weights, 0) / total
        coarse.append(mixed.astype(jnp.bfloat16))
    coarse = jnp.concatenate(coarse, 1)
    stores = []
    for block in range(4):
        rows = slice(block * 128, (block + 1) * 128)
        up = jnp.dot(spread[rows, :], coarse, preferred_element_type=jnp.float32)
        done_ref[rows, :] = (fine_ref[rows, :].astype(jnp.float32) + up).astype(jnp.bfloat16)
        store = pltpu.make_async_copy(
            done_ref.at[pl.ds(block * 128, 128), :],
            out_ref.at[pl.ds(block * 128, 128), :],
            sems.at[block],
        )
        store.start()
        stores.append(store)
    for store in stores:
        store.wait()


def finish(parts, fine):
    whole = pl.BlockSpec(memory_space=pltpu.VMEM)
    return pl.pallas_call(
        final_kernel,
        in_specs=[whole] * 2,
        out_specs=pl.BlockSpec(memory_space=pl.ANY),
        out_shape=jax.ShapeDtypeStruct((ROWS, HALF), jnp.bfloat16),
        scratch_shapes=[
            pltpu.VMEM((ROWS, HALF), jnp.bfloat16),
            pltpu.SemaphoreType.DMA((4,)),
        ],
        compiler_params=limit(16),
        name="finish",
    )(parts, fine)


def per_device(fine_q, fine_k, fine_v, norm_gain, short_weight):
    x, y, z, c, m = (lax.axis_index(a) for a in CTX + ("m",))
    index = ((x * 4 + y) * 4 + z) * 2 + c
    info = jnp.stack([index, c, x, y, z, m]).astype(jnp.int32)

    k2 = shifted(fine_k, 2)
    v2 = shifted(fine_v, 2)
    ko = rolled(fine_k, "c", 1)
    vo = rolled(fine_v, "c", 1)
    part, own_columns = pick_columns(info, short_weight)
    k2, part = lax.optimization_barrier((k2, part))
    ks = [rolled(piece, "c", 1) for piece in halves(k2)]
    far, mid, near, l, acc = fine_probs(info, fine_q, k2, ks, ko, fine_k, vo, fine_v)
    v2, l = lax.optimization_barrier((v2, l))
    vs = rolled(v2, "c", 1)
    acc = far_mix(far, mid, acc, v2)
    tail = shifted(last_rows(info, near, l, acc, vs), 1)
    fine_out, pooled = fine_mix(info, near, l, acc, vs)

    part = rolled(part, "m", 1)
    pooled = add_tail(pooled, tail, norm_gain[None])
    part, pooled = lax.optimization_barrier((part, pooled))
    eighths = [part] + [rolled(part, "x", k) for k in (1, 2, 3)]

    other = rolled(pooled, "m", 1)
    normed = normalise(pooled, other)
    normed, *eighths = lax.optimization_barrier((normed, *eighths))
    columns = []
    for piece in eighths:
        columns += [piece, rolled(piece, "c", 1)]
    rows = [normed] + [rolled(normed, "y", k) for k in (1, 2, 3)]
    kv, own_keys = project(info, rows, own_columns, columns)

    queries = [own_keys] + [paired(own_keys, "z", k) for k in (1, 2, 3)]
    pieces = [kv] + [rolled(kv, "x", k) for k in (1, 2, 3)]
    held = lax.optimization_barrier((*queries, *pieces))
    queries, pieces = held[:4], held[4:]
    pairs = []
    for piece in pieces:
        pairs += [piece, rolled(piece, "c", 1)]
    parts = coarse_attend(info, queries, pairs)
    parts = lax.all_to_all(parts, ("y", "z"), split_axis=0, concat_axis=0, tiled=True)
    return finish(parts, fine_out)


def solution(mesh):
    grid = Mesh(mesh.devices.reshape(4, 4, 4, 2, 2), ("x", "y", "z", "c", "m"))
    rows = P(CTX, "m")
    return jax.shard_map(
        per_device,
        mesh=grid,
        in_specs=(rows, rows, rows, P("m"), P("m", None)),
        out_specs=rows,
        check_vma=False,
    )
```

```python
import functools
import math

import jax
import jax.numpy as jnp
from jax import lax
from jax.experimental import pallas as pl
from jax.experimental.pallas import tpu as pltpu
from jax.sharding import Mesh
from jax.sharding import PartitionSpec as P

D_FINE = 2048
HEADS = 16
HEAD = 128
C_HEADS = 8
C_HEAD = 256
WINDOW = 1024
SHORT = 16
EPS = 1e-05
NEG = -1e30
LOG2E = 1.4426950408889634

ROWS = 512
HALF = 1024
LOCAL_HEADS = HALF // HEAD
TILE = 256
CROWS = ROWS // SHORT
GROUP = 4 * CROWS
SMALL = pl.CostEstimate(flops=1, bytes_accessed=1, transcendentals=0)
CTX = ("x", "y", "z", "c")
MIB = 1 << 20


def shifted(value, steps):
    count = 128
    return lax.ppermute(
        value, CTX, [(s, s + steps) for s in range(max(0, -steps), min(count, count - steps))]
    )


def rolled(value, axis, steps):
    count = lax.axis_size(axis)
    return lax.ppermute(value, axis, [(s, (s + steps) % count) for s in range(count)])


def paired(value, axis, distance):
    count = lax.axis_size(axis)
    return lax.ppermute(value, axis, [(s, s ^ distance) for s in range(count)])


def limit(mib):
    return pltpu.CompilerParams(vmem_limit_bytes=mib * MIB)


def halves_kernel(in_ref, low_ref, high_ref):
    low_ref[...] = in_ref[0:TILE, :]
    high_ref[...] = in_ref[TILE : 2 * TILE, :]


def halves(value):
    half = pl.BlockSpec((TILE, 512), lambda i: (0, i))
    return pl.pallas_call(
        halves_kernel,
        grid=(2,),
        in_specs=[pl.BlockSpec((ROWS, 512), lambda i: (0, i))],
        out_specs=[half] * 2,
        out_shape=[jax.ShapeDtypeStruct((TILE, HALF), jnp.bfloat16)] * 2,
        compiler_params=limit(8),
        cost_estimate=SMALL,
        name="halves",
    )(value)


def pick_kernel(info, part_ref, own_ref, part_out, own_out):
    part_out[...] = part_ref[...]
    own_out[...] = own_ref[...]


def pick_columns(info, weight):
    wide = 2 * C_HEAD
    size = HALF // 8
    part = pl.BlockSpec(
        (size, wide), lambda i, info: (info[2] * 2 + info[1], (1 - info[5]) * 4 + info[3])
    )
    own = pl.BlockSpec((HALF // 4, wide), lambda i, info: (i, info[5] * 4 + info[3]))
    return pl.pallas_call(
        pick_kernel,
        grid_spec=pltpu.PrefetchScalarGridSpec(
            num_scalar_prefetch=1,
            grid=(4,),
            in_specs=[part, own],
            out_specs=[
                pl.BlockSpec((size, wide), lambda i, info: (0, 0)),
                pl.BlockSpec((HALF // 4, wide), lambda i, info: (i, 0)),
            ],
        ),
        out_shape=[
            jax.ShapeDtypeStruct((size, wide), jnp.bfloat16),
            jax.ShapeDtypeStruct((HALF, wide), jnp.bfloat16),
        ],
        compiler_params=limit(8),
        cost_estimate=pl.CostEstimate(flops=1 << 30, bytes_accessed=2 * MIB, transcendentals=0),
        name="pick_columns",
    )(info, weight, weight)


def start_kernel(pool_ref, tail_ref, gain_ref, out_ref):
    row = lax.broadcasted_iota(jnp.int32, (CROWS, 1), 0)
    pooled = pool_ref[...] + jnp.where(row == 0, tail_ref[0:1, :], 0.0)
    out_ref[:, 0:HALF] = pooled * gain_ref[...]
    out_ref[:, HALF : HALF + 128] = jnp.broadcast_to(
        jnp.sum(pooled * pooled, -1, keepdims=True), (CROWS, 128)
    )


def add_tail(pooled, tail, gain):
    whole = pl.BlockSpec(memory_space=pltpu.VMEM)
    return pl.pallas_call(
        start_kernel,
        in_specs=[whole] * 3,
        out_specs=whole,
        out_shape=jax.ShapeDtypeStruct((CROWS, HALF + 128), jnp.float32),
        compiler_params=limit(4),
        cost_estimate=SMALL,
        name="add_tail",
    )(pooled, tail, gain)


def attend(q, pieces, store):
    scale = LOG2E / math.sqrt(HEAD)
    scores = []
    top = None
    for keys, okay, mask in pieces:
        s = lax.dot_general(
            q, keys, (((1,), (1,)), ((), ())), preferred_element_type=jnp.float32
        )
        if mask is not None:
            s = jnp.where(mask, s, NEG)
        scores.append(s)
        high = jnp.max(s, -1, keepdims=True)
        if okay is not None:
            high = jnp.where(okay, high, NEG)
        top = high if top is None else jnp.maximum(top, high)
    total = jnp.zeros((q.shape[0], 1), jnp.float32)
    for step, (keys, okay, mask) in enumerate(pieces):
        base = top if okay is None else jnp.where(okay, top, -NEG)
        p = jnp.exp2((scores[step] - base) * scale)
        total = total + jnp.sum(p, -1, keepdims=True)
        store(step, p.astype(jnp.bfloat16))
    return total


def probs_kernel(
    pieces, info, q_ref, ka_ref, ko_ref, kc_ref, vo_ref, vc_ref, *refs
):
    ks_refs, (far_ref, mid_ref, near_ref, l_ref, acc_ref) = refs[:pieces], refs[pieces:]
    head = pl.program_id(0)
    index = info[0]
    core = info[1]
    kb = jnp.where(core == 0, jnp.concatenate([r[...] for r in ks_refs], 0), ko_ref[...])
    chunks = [
        ka_ref[0:TILE, :],
        ka_ref[TILE : 2 * TILE, :],
        kb[0:TILE, :],
        kb[TILE : 2 * TILE, :],
        kc_ref[0:TILE, :],
        kc_ref[TILE : 2 * TILE, :],
    ]
    valid = [index >= 2, index >= 2, index >= 1, index >= 1, None, None]
    row = lax.broadcasted_iota(jnp.int32, (TILE, TILE), 0)
    col = lax.broadcasted_iota(jnp.int32, (TILE, TILE), 1)
    lane = lax.broadcasted_iota(jnp.int32, (TILE, 128), 1)
    for tile in range(ROWS // TILE):
        masks = [col > row, None, None, None, col <= row]
        keys = [(chunks[tile + j], valid[tile + j], masks[j]) for j in range(5)]
        rows = slice(tile * TILE, (tile + 1) * TILE)

        def store(step, p, tile=tile, rows=rows):
            chunk = tile + step
            if chunk == 0:
                far_ref[0] = p
            elif chunk == 1:
                mid_ref[0, rows, :] = p
            elif chunk < 4:
                near_ref[0, rows, (chunk - 2) * TILE : (chunk - 1) * TILE] = p
            else:
                values = vc_ref[(chunk - 4) * TILE : (chunk - 3) * TILE, :]
                part = jnp.dot(p, values, preferred_element_type=jnp.float32)
                if chunk == 5:
                    part = part + acc_ref[rows, :]
                acc_ref[rows, :] = part

        total = attend(q_ref[rows, :], keys, store)
        before = jnp.where(head == 0, 1.0, l_ref[rows, :])
        l_ref[rows, :] = jnp.where(lane == head, total, before)

    @pl.when(core == 1)
    def _():
        acc_ref[...] = acc_ref[...] + jnp.dot(
            near_ref[0], vo_ref[...], preferred_element_type=jnp.float32
        )


def fine_probs(info, q, ka, ks, ko, kc, vo, vc):
    column = pl.BlockSpec((ROWS, HEAD), lambda h, info: (0, h))
    piece = pl.BlockSpec((ROWS // len(ks), HEAD), lambda h, info: (0, h))
    return pl.pallas_call(
        functools.partial(probs_kernel, len(ks)),
        grid_spec=pltpu.PrefetchScalarGridSpec(
            num_scalar_prefetch=1,
            grid=(LOCAL_HEADS,),
            in_specs=[column] * 6 + [piece] * len(ks),
            out_specs=[
                pl.BlockSpec((1, TILE, TILE), lambda h, info: (h, 0, 0)),
                pl.BlockSpec((1, ROWS, TILE), lambda h, info: (h, 0, 0)),
                pl.BlockSpec((1, ROWS, ROWS), lambda h, info: (h, 0, 0)),
                pl.BlockSpec((ROWS, 128), lambda h, info: (0, 0)),
                column,
            ],
        ),
        out_shape=[
            jax.ShapeDtypeStruct((LOCAL_HEADS, TILE, TILE), jnp.bfloat16),
            jax.ShapeDtypeStruct((LOCAL_HEADS, ROWS, TILE), jnp.bfloat16),
            jax.ShapeDtypeStruct((LOCAL_HEADS, ROWS, ROWS), jnp.bfloat16),
            jax.ShapeDtypeStruct((ROWS, 128), jnp.float32),
            jax.ShapeDtypeStruct((ROWS, HALF), jnp.float32),
        ],
        compiler_params=limit(20),
        cost_estimate=SMALL,
        name="fine_probs",
    )(info, q, ka, ko, kc, vo, vc, *ks)


def far_kernel(far_ref, mid_ref, acc_ref, va_ref, out_ref):
    for head in range(LOCAL_HEADS):
        columns = slice(head * HEAD, (head + 1) * HEAD)
        mixed = acc_ref[:, columns] + jnp.dot(
            mid_ref[head], va_ref[TILE : 2 * TILE, columns], preferred_element_type=jnp.float32
        )
        out_ref[0:TILE, columns] = mixed[0:TILE, :] + jnp.dot(
            far_ref[head], va_ref[0:TILE, columns], preferred_element_type=jnp.float32
        )
        out_ref[TILE : 2 * TILE, columns] = mixed[TILE : 2 * TILE, :]


def far_mix(far, mid, acc, va):
    whole = pl.BlockSpec(memory_space=pltpu.VMEM)
    return pl.pallas_call(
        far_kernel,
        in_specs=[whole] * 4,
        out_specs=whole,
        out_shape=jax.ShapeDtypeStruct((ROWS, HALF), jnp.float32),
        compiler_params=limit(16),
        cost_estimate=pl.CostEstimate(flops=1 << 30, bytes_accessed=8 * MIB, transcendentals=0),
        name="far_mix",
    )(far, mid, acc, va)


def last_kernel(info, near_ref, l_ref, acc_ref, vs_ref, tail_ref):
    core = info[1]
    rows = slice(ROWS - SHORT, ROWS)

    def mix(with_near):
        j = lax.broadcasted_iota(jnp.int32, (8, SHORT), 0)
        r = lax.broadcasted_iota(jnp.int32, (8, SHORT), 1)
        pick = jnp.where((j == 0) & (r > 0), 1.0, 0.0).astype(jnp.bfloat16)
        share = 1.0 / l_ref[rows, :]
        for head in range(LOCAL_HEADS):
            columns = slice(head * HEAD, (head + 1) * HEAD)
            mixed = acc_ref[rows, columns]
            if with_near:
                mixed = mixed + jnp.dot(
                    near_ref[head, rows, :], vs_ref[:, columns],
                    preferred_element_type=jnp.float32,
                )
            out = (mixed * share[:, head : head + 1]).astype(jnp.bfloat16)
            sums = jnp.dot(pick, out, preferred_element_type=jnp.float32)
            tail_ref[:, columns] = sums * (1.0 / SHORT)

    @pl.when(core == 0)
    def _():
        mix(True)

    @pl.when(core == 1)
    def _():
        mix(False)


def last_rows(info, near, l, acc, vs):
    whole = pl.BlockSpec(memory_space=pltpu.VMEM)
    return pl.pallas_call(
        last_kernel,
        in_specs=[pl.BlockSpec(memory_space=pltpu.SMEM)] + [whole] * 4,
        out_specs=whole,
        out_shape=jax.ShapeDtypeStruct((8, HALF), jnp.float32),
        compiler_params=limit(16),
        cost_estimate=SMALL,
        name="last_rows",
    )(info, near, l, acc, vs)


def mix_kernel(info, near_ref, l_ref, acc_ref, vs_ref, out_ref, pool_ref):
    core = info[1]

    def mix(with_near):
        j = lax.broadcasted_iota(jnp.int32, (CROWS, ROWS), 0)
        r = lax.broadcasted_iota(jnp.int32, (CROWS, ROWS), 1)
        pick = jnp.where((r > SHORT * j - SHORT) & (r <= SHORT * j), 1.0, 0.0)
        pick = pick.astype(jnp.bfloat16)
        share = 1.0 / l_ref[...]
        for head in range(LOCAL_HEADS):
            columns = slice(head * HEAD, (head + 1) * HEAD)
            mixed = acc_ref[:, columns]
            if with_near:
                mixed = mixed + jnp.dot(
                    near_ref[head], vs_ref[:, columns], preferred_element_type=jnp.float32
                )
            out = (mixed * share[:, head : head + 1]).astype(jnp.bfloat16)
            out_ref[:, columns] = out
            sums = jnp.dot(pick, out, preferred_element_type=jnp.float32)
            pool_ref[:, columns] = sums * (1.0 / SHORT)

    @pl.when(core == 0)
    def _():
        mix(True)

    @pl.when(core == 1)
    def _():
        mix(False)


def fine_mix(info, near, l, acc, vs):
    whole = pl.BlockSpec(memory_space=pltpu.VMEM)
    return pl.pallas_call(
        mix_kernel,
        in_specs=[pl.BlockSpec(memory_space=pltpu.SMEM)] + [whole] * 4,
        out_specs=[whole] * 2,
        out_shape=[
            jax.ShapeDtypeStruct((ROWS, HALF), jnp.bfloat16),
            jax.ShapeDtypeStruct((CROWS, HALF), jnp.float32),
        ],
        compiler_params=limit(20),
        cost_estimate=pl.CostEstimate(flops=1 << 30, bytes_accessed=8 * MIB, transcendentals=0),
        name="fine_mix",
    )(info, near, l, acc, vs)


def norm_kernel(own_ref, other_ref, out_ref):
    squares = own_ref[:, HALF : HALF + 1] + other_ref[:, HALF : HALF + 1]
    factor = lax.rsqrt(squares / D_FINE + EPS)
    out_ref[:, 0:HALF] = (own_ref[:, 0:HALF] * factor).astype(jnp.bfloat16)
    out_ref[:, HALF : 2 * HALF] = (other_ref[:, 0:HALF] * factor).astype(jnp.bfloat16)


def normalise(own, other):
    whole = pl.BlockSpec(memory_space=pltpu.VMEM)
    return pl.pallas_call(
        norm_kernel,
        in_specs=[whole] * 2,
        out_specs=whole,
        out_shape=jax.ShapeDtypeStruct((CROWS, 2 * HALF), jnp.bfloat16),
        compiler_params=limit(4),
        cost_estimate=SMALL,
        name="normalise",
    )(own, other)


def project_kernel(info, *refs):
    row_refs, own_ref, far_refs, (kv_ref, key_ref, rows_ref, w_ref) = (
        refs[0:4], refs[4], refs[5:13], refs[13:],
    )
    c, x, y = info[1], info[2], info[3]
    for k in range(4):
        begin = pl.multiple_of((y - k + 4) % 4 * CROWS, CROWS)
        rows_ref[pl.ds(begin, CROWS), :] = row_refs[k][...]
    size = HALF // 8
    for piece in range(8):
        from_x = (x - piece // 2 + 4) % 4
        from_c = c if piece % 2 == 0 else 1 - c
        begin = pl.multiple_of((from_x * 2 + from_c) * size, size)
        w_ref[pl.ds(begin, size), :] = far_refs[piece][...]
    kv = jnp.dot(rows_ref[:, 0:HALF], own_ref[...], preferred_element_type=jnp.float32)
    kv = kv + jnp.dot(
        rows_ref[:, HALF : 2 * HALF], w_ref[...], preferred_element_type=jnp.float32
    )
    kv = kv.astype(jnp.bfloat16)
    kv_ref[...] = kv
    key_ref[...] = kv[:, 0:C_HEAD]


def project(info, rows, own, far):
    whole = pl.BlockSpec(memory_space=pltpu.VMEM)
    return pl.pallas_call(
        project_kernel,
        in_specs=[pl.BlockSpec(memory_space=pltpu.SMEM)] + [whole] * 13,
        out_specs=[whole, whole],
        out_shape=[
            jax.ShapeDtypeStruct((GROUP, 2 * C_HEAD), jnp.bfloat16),
            jax.ShapeDtypeStruct((GROUP, C_HEAD), jnp.bfloat16),
        ],
        scratch_shapes=[
            pltpu.VMEM((GROUP, 2 * HALF), jnp.bfloat16),
            pltpu.VMEM((HALF, 2 * C_HEAD), jnp.bfloat16),
        ],
        compiler_params=limit(20),
        cost_estimate=SMALL,
        name="project",
    )(info, *rows, own, *far)


def split3(value):
    first = value.astype(jnp.bfloat16).astype(jnp.float32)
    rest = value - first
    second = rest.astype(jnp.bfloat16).astype(jnp.float32)
    return first, second, rest - second


def coarse_kernel(info, *refs):
    q_refs, kv_refs, (out_ref, kv_all, q_all) = refs[0:4], refs[4:12], refs[12:]
    x, z, c = info[2], info[4], info[1]
    scale = 1.0 / math.sqrt(C_HEAD)
    keys = 8 * GROUP
    for piece in range(8):
        kv_all[piece * GROUP : (piece + 1) * GROUP, :] = kv_refs[piece][...]
    for k in range(4):
        begin = pl.multiple_of((x - k + 4) % 4 * GROUP, GROUP)
        q_all[pl.ds(begin, GROUP), :] = q_refs[k][...]
    slot = lax.broadcasted_iota(jnp.int32, (1, keys), 1)
    piece = slot // GROUP
    inside = slot % GROUP
    from_z = jnp.bitwise_xor(z, piece // 2)
    from_c = jnp.where(piece % 2 == 0, c, 1 - c)
    key_pos = (
        x * 1024 + (inside // CROWS) * 256 + from_z * 64 + from_c * 32 + inside % CROWS
    )
    place = lax.broadcasted_iota(jnp.int32, (4 * GROUP, 1), 0)
    inner = place % GROUP
    pos = (place // GROUP) * 1024 + (inner // CROWS) * 256 + z * 64 + c * 32 + inner % CROWS
    lane = lax.broadcasted_iota(jnp.int32, (4 * GROUP, 128), 1)
    allowed = key_pos < jnp.maximum(pos, 1)
    s = lax.dot_general(
        q_all[...], kv_all[:, 0:C_HEAD], (((1,), (1,)), ((), ())),
        preferred_element_type=jnp.float32,
    ) * scale
    s = jnp.where(allowed, s, NEG)
    top = jnp.max(s, -1, keepdims=True)
    p = jnp.where(allowed, jnp.exp(s - top), 0.0)
    total = jnp.sum(p, -1, keepdims=True)
    mixed = jnp.dot(
        p.astype(jnp.bfloat16), kv_all[:, C_HEAD : 2 * C_HEAD],
        preferred_element_type=jnp.float32,
    )
    some = total > 0.0
    safe = jnp.where(some, total, 1.0)
    mixed = jnp.where(some, mixed / safe, 0.0).astype(jnp.bfloat16)
    level = jnp.where(some, top + jnp.log(safe), NEG)
    a, b, d = split3(level)
    extra = jnp.where(lane == 0, a, jnp.where(lane == 1, b, jnp.where(lane == 2, d, 0.0)))
    extra = extra.astype(jnp.bfloat16)
    for piece in range(16):
        rows = slice(piece * CROWS, (piece + 1) * CROWS)
        out_ref[piece, :, 0:C_HEAD] = mixed[rows, :]
        out_ref[piece, :, C_HEAD : C_HEAD + 128] = extra[rows, :]


def coarse_attend(info, queries, pairs):
    whole = pl.BlockSpec(memory_space=pltpu.VMEM)
    return pl.pallas_call(
        coarse_kernel,
        grid=(1,),
        in_specs=[pl.BlockSpec(memory_space=pltpu.SMEM)]
        + [pl.BlockSpec((GROUP, C_HEAD), lambda i: (0, 0))]
        + [whole] * 3
        + [pl.BlockSpec((GROUP, 2 * C_HEAD), lambda i: (0, 0))]
        + [whole] * 7,
        out_specs=whole,
        out_shape=jax.ShapeDtypeStruct((16, CROWS, C_HEAD + 128), jnp.bfloat16),
        scratch_shapes=[
            pltpu.VMEM((8 * GROUP, 2 * C_HEAD), jnp.bfloat16),
            pltpu.VMEM((4 * GROUP, C_HEAD), jnp.bfloat16),
        ],
        compiler_params=limit(16),
        cost_estimate=pl.CostEstimate(
            flops=4 * 4 * GROUP * 8 * GROUP * C_HEAD,
            bytes_accessed=2 * MIB,
            transcendentals=4 * GROUP * 8 * GROUP,
        ),
        name="coarse_attend",
    )(info, *queries, *pairs)


def final_kernel(part_ref, fine_ref, out_ref, done_ref, sems):
    r = lax.broadcasted_iota(jnp.int32, (ROWS, CROWS), 0)
    j = lax.broadcasted_iota(jnp.int32, (ROWS, CROWS), 1)
    spread = jnp.where(r // SHORT == j, 1.0, 0.0).astype(jnp.bfloat16)
    coarse = []
    for head in range(4):
        parts = jnp.stack([part_ref[4 * i + head] for i in range(4)]).astype(jnp.float32)
        levels = jnp.sum(parts[:, :, C_HEAD : C_HEAD + 128], -1, keepdims=True)
        top = jnp.max(levels, 0, keepdims=True)
        weights = jnp.exp(levels - top)
        total = jnp.sum(weights, 0)
        mixed = jnp.sum(parts[:, :, 0:C_HEAD] * weights, 0) / total
        coarse.append(mixed.astype(jnp.bfloat16))
    coarse = jnp.concatenate(coarse, 1)
    stores = []
    for block in range(4):
        rows = slice(block * 128, (block + 1) * 128)
        up = jnp.dot(spread[rows, :], coarse, preferred_element_type=jnp.float32)
        done_ref[rows, :] = (fine_ref[rows, :].astype(jnp.float32) + up).astype(jnp.bfloat16)
        store = pltpu.make_async_copy(
            done_ref.at[pl.ds(block * 128, 128), :],
            out_ref.at[pl.ds(block * 128, 128), :],
            sems.at[block],
        )
        store.start()
        stores.append(store)
    for store in stores:
        store.wait()


def finish(parts, fine):
    whole = pl.BlockSpec(memory_space=pltpu.VMEM)
    return pl.pallas_call(
        final_kernel,
        in_specs=[whole] * 2,
        out_specs=pl.BlockSpec(memory_space=pl.ANY),
        out_shape=jax.ShapeDtypeStruct((ROWS, HALF), jnp.bfloat16),
        scratch_shapes=[
            pltpu.VMEM((ROWS, HALF), jnp.bfloat16),
            pltpu.SemaphoreType.DMA((4,)),
        ],
        compiler_params=limit(16),
        name="finish",
    )(parts, fine)


def per_device(fine_q, fine_k, fine_v, norm_gain, short_weight):
    x, y, z, c, m = (lax.axis_index(a) for a in CTX + ("m",))
    index = ((x * 4 + y) * 4 + z) * 2 + c
    info = jnp.stack([index, c, x, y, z, m]).astype(jnp.int32)

    k2 = shifted(fine_k, 2)
    v2 = shifted(fine_v, 2)
    ko = rolled(fine_k, "c", 1)
    vo = rolled(fine_v, "c", 1)
    part, own_columns = pick_columns(info, short_weight)
    k2, part = lax.optimization_barrier((k2, part))
    ks = [rolled(piece, "c", 1) for piece in halves(k2)]
    far, mid, near, l, acc = fine_probs(info, fine_q, k2, ks, ko, fine_k, vo, fine_v)
    v2, l = lax.optimization_barrier((v2, l))
    vs = rolled(v2, "c", 1)
    acc = far_mix(far, mid, acc, v2)
    tail = last_rows(info, near, l, acc, vs)
    tail, part = lax.optimization_barrier((tail, part))
    tail = shifted(tail, 1)
    fine_out, pooled = fine_mix(info, near, l, acc, vs)

    part = rolled(part, "m", 1)
    pooled = add_tail(pooled, tail, norm_gain[None])
    part, pooled = lax.optimization_barrier((part, pooled))
    eighths = [part] + [rolled(part, "x", k) for k in (1, 2, 3)]

    other = rolled(pooled, "m", 1)
    normed = normalise(pooled, other)
    normed, *eighths = lax.optimization_barrier((normed, *eighths))
    columns = []
    for piece in eighths:
        columns += [piece, rolled(piece, "c", 1)]
    rows = [normed] + [rolled(normed, "y", k) for k in (1, 2, 3)]
    kv, own_keys = project(info, rows, own_columns, columns)

    queries = [own_keys] + [rolled(own_keys, "x", k) for k in (1, 2, 3)]
    far = [paired(kv, "z", k) for k in (2, 3)]
    pieces = [kv, paired(kv, "z", 1)] + far
    held = lax.optimization_barrier((*queries, *pieces))
    queries, pieces = held[:4], held[4:]
    pairs = []
    for piece in pieces:
        pairs += [piece, rolled(piece, "c", 1)]
    parts = coarse_attend(info, queries, pairs)
    parts = lax.all_to_all(parts, ("x", "y"), split_axis=0, concat_axis=0, tiled=True)
    return finish(parts, fine_out)


def solution(mesh):
    grid = Mesh(mesh.devices.reshape(4, 4, 4, 2, 2), ("x", "y", "z", "c", "m"))
    rows = P(CTX, "m")
    return jax.shard_map(
        per_device,
        mesh=grid,
        in_specs=(rows, rows, rows, P("m"), P("m", None)),
        out_specs=rows,
        check_vma=False,
    )
```

```python
import functools
import math

import jax
import jax.numpy as jnp
from jax import lax
from jax.experimental import pallas as pl
from jax.experimental.pallas import tpu as pltpu
from jax.sharding import Mesh
from jax.sharding import PartitionSpec as P

D_FINE = 2048
HEADS = 16
HEAD = 128
C_HEADS = 8
C_HEAD = 256
WINDOW = 1024
SHORT = 16
EPS = 1e-05
NEG = -1e30
LOG2E = 1.4426950408889634

ROWS = 512
HALF = 1024
LOCAL_HEADS = HALF // HEAD
TILE = 256
CROWS = ROWS // SHORT
TAIL = 128 + 2 * ROWS
GROUP = 4 * CROWS
SMALL = pl.CostEstimate(flops=1, bytes_accessed=1, transcendentals=0)
CTX = ("x", "y", "z", "c")
MIB = 1 << 20


def shifted(value, steps):
    count = 128
    return lax.ppermute(
        value, CTX, [(s, s + steps) for s in range(max(0, -steps), min(count, count - steps))]
    )


def rolled(value, axis, steps):
    count = lax.axis_size(axis)
    return lax.ppermute(value, axis, [(s, (s + steps) % count) for s in range(count)])


def paired(value, axis, distance):
    count = lax.axis_size(axis)
    return lax.ppermute(value, axis, [(s, s ^ distance) for s in range(count)])


def limit(mib):
    return pltpu.CompilerParams(vmem_limit_bytes=mib * MIB)


def halves_kernel(in_ref, low_ref, high_ref):
    low_ref[...] = in_ref[0:TILE, :]
    high_ref[...] = in_ref[TILE : 2 * TILE, :]


def halves(value):
    half = pl.BlockSpec((TILE, 512), lambda i: (0, i))
    return pl.pallas_call(
        halves_kernel,
        grid=(2,),
        in_specs=[pl.BlockSpec((ROWS, 512), lambda i: (0, i))],
        out_specs=[half] * 2,
        out_shape=[jax.ShapeDtypeStruct((TILE, HALF), jnp.bfloat16)] * 2,
        compiler_params=limit(8),
        cost_estimate=SMALL,
        name="halves",
    )(value)


def pick_kernel(
    info, part_ref, own_ref, q_ref, k_ref, v_ref, part_out, own_out, q_out, kv_out
):
    part_out[...] = part_ref[...]
    own_out[...] = own_ref[...]
    q_out[...] = q_ref[...]
    kv_out[0:SHORT, :] = k_ref[...]
    kv_out[SHORT : 2 * SHORT, :] = v_ref[...]


def pick_columns(info, weight, q, k, v):
    wide = 2 * C_HEAD
    size = HALF // 8
    part = pl.BlockSpec(
        (size, wide), lambda i, info: (info[2] * 2 + info[1], (1 - info[5]) * 4 + info[3])
    )
    own = pl.BlockSpec((HALF // 4, wide), lambda i, info: (i, info[5] * 4 + info[3]))
    end = pl.BlockSpec((SHORT, HALF), lambda i, info: (ROWS // SHORT - 1, 0))
    first = lambda rows, columns: pl.BlockSpec((rows, columns), lambda i, info: (0, 0))
    return pl.pallas_call(
        pick_kernel,
        grid_spec=pltpu.PrefetchScalarGridSpec(
            num_scalar_prefetch=1,
            grid=(4,),
            in_specs=[part, own, end, end, end],
            out_specs=[
                first(size, wide),
                pl.BlockSpec((HALF // 4, wide), lambda i, info: (i, 0)),
                first(SHORT, HALF),
                first(2 * SHORT, HALF),
            ],
        ),
        out_shape=[
            jax.ShapeDtypeStruct((size, wide), jnp.bfloat16),
            jax.ShapeDtypeStruct((HALF, wide), jnp.bfloat16),
            jax.ShapeDtypeStruct((SHORT, HALF), jnp.bfloat16),
            jax.ShapeDtypeStruct((2 * SHORT, HALF), jnp.bfloat16),
        ],
        compiler_params=limit(8),
        cost_estimate=pl.CostEstimate(flops=1 << 30, bytes_accessed=2 * MIB, transcendentals=0),
        name="pick_columns",
    )(info, weight, weight, q, k, v)


def attend(q, pieces, store):
    scale = LOG2E / math.sqrt(HEAD)
    scores = []
    top = None
    for keys, okay, mask in pieces:
        s = lax.dot_general(
            q, keys, (((1,), (1,)), ((), ())), preferred_element_type=jnp.float32
        )
        if mask is not None:
            s = jnp.where(mask, s, NEG)
        scores.append(s)
        high = jnp.max(s, -1, keepdims=True)
        if okay is not None:
            high = jnp.where(okay, high, NEG)
        top = high if top is None else jnp.maximum(top, high)
    total = jnp.zeros((q.shape[0], 1), jnp.float32)
    for step, (keys, okay, mask) in enumerate(pieces):
        base = top if okay is None else jnp.where(okay, top, -NEG)
        p = jnp.exp2((scores[step] - base) * scale)
        total = total + jnp.sum(p, -1, keepdims=True)
        store(step, p.astype(jnp.bfloat16))
    return total


def probs_kernel(
    pieces, info, q_ref, ka_ref, ko_ref, kc_ref, vo_ref, vc_ref, *refs
):
    ks_refs, (far_ref, mid_ref, near_ref, l_ref, acc_ref) = refs[:pieces], refs[pieces:]
    head = pl.program_id(0)
    index = info[0]
    core = info[1]
    kb = jnp.where(core == 0, jnp.concatenate([r[...] for r in ks_refs], 0), ko_ref[...])
    chunks = [
        ka_ref[0:TILE, :],
        ka_ref[TILE : 2 * TILE, :],
        kb[0:TILE, :],
        kb[TILE : 2 * TILE, :],
        kc_ref[0:TILE, :],
        kc_ref[TILE : 2 * TILE, :],
    ]
    valid = [index >= 2, index >= 2, index >= 1, index >= 1, None, None]
    row = lax.broadcasted_iota(jnp.int32, (TILE, TILE), 0)
    col = lax.broadcasted_iota(jnp.int32, (TILE, TILE), 1)
    lane = lax.broadcasted_iota(jnp.int32, (TILE, 128), 1)
    for tile in range(ROWS // TILE):
        masks = [col > row, None, None, None, col <= row]
        keys = [(chunks[tile + j], valid[tile + j], masks[j]) for j in range(5)]
        rows = slice(tile * TILE, (tile + 1) * TILE)

        def store(step, p, tile=tile, rows=rows):
            chunk = tile + step
            if chunk == 0:
                far_ref[0] = p
            elif chunk == 1:
                mid_ref[0, rows, :] = p
            elif chunk < 4:
                near_ref[0, rows, (chunk - 2) * TILE : (chunk - 1) * TILE] = p
            else:
                values = vc_ref[(chunk - 4) * TILE : (chunk - 3) * TILE, :]
                part = jnp.dot(p, values, preferred_element_type=jnp.float32)
                if chunk == 5:
                    part = part + acc_ref[rows, :]
                acc_ref[rows, :] = part

        total = attend(q_ref[rows, :], keys, store)
        before = jnp.where(head == 0, 1.0, l_ref[rows, :])
        l_ref[rows, :] = jnp.where(lane == head, total, before)

    @pl.when(core == 1)
    def _():
        acc_ref[...] = acc_ref[...] + jnp.dot(
            near_ref[0], vo_ref[...], preferred_element_type=jnp.float32
        )


def fine_probs(info, q, ka, ks, ko, kc, vo, vc):
    column = pl.BlockSpec((ROWS, HEAD), lambda h, info: (0, h))
    piece = pl.BlockSpec((ROWS // len(ks), HEAD), lambda h, info: (0, h))
    return pl.pallas_call(
        functools.partial(probs_kernel, len(ks)),
        grid_spec=pltpu.PrefetchScalarGridSpec(
            num_scalar_prefetch=1,
            grid=(LOCAL_HEADS,),
            in_specs=[column] * 6 + [piece] * len(ks),
            out_specs=[
                pl.BlockSpec((1, TILE, TILE), lambda h, info: (h, 0, 0)),
                pl.BlockSpec((1, ROWS, TILE), lambda h, info: (h, 0, 0)),
                pl.BlockSpec((1, ROWS, ROWS), lambda h, info: (h, 0, 0)),
                pl.BlockSpec((ROWS, 128), lambda h, info: (0, 0)),
                column,
            ],
        ),
        out_shape=[
            jax.ShapeDtypeStruct((LOCAL_HEADS, TILE, TILE), jnp.bfloat16),
            jax.ShapeDtypeStruct((LOCAL_HEADS, ROWS, TILE), jnp.bfloat16),
            jax.ShapeDtypeStruct((LOCAL_HEADS, ROWS, ROWS), jnp.bfloat16),
            jax.ShapeDtypeStruct((ROWS, 128), jnp.float32),
            jax.ShapeDtypeStruct((ROWS, HALF), jnp.float32),
        ],
        compiler_params=limit(20),
        cost_estimate=SMALL,
        name="fine_probs",
    )(info, q, ka, ko, kc, vo, vc, *ks)


def far_kernel(far_ref, mid_ref, acc_ref, va_ref, out_ref):
    for head in range(LOCAL_HEADS):
        columns = slice(head * HEAD, (head + 1) * HEAD)
        mixed = acc_ref[:, columns] + jnp.dot(
            mid_ref[head], va_ref[TILE : 2 * TILE, columns], preferred_element_type=jnp.float32
        )
        out_ref[0:TILE, columns] = mixed[0:TILE, :] + jnp.dot(
            far_ref[head], va_ref[0:TILE, columns], preferred_element_type=jnp.float32
        )
        out_ref[TILE : 2 * TILE, columns] = mixed[TILE : 2 * TILE, :]


def far_mix(far, mid, acc, va):
    whole = pl.BlockSpec(memory_space=pltpu.VMEM)
    return pl.pallas_call(
        far_kernel,
        in_specs=[whole] * 4,
        out_specs=whole,
        out_shape=jax.ShapeDtypeStruct((ROWS, HALF), jnp.float32),
        compiler_params=limit(16),
        cost_estimate=pl.CostEstimate(flops=1 << 30, bytes_accessed=8 * MIB, transcendentals=0),
        name="far_mix",
    )(far, mid, acc, va)


def tail_kernel(info, _, q_ref, kv_ref, ka_ref, ko_ref, kl_ref, kh_ref, pt_ref, lt_ref):
    index, core = info[0], info[1]
    r16 = lax.broadcasted_iota(jnp.int32, (SHORT, 128), 0)
    c16 = lax.broadcasted_iota(jnp.int32, (SHORT, 128), 1)
    r512 = lax.broadcasted_iota(jnp.int32, (SHORT, ROWS), 0)
    c512 = lax.broadcasted_iota(jnp.int32, (SHORT, ROWS), 1)
    blank = jnp.zeros((128 - SHORT, HALF), jnp.bfloat16)
    first = jnp.concatenate([kv_ref[0:SHORT, :], blank], 0)
    places = [0, 128, 128 + ROWS, TAIL]
    totals = jnp.zeros((SHORT, 128), jnp.float32)
    for head in range(LOCAL_HEADS):
        columns = slice(head * HEAD, (head + 1) * HEAD)
        swapped = jnp.concatenate([kl_ref[:, columns], kh_ref[:, columns]], 0)
        kb = jnp.where(core == 0, swapped, ko_ref[:, columns])
        pieces = [
            (first[:, columns], index >= 3, (c16 > r16) & (c16 < SHORT)),
            (ka_ref[:, columns], index >= 2, None),
            (kb, index >= 1, c512 <= r512 + (ROWS - SHORT)),
        ]

        def store(step, p, head=head):
            pt_ref[head, :, places[step] : places[step + 1]] = p

        total = attend(q_ref[:, columns], pieces, store)
        totals = jnp.where(c16 == head, total, totals)
    lt_ref[...] = totals


def tail_probs(info, after, q, kv, ka, ko, ks):
    whole = pl.BlockSpec(memory_space=pltpu.VMEM)
    return pl.pallas_call(
        tail_kernel,
        in_specs=[pl.BlockSpec(memory_space=pltpu.SMEM), pl.BlockSpec(memory_space=pl.ANY)]
        + [whole] * 6,
        out_specs=[whole] * 2,
        out_shape=[
            jax.ShapeDtypeStruct((LOCAL_HEADS, SHORT, TAIL), jnp.bfloat16),
            jax.ShapeDtypeStruct((SHORT, 128), jnp.float32),
        ],
        compiler_params=limit(16),
        cost_estimate=pl.CostEstimate(flops=1 << 30, bytes_accessed=8 * MIB, transcendentals=0),
        name="tail_probs",
    )(info, after, q, kv, ka, ko, *ks)


def mix_kernel(
    info, near_ref, l_ref, acc_ref, va_ref, vs_ref, vo_ref, pt_ref, lt_ref, kv_ref, gain_ref,
    out_ref, sent_ref,
):
    core = info[1]

    def mix(with_near):
        j = lax.broadcasted_iota(jnp.int32, (CROWS, ROWS), 0)
        r = lax.broadcasted_iota(jnp.int32, (CROWS, ROWS), 1)
        pick = jnp.where((r > SHORT * j - SHORT) & (r <= SHORT * j), 1.0, 0.0)
        pick = pick.astype(jnp.bfloat16)
        j = lax.broadcasted_iota(jnp.int32, (CROWS, SHORT), 0)
        r = lax.broadcasted_iota(jnp.int32, (CROWS, SHORT), 1)
        pick_tail = jnp.where((j == 0) & (r > 0), 1.0, 0.0).astype(jnp.bfloat16)
        share = 1.0 / l_ref[...]
        some = lt_ref[...] > 0.0
        share_tail = jnp.where(some, 1.0 / jnp.where(some, lt_ref[...], 1.0), 0.0)
        blank = jnp.zeros((128 - SHORT, HALF), jnp.bfloat16)
        first = jnp.concatenate([kv_ref[SHORT : 2 * SHORT, :], blank], 0)
        squares = jnp.zeros((CROWS, HEAD), jnp.float32)
        before_ref = vs_ref if with_near else vo_ref
        for head in range(LOCAL_HEADS):
            columns = slice(head * HEAD, (head + 1) * HEAD)
            mixed = acc_ref[:, columns]
            if with_near:
                mixed = mixed + jnp.dot(
                    near_ref[head], vs_ref[:, columns], preferred_element_type=jnp.float32
                )
            out = (mixed * share[:, head : head + 1]).astype(jnp.bfloat16)
            out_ref[:, columns] = out
            tail = jnp.dot(
                pt_ref[head, :, 0:128], first[:, columns], preferred_element_type=jnp.float32
            )
            tail = tail + jnp.dot(
                pt_ref[head, :, 128 : 128 + ROWS], va_ref[:, columns],
                preferred_element_type=jnp.float32,
            )
            tail = tail + jnp.dot(
                pt_ref[head, :, 128 + ROWS : TAIL], before_ref[:, columns],
                preferred_element_type=jnp.float32,
            )
            tail = (tail * share_tail[:, head : head + 1]).astype(jnp.bfloat16)
            sums = jnp.dot(pick, out, preferred_element_type=jnp.float32)
            sums = sums + jnp.dot(pick_tail, tail, preferred_element_type=jnp.float32)
            pooled = sums * (1.0 / SHORT)
            squares = squares + pooled * pooled
            sent_ref[:, columns] = pooled * gain_ref[:, columns]
        sent_ref[:, HALF : HALF + 128] = jnp.broadcast_to(
            jnp.sum(squares, -1, keepdims=True), (CROWS, 128)
        )

    @pl.when(core == 0)
    def _():
        mix(True)

    @pl.when(core == 1)
    def _():
        mix(False)


def fine_mix(info, near, l, acc, va, vs, vo, pt, lt, kv, gain):
    whole = pl.BlockSpec(memory_space=pltpu.VMEM)
    return pl.pallas_call(
        mix_kernel,
        in_specs=[pl.BlockSpec(memory_space=pltpu.SMEM)] + [whole] * 10,
        out_specs=[whole] * 2,
        out_shape=[
            jax.ShapeDtypeStruct((ROWS, HALF), jnp.bfloat16),
            jax.ShapeDtypeStruct((CROWS, HALF + 128), jnp.float32),
        ],
        compiler_params=limit(20),
        cost_estimate=pl.CostEstimate(flops=1 << 30, bytes_accessed=8 * MIB, transcendentals=0),
        name="fine_mix",
    )(info, near, l, acc, va, vs, vo, pt, lt, kv, gain)


def norm_kernel(own_ref, other_ref, out_ref):
    squares = own_ref[:, HALF : HALF + 1] + other_ref[:, HALF : HALF + 1]
    factor = lax.rsqrt(squares / D_FINE + EPS)
    out_ref[:, 0:HALF] = (own_ref[:, 0:HALF] * factor).astype(jnp.bfloat16)
    out_ref[:, HALF : 2 * HALF] = (other_ref[:, 0:HALF] * factor).astype(jnp.bfloat16)


def normalise(own, other):
    whole = pl.BlockSpec(memory_space=pltpu.VMEM)
    return pl.pallas_call(
        norm_kernel,
        in_specs=[whole] * 2,
        out_specs=whole,
        out_shape=jax.ShapeDtypeStruct((CROWS, 2 * HALF), jnp.bfloat16),
        compiler_params=limit(4),
        cost_estimate=SMALL,
        name="normalise",
    )(own, other)


def project_kernel(info, *refs):
    row_refs, own_ref, far_refs, (kv_ref, key_ref, rows_ref, w_ref) = (
        refs[0:4], refs[4], refs[5:13], refs[13:],
    )
    c, x, y = info[1], info[2], info[3]
    for k in range(4):
        begin = pl.multiple_of((y - k + 4) % 4 * CROWS, CROWS)
        rows_ref[pl.ds(begin, CROWS), :] = row_refs[k][...]
    size = HALF // 8
    for piece in range(8):
        from_x = (x - piece // 2 + 4) % 4
        from_c = c if piece % 2 == 0 else 1 - c
        begin = pl.multiple_of((from_x * 2 + from_c) * size, size)
        w_ref[pl.ds(begin, size), :] = far_refs[piece][...]
    kv = jnp.dot(rows_ref[:, 0:HALF], own_ref[...], preferred_element_type=jnp.float32)
    kv = kv + jnp.dot(
        rows_ref[:, HALF : 2 * HALF], w_ref[...], preferred_element_type=jnp.float32
    )
    kv = kv.astype(jnp.bfloat16)
    kv_ref[...] = kv
    key_ref[...] = kv[:, 0:C_HEAD]


def project(info, rows, own, far):
    whole = pl.BlockSpec(memory_space=pltpu.VMEM)
    return pl.pallas_call(
        project_kernel,
        in_specs=[pl.BlockSpec(memory_space=pltpu.SMEM)] + [whole] * 13,
        out_specs=[whole, whole],
        out_shape=[
            jax.ShapeDtypeStruct((GROUP, 2 * C_HEAD), jnp.bfloat16),
            jax.ShapeDtypeStruct((GROUP, C_HEAD), jnp.bfloat16),
        ],
        scratch_shapes=[
            pltpu.VMEM((GROUP, 2 * HALF), jnp.bfloat16),
            pltpu.VMEM((HALF, 2 * C_HEAD), jnp.bfloat16),
        ],
        compiler_params=limit(20),
        cost_estimate=SMALL,
        name="project",
    )(info, *rows, own, *far)


def split3(value):
    first = value.astype(jnp.bfloat16).astype(jnp.float32)
    rest = value - first
    second = rest.astype(jnp.bfloat16).astype(jnp.float32)
    return first, second, rest - second


def coarse_kernel(info, *refs):
    q_refs, kv_refs, (out_ref, kv_all, q_all) = refs[0:4], refs[4:12], refs[12:]
    x, z, c = info[2], info[4], info[1]
    scale = 1.0 / math.sqrt(C_HEAD)
    keys = 8 * GROUP
    for piece in range(8):
        kv_all[piece * GROUP : (piece + 1) * GROUP, :] = kv_refs[piece][...]
    for k in range(4):
        begin = pl.multiple_of((x - k + 4) % 4 * GROUP, GROUP)
        q_all[pl.ds(begin, GROUP), :] = q_refs[k][...]
    slot = lax.broadcasted_iota(jnp.int32, (1, keys), 1)
    piece = slot // GROUP
    inside = slot % GROUP
    from_z = jnp.bitwise_xor(z, piece // 2)
    from_c = jnp.where(piece % 2 == 0, c, 1 - c)
    key_pos = (
        x * 1024 + (inside // CROWS) * 256 + from_z * 64 + from_c * 32 + inside % CROWS
    )
    place = lax.broadcasted_iota(jnp.int32, (4 * GROUP, 1), 0)
    inner = place % GROUP
    pos = (place // GROUP) * 1024 + (inner // CROWS) * 256 + z * 64 + c * 32 + inner % CROWS
    lane = lax.broadcasted_iota(jnp.int32, (4 * GROUP, 128), 1)
    allowed = key_pos < jnp.maximum(pos, 1)
    s = lax.dot_general(
        q_all[...], kv_all[:, 0:C_HEAD], (((1,), (1,)), ((), ())),
        preferred_element_type=jnp.float32,
    ) * scale
    s = jnp.where(allowed, s, NEG)
    top = jnp.max(s, -1, keepdims=True)
    p = jnp.where(allowed, jnp.exp(s - top), 0.0)
    total = jnp.sum(p, -1, keepdims=True)
    mixed = jnp.dot(
        p.astype(jnp.bfloat16), kv_all[:, C_HEAD : 2 * C_HEAD],
        preferred_element_type=jnp.float32,
    )
    some = total > 0.0
    safe = jnp.where(some, total, 1.0)
    mixed = jnp.where(some, mixed / safe, 0.0).astype(jnp.bfloat16)
    level = jnp.where(some, top + jnp.log(safe), NEG)
    a, b, d = split3(level)
    extra = jnp.where(lane == 0, a, jnp.where(lane == 1, b, jnp.where(lane == 2, d, 0.0)))
    extra = extra.astype(jnp.bfloat16)
    for piece in range(16):
        rows = slice(piece * CROWS, (piece + 1) * CROWS)
        out_ref[piece, :, 0:C_HEAD] = mixed[rows, :]
        out_ref[piece, :, C_HEAD : C_HEAD + 128] = extra[rows, :]


def coarse_attend(info, queries, pairs):
    whole = pl.BlockSpec(memory_space=pltpu.VMEM)
    return pl.pallas_call(
        coarse_kernel,
        grid=(1,),
        in_specs=[pl.BlockSpec(memory_space=pltpu.SMEM)]
        + [pl.BlockSpec((GROUP, C_HEAD), lambda i: (0, 0))]
        + [whole] * 3
        + [pl.BlockSpec((GROUP, 2 * C_HEAD), lambda i: (0, 0))]
        + [whole] * 7,
        out_specs=whole,
        out_shape=jax.ShapeDtypeStruct((16, CROWS, C_HEAD + 128), jnp.bfloat16),
        scratch_shapes=[
            pltpu.VMEM((8 * GROUP, 2 * C_HEAD), jnp.bfloat16),
            pltpu.VMEM((4 * GROUP, C_HEAD), jnp.bfloat16),
        ],
        compiler_params=limit(16),
        cost_estimate=pl.CostEstimate(
            flops=4 * 4 * GROUP * 8 * GROUP * C_HEAD,
            bytes_accessed=2 * MIB,
            transcendentals=4 * GROUP * 8 * GROUP,
        ),
        name="coarse_attend",
    )(info, *queries, *pairs)


def final_kernel(part_ref, fine_ref, out_ref, done_ref, sems):
    r = lax.broadcasted_iota(jnp.int32, (ROWS, CROWS), 0)
    j = lax.broadcasted_iota(jnp.int32, (ROWS, CROWS), 1)
    spread = jnp.where(r // SHORT == j, 1.0, 0.0).astype(jnp.bfloat16)
    coarse = []
    for head in range(4):
        parts = jnp.stack([part_ref[4 * i + head] for i in range(4)]).astype(jnp.float32)
        levels = jnp.sum(parts[:, :, C_HEAD : C_HEAD + 128], -1, keepdims=True)
        top = jnp.max(levels, 0, keepdims=True)
        weights = jnp.exp(levels - top)
        total = jnp.sum(weights, 0)
        mixed = jnp.sum(parts[:, :, 0:C_HEAD] * weights, 0) / total
        coarse.append(mixed.astype(jnp.bfloat16))
    coarse = jnp.concatenate(coarse, 1)
    stores = []
    for block in range(4):
        rows = slice(block * 128, (block + 1) * 128)
        up = jnp.dot(spread[rows, :], coarse, preferred_element_type=jnp.float32)
        done_ref[rows, :] = (fine_ref[rows, :].astype(jnp.float32) + up).astype(jnp.bfloat16)
        store = pltpu.make_async_copy(
            done_ref.at[pl.ds(block * 128, 128), :],
            out_ref.at[pl.ds(block * 128, 128), :],
            sems.at[block],
        )
        store.start()
        stores.append(store)
    for store in stores:
        store.wait()


def finish(parts, fine):
    whole = pl.BlockSpec(memory_space=pltpu.VMEM)
    return pl.pallas_call(
        final_kernel,
        in_specs=[whole] * 2,
        out_specs=pl.BlockSpec(memory_space=pl.ANY),
        out_shape=jax.ShapeDtypeStruct((ROWS, HALF), jnp.bfloat16),
        scratch_shapes=[
            pltpu.VMEM((ROWS, HALF), jnp.bfloat16),
            pltpu.SemaphoreType.DMA((4,)),
        ],
        compiler_params=limit(16),
        name="finish",
    )(parts, fine)


def per_device(fine_q, fine_k, fine_v, norm_gain, short_weight):
    x, y, z, c, m = (lax.axis_index(a) for a in CTX + ("m",))
    index = ((x * 4 + y) * 4 + z) * 2 + c
    info = jnp.stack([index, c, x, y, z, m]).astype(jnp.int32)

    k2 = shifted(fine_k, 2)
    v2 = shifted(fine_v, 2)
    ko = rolled(fine_k, "c", 1)
    vo = rolled(fine_v, "c", 1)
    part, own_columns, last_q, last_kv = pick_columns(
        info, short_weight, fine_q, fine_k, fine_v
    )
    k2, part, last_q, last_kv = lax.optimization_barrier((k2, part, last_q, last_kv))
    tail_q = shifted(last_q, 1)
    tail_kv = shifted(last_kv, 3)
    ks = [rolled(piece, "c", 1) for piece in halves(k2)]
    far, mid, near, l, acc = fine_probs(info, fine_q, k2, ks, ko, fine_k, vo, fine_v)
    v2, l, tail_q, tail_kv = lax.optimization_barrier((v2, l, tail_q, tail_kv))
    vs = rolled(v2, "c", 1)
    acc = far_mix(far, mid, acc, v2)
    pt, lt = tail_probs(info, v2, tail_q, tail_kv, k2, ko, ks)
    fine_out, pooled = fine_mix(
        info, near, l, acc, v2, vs, vo, pt, lt, tail_kv, norm_gain[None]
    )

    part = rolled(part, "m", 1)
    part, pooled = lax.optimization_barrier((part, pooled))
    eighths = [part] + [rolled(part, "x", k) for k in (1, 2, 3)]

    other = rolled(pooled, "m", 1)
    normed = normalise(pooled, other)
    normed, *eighths = lax.optimization_barrier((normed, *eighths))
    columns = []
    for piece in eighths:
        columns += [piece, rolled(piece, "c", 1)]
    rows = [normed] + [rolled(normed, "y", k) for k in (1, 2, 3)]
    kv, own_keys = project(info, rows, own_columns, columns)

    queries = [own_keys] + [rolled(own_keys, "x", k) for k in (1, 2, 3)]
    far = [paired(kv, "z", k) for k in (2, 3)]
    pieces = [kv, paired(kv, "z", 1)] + far
    held = lax.optimization_barrier((*queries, *pieces))
    queries, pieces = held[:4], held[4:]
    pairs = []
    for piece in pieces:
        pairs += [piece, rolled(piece, "c", 1)]
    parts = coarse_attend(info, queries, pairs)
    parts = lax.all_to_all(parts, ("x", "y"), split_axis=0, concat_axis=0, tiled=True)
    return finish(parts, fine_out)


def solution(mesh):
    grid = Mesh(mesh.devices.reshape(4, 4, 4, 2, 2), ("x", "y", "z", "c", "m"))
    rows = P(CTX, "m")
    return jax.shard_map(
        per_device,
        mesh=grid,
        in_specs=(rows, rows, rows, P("m"), P("m", None)),
        out_specs=rows,
        check_vma=False,
    )
```

```python
import functools
import math

import jax
import jax.numpy as jnp
from jax import lax
from jax.experimental import pallas as pl
from jax.experimental.pallas import tpu as pltpu
from jax.sharding import Mesh
from jax.sharding import PartitionSpec as P

D_FINE = 2048
HEADS = 16
HEAD = 128
C_HEADS = 8
C_HEAD = 256
WINDOW = 1024
SHORT = 16
EPS = 1e-05
NEG = -1e30
LOG2E = 1.4426950408889634

ROWS = 512
HALF = 1024
LOCAL_HEADS = HALF // HEAD
TILE = 256
CROWS = ROWS // SHORT
UNROLL = 1
TAIL = 128 + 2 * ROWS
GROUP = 4 * CROWS
SMALL = pl.CostEstimate(flops=1, bytes_accessed=1, transcendentals=0)
CTX = ("x", "y", "z", "c")
MIB = 1 << 20


def shifted(value, steps):
    count = 128
    return lax.ppermute(
        value, CTX, [(s, s + steps) for s in range(max(0, -steps), min(count, count - steps))]
    )


def rolled(value, axis, steps):
    count = lax.axis_size(axis)
    return lax.ppermute(value, axis, [(s, (s + steps) % count) for s in range(count)])


def paired(value, axis, distance):
    count = lax.axis_size(axis)
    return lax.ppermute(value, axis, [(s, s ^ distance) for s in range(count)])


def limit(mib):
    return pltpu.CompilerParams(vmem_limit_bytes=mib * MIB)


def halves_kernel(in_ref, low_ref, high_ref):
    low_ref[...] = in_ref[0:TILE, :]
    high_ref[...] = in_ref[TILE : 2 * TILE, :]


def halves(value):
    half = pl.BlockSpec((TILE, 512), lambda i: (0, i))
    return pl.pallas_call(
        halves_kernel,
        grid=(2,),
        in_specs=[pl.BlockSpec((ROWS, 512), lambda i: (0, i))],
        out_specs=[half] * 2,
        out_shape=[jax.ShapeDtypeStruct((TILE, HALF), jnp.bfloat16)] * 2,
        compiler_params=limit(8),
        cost_estimate=SMALL,
        name="halves",
    )(value)


def pick_kernel(
    info, part_ref, own_ref, q_ref, k_ref, v_ref, part_out, own_out, q_out, kv_out
):
    part_out[...] = part_ref[...]
    own_out[...] = own_ref[...]
    q_out[...] = q_ref[...]
    kv_out[0:SHORT, :] = k_ref[...]
    kv_out[SHORT : 2 * SHORT, :] = v_ref[...]


def pick_columns(info, weight, q, k, v):
    wide = 2 * C_HEAD
    size = HALF // 8
    part = pl.BlockSpec(
        (size, wide), lambda i, info: (info[2] * 2 + info[1], (1 - info[5]) * 4 + info[3])
    )
    own = pl.BlockSpec((HALF // 4, wide), lambda i, info: (i, info[5] * 4 + info[3]))
    end = pl.BlockSpec((SHORT, HALF), lambda i, info: (ROWS // SHORT - 1, 0))
    first = lambda rows, columns: pl.BlockSpec((rows, columns), lambda i, info: (0, 0))
    return pl.pallas_call(
        pick_kernel,
        grid_spec=pltpu.PrefetchScalarGridSpec(
            num_scalar_prefetch=1,
            grid=(4,),
            in_specs=[part, own, end, end, end],
            out_specs=[
                first(size, wide),
                pl.BlockSpec((HALF // 4, wide), lambda i, info: (i, 0)),
                first(SHORT, HALF),
                first(2 * SHORT, HALF),
            ],
        ),
        out_shape=[
            jax.ShapeDtypeStruct((size, wide), jnp.bfloat16),
            jax.ShapeDtypeStruct((HALF, wide), jnp.bfloat16),
            jax.ShapeDtypeStruct((SHORT, HALF), jnp.bfloat16),
            jax.ShapeDtypeStruct((2 * SHORT, HALF), jnp.bfloat16),
        ],
        compiler_params=limit(8),
        cost_estimate=pl.CostEstimate(flops=1 << 30, bytes_accessed=2 * MIB, transcendentals=0),
        name="pick_columns",
    )(info, weight, weight, q, k, v)


def attend(q, pieces, store):
    scale = LOG2E / math.sqrt(HEAD)

    def fold(combine, value):
        lanes = value[:, 0:128]
        for i in range(1, value.shape[1] // 128):
            lanes = combine(lanes, value[:, i * 128 : (i + 1) * 128])
        return lanes

    scores = []
    top = None
    for keys, okay, mask in pieces:
        s = lax.dot_general(
            q, keys, (((1,), (1,)), ((), ())), preferred_element_type=jnp.float32
        )
        if mask is not None:
            s = jnp.where(mask, s, NEG)
        scores.append(s)
        high = fold(jnp.maximum, s)
        if okay is not None:
            high = jnp.where(okay, high, NEG)
        top = high if top is None else jnp.maximum(top, high)
    top = jnp.max(top, -1, keepdims=True)
    total = None
    for step, (keys, okay, mask) in enumerate(pieces):
        base = top if okay is None else jnp.where(okay, top, -NEG)
        p = jnp.exp2((scores[step] - base) * scale)
        part = fold(jnp.add, p)
        total = part if total is None else total + part
        store(step, p.astype(jnp.bfloat16))
    return jnp.sum(total, -1, keepdims=True)


def probs_kernel(
    info, q_ref, ka_ref, ko_ref, kc_ref, vo_ref, vc_ref, kl_ref, kh_ref,
    far_ref, mid_ref, near_ref, l_ref, acc_ref,
):
    index = info[0]
    core = info[1]
    valid = [index >= 2, index >= 2, index >= 1, index >= 1, None, None]
    row = lax.broadcasted_iota(jnp.int32, (TILE, TILE), 0)
    col = lax.broadcasted_iota(jnp.int32, (TILE, TILE), 1)
    lane = lax.broadcasted_iota(jnp.int32, (TILE, 128), 1)
    low, high = slice(0, TILE), slice(TILE, 2 * TILE)
    l_ref[...] = jnp.ones_like(l_ref)

    def one_head(head, carry):
        columns = pl.ds(pl.multiple_of(head * HEAD, HEAD), HEAD)
        chunks = [
            ka_ref[low, columns],
            ka_ref[high, columns],
            jnp.where(core == 0, kl_ref[:, columns], ko_ref[low, columns]),
            jnp.where(core == 0, kh_ref[:, columns], ko_ref[high, columns]),
            kc_ref[low, columns],
            kc_ref[high, columns],
        ]
        for tile in range(ROWS // TILE):
            masks = [col > row, None, None, None, col <= row]
            keys = [(chunks[tile + j], valid[tile + j], masks[j]) for j in range(5)]
            rows = slice(tile * TILE, (tile + 1) * TILE)

            def store(step, p, tile=tile, rows=rows):
                chunk = tile + step
                if chunk == 0:
                    far_ref[head] = p
                elif chunk == 1:
                    mid_ref[head, rows, :] = p
                elif chunk < 4:
                    near_ref[head, rows, (chunk - 2) * TILE : (chunk - 1) * TILE] = p
                else:
                    values = vc_ref[low if chunk == 4 else high, columns]
                    part = jnp.dot(p, values, preferred_element_type=jnp.float32)
                    if chunk == 5:
                        part = part + acc_ref[rows, columns]
                    acc_ref[rows, columns] = part

            total = attend(q_ref[rows, columns], keys, store)
            l_ref[rows, :] = jnp.where(lane == head, total, l_ref[rows, :])

        @pl.when(core == 1)
        def _():
            acc_ref[:, columns] = acc_ref[:, columns] + jnp.dot(
                near_ref[head], vo_ref[:, columns], preferred_element_type=jnp.float32
            )

        return carry

    lax.fori_loop(0, LOCAL_HEADS, one_head, 0, unroll=UNROLL)


def fine_probs(info, q, ka, ks, ko, kc, vo, vc):
    whole = pl.BlockSpec(memory_space=pltpu.VMEM)
    return pl.pallas_call(
        probs_kernel,
        in_specs=[pl.BlockSpec(memory_space=pltpu.SMEM)] + [whole] * 8,
        out_specs=[whole] * 5,
        out_shape=[
            jax.ShapeDtypeStruct((LOCAL_HEADS, TILE, TILE), jnp.bfloat16),
            jax.ShapeDtypeStruct((LOCAL_HEADS, ROWS, TILE), jnp.bfloat16),
            jax.ShapeDtypeStruct((LOCAL_HEADS, ROWS, ROWS), jnp.bfloat16),
            jax.ShapeDtypeStruct((ROWS, 128), jnp.float32),
            jax.ShapeDtypeStruct((ROWS, HALF), jnp.float32),
        ],
        compiler_params=limit(20),
        cost_estimate=SMALL,
        name="fine_probs",
    )(info, q, ka, ko, kc, vo, vc, *ks)


def far_kernel(far_ref, mid_ref, acc_ref, va_ref, out_ref):
    for head in range(LOCAL_HEADS):
        columns = slice(head * HEAD, (head + 1) * HEAD)
        mixed = acc_ref[:, columns] + jnp.dot(
            mid_ref[head], va_ref[TILE : 2 * TILE, columns], preferred_element_type=jnp.float32
        )
        out_ref[0:TILE, columns] = mixed[0:TILE, :] + jnp.dot(
            far_ref[head], va_ref[0:TILE, columns], preferred_element_type=jnp.float32
        )
        out_ref[TILE : 2 * TILE, columns] = mixed[TILE : 2 * TILE, :]


def far_mix(far, mid, acc, va):
    whole = pl.BlockSpec(memory_space=pltpu.VMEM)
    return pl.pallas_call(
        far_kernel,
        in_specs=[whole] * 4,
        out_specs=whole,
        out_shape=jax.ShapeDtypeStruct((ROWS, HALF), jnp.float32),
        compiler_params=limit(16),
        cost_estimate=pl.CostEstimate(flops=1 << 30, bytes_accessed=8 * MIB, transcendentals=0),
        name="far_mix",
    )(far, mid, acc, va)


def tail_kernel(info, _, q_ref, kv_ref, ka_ref, ko_ref, kl_ref, kh_ref, pt_ref, lt_ref):
    index, core = info[0], info[1]
    r16 = lax.broadcasted_iota(jnp.int32, (SHORT, 128), 0)
    c16 = lax.broadcasted_iota(jnp.int32, (SHORT, 128), 1)
    r512 = lax.broadcasted_iota(jnp.int32, (SHORT, ROWS), 0)
    c512 = lax.broadcasted_iota(jnp.int32, (SHORT, ROWS), 1)
    blank = jnp.zeros((128 - SHORT, HALF), jnp.bfloat16)
    first = jnp.concatenate([kv_ref[0:SHORT, :], blank], 0)
    places = [0, 128, 128 + ROWS, TAIL]
    totals = jnp.zeros((SHORT, 128), jnp.float32)
    for head in range(LOCAL_HEADS):
        columns = slice(head * HEAD, (head + 1) * HEAD)
        swapped = jnp.concatenate([kl_ref[:, columns], kh_ref[:, columns]], 0)
        kb = jnp.where(core == 0, swapped, ko_ref[:, columns])
        pieces = [
            (first[:, columns], index >= 3, (c16 > r16) & (c16 < SHORT)),
            (ka_ref[:, columns], index >= 2, None),
            (kb, index >= 1, c512 <= r512 + (ROWS - SHORT)),
        ]

        def store(step, p, head=head):
            pt_ref[head, :, places[step] : places[step + 1]] = p

        total = attend(q_ref[:, columns], pieces, store)
        totals = jnp.where(c16 == head, total, totals)
    lt_ref[...] = totals


def tail_probs(info, after, q, kv, ka, ko, ks):
    whole = pl.BlockSpec(memory_space=pltpu.VMEM)
    return pl.pallas_call(
        tail_kernel,
        in_specs=[pl.BlockSpec(memory_space=pltpu.SMEM)]
        + [pl.BlockSpec(memory_space=pl.ANY)]
        + [whole] * 6,
        out_specs=[whole] * 2,
        out_shape=[
            jax.ShapeDtypeStruct((LOCAL_HEADS, SHORT, TAIL), jnp.bfloat16),
            jax.ShapeDtypeStruct((SHORT, 128), jnp.float32),
        ],
        compiler_params=limit(16),
        cost_estimate=pl.CostEstimate(flops=1 << 30, bytes_accessed=8 * MIB, transcendentals=0),
        name="tail_probs",
    )(info, after, q, kv, ka, ko, *ks)


def mix_kernel(
    info, near_ref, l_ref, acc_ref, va_ref, vs_ref, vo_ref, pt_ref, lt_ref, kv_ref, gain_ref,
    out_ref, sent_ref,
):
    core = info[1]

    def mix(with_near):
        j = lax.broadcasted_iota(jnp.int32, (CROWS, ROWS), 0)
        r = lax.broadcasted_iota(jnp.int32, (CROWS, ROWS), 1)
        pick = jnp.where((r > SHORT * j - SHORT) & (r <= SHORT * j), 1.0, 0.0)
        pick = pick.astype(jnp.bfloat16)
        j = lax.broadcasted_iota(jnp.int32, (CROWS, SHORT), 0)
        r = lax.broadcasted_iota(jnp.int32, (CROWS, SHORT), 1)
        pick_tail = jnp.where((j == 0) & (r > 0), 1.0, 0.0).astype(jnp.bfloat16)
        share = 1.0 / l_ref[...]
        some = lt_ref[...] > 0.0
        share_tail = jnp.where(some, 1.0 / jnp.where(some, lt_ref[...], 1.0), 0.0)
        blank = jnp.zeros((128 - SHORT, HALF), jnp.bfloat16)
        first = jnp.concatenate([kv_ref[SHORT : 2 * SHORT, :], blank], 0)
        squares = jnp.zeros((CROWS, HEAD), jnp.float32)
        before_ref = vs_ref if with_near else vo_ref
        for head in range(LOCAL_HEADS):
            columns = slice(head * HEAD, (head + 1) * HEAD)
            mixed = acc_ref[:, columns]
            if with_near:
                mixed = mixed + jnp.dot(
                    near_ref[head], vs_ref[:, columns], preferred_element_type=jnp.float32
                )
            out = (mixed * share[:, head : head + 1]).astype(jnp.bfloat16)
            out_ref[:, columns] = out
            tail = jnp.dot(
                pt_ref[head, :, 0:128], first[:, columns], preferred_element_type=jnp.float32
            )
            tail = tail + jnp.dot(
                pt_ref[head, :, 128 : 128 + ROWS], va_ref[:, columns],
                preferred_element_type=jnp.float32,
            )
            tail = tail + jnp.dot(
                pt_ref[head, :, 128 + ROWS : TAIL], before_ref[:, columns],
                preferred_element_type=jnp.float32,
            )
            tail = (tail * share_tail[:, head : head + 1]).astype(jnp.bfloat16)
            sums = jnp.dot(pick, out, preferred_element_type=jnp.float32)
            sums = sums + jnp.dot(pick_tail, tail, preferred_element_type=jnp.float32)
            pooled = sums * (1.0 / SHORT)
            squares = squares + pooled * pooled
            sent_ref[:, columns] = pooled * gain_ref[:, columns]
        sent_ref[:, HALF : HALF + 128] = jnp.broadcast_to(
            jnp.sum(squares, -1, keepdims=True), (CROWS, 128)
        )

    @pl.when(core == 0)
    def _():
        mix(True)

    @pl.when(core == 1)
    def _():
        mix(False)


def fine_mix(info, near, l, acc, va, vs, vo, pt, lt, kv, gain):
    whole = pl.BlockSpec(memory_space=pltpu.VMEM)
    return pl.pallas_call(
        mix_kernel,
        in_specs=[pl.BlockSpec(memory_space=pltpu.SMEM)] + [whole] * 10,
        out_specs=[whole] * 2,
        out_shape=[
            jax.ShapeDtypeStruct((ROWS, HALF), jnp.bfloat16),
            jax.ShapeDtypeStruct((CROWS, HALF + 128), jnp.float32),
        ],
        compiler_params=limit(20),
        cost_estimate=pl.CostEstimate(flops=1 << 30, bytes_accessed=8 * MIB, transcendentals=0),
        name="fine_mix",
    )(info, near, l, acc, va, vs, vo, pt, lt, kv, gain)


def norm_kernel(own_ref, other_ref, out_ref):
    squares = own_ref[:, HALF : HALF + 1] + other_ref[:, HALF : HALF + 1]
    factor = lax.rsqrt(squares / D_FINE + EPS)
    out_ref[:, 0:HALF] = (own_ref[:, 0:HALF] * factor).astype(jnp.bfloat16)
    out_ref[:, HALF : 2 * HALF] = (other_ref[:, 0:HALF] * factor).astype(jnp.bfloat16)


def normalise(own, other):
    whole = pl.BlockSpec(memory_space=pltpu.VMEM)
    return pl.pallas_call(
        norm_kernel,
        in_specs=[whole] * 2,
        out_specs=whole,
        out_shape=jax.ShapeDtypeStruct((CROWS, 2 * HALF), jnp.bfloat16),
        compiler_params=limit(4),
        cost_estimate=SMALL,
        name="normalise",
    )(own, other)


def project_kernel(info, *refs):
    row_refs, own_ref, far_refs, (kv_ref, key_ref, rows_ref, w_ref) = (
        refs[0:4], refs[4], refs[5:13], refs[13:],
    )
    c, x, y = info[1], info[2], info[3]
    for k in range(4):
        begin = pl.multiple_of((y - k + 4) % 4 * CROWS, CROWS)
        rows_ref[pl.ds(begin, CROWS), :] = row_refs[k][...]
    size = HALF // 8
    for piece in range(8):
        from_x = (x - piece // 2 + 4) % 4
        from_c = c if piece % 2 == 0 else 1 - c
        begin = pl.multiple_of((from_x * 2 + from_c) * size, size)
        w_ref[pl.ds(begin, size), :] = far_refs[piece][...]
    kv = jnp.dot(rows_ref[:, 0:HALF], own_ref[...], preferred_element_type=jnp.float32)
    kv = kv + jnp.dot(
        rows_ref[:, HALF : 2 * HALF], w_ref[...], preferred_element_type=jnp.float32
    )
    kv = kv.astype(jnp.bfloat16)
    kv_ref[...] = kv
    key_ref[...] = kv[:, 0:C_HEAD]


def project(info, rows, own, far):
    whole = pl.BlockSpec(memory_space=pltpu.VMEM)
    return pl.pallas_call(
        project_kernel,
        in_specs=[pl.BlockSpec(memory_space=pltpu.SMEM)] + [whole] * 13,
        out_specs=[whole, whole],
        out_shape=[
            jax.ShapeDtypeStruct((GROUP, 2 * C_HEAD), jnp.bfloat16),
            jax.ShapeDtypeStruct((GROUP, C_HEAD), jnp.bfloat16),
        ],
        scratch_shapes=[
            pltpu.VMEM((GROUP, 2 * HALF), jnp.bfloat16),
            pltpu.VMEM((HALF, 2 * C_HEAD), jnp.bfloat16),
        ],
        compiler_params=limit(20),
        cost_estimate=SMALL,
        name="project",
    )(info, *rows, own, *far)


def split3(value):
    first = value.astype(jnp.bfloat16).astype(jnp.float32)
    rest = value - first
    second = rest.astype(jnp.bfloat16).astype(jnp.float32)
    return first, second, rest - second


def coarse_kernel(info, *refs):
    q_refs, kv_refs, (out_ref, kv_all, q_all) = refs[0:4], refs[4:12], refs[12:]
    x, z, c = info[2], info[4], info[1]
    scale = 1.0 / math.sqrt(C_HEAD)
    keys = 8 * GROUP
    for piece in range(8):
        kv_all[piece * GROUP : (piece + 1) * GROUP, :] = kv_refs[piece][...]
    for k in range(4):
        begin = pl.multiple_of((x - k + 4) % 4 * GROUP, GROUP)
        q_all[pl.ds(begin, GROUP), :] = q_refs[k][...]
    slot = lax.broadcasted_iota(jnp.int32, (1, keys), 1)
    piece = slot // GROUP
    inside = slot % GROUP
    from_z = jnp.bitwise_xor(z, piece // 2)
    from_c = jnp.where(piece % 2 == 0, c, 1 - c)
    key_pos = (
        x * 1024 + (inside // CROWS) * 256 + from_z * 64 + from_c * 32 + inside % CROWS
    )
    place = lax.broadcasted_iota(jnp.int32, (4 * GROUP, 1), 0)
    inner = place % GROUP
    pos = (place // GROUP) * 1024 + (inner // CROWS) * 256 + z * 64 + c * 32 + inner % CROWS
    lane = lax.broadcasted_iota(jnp.int32, (4 * GROUP, 128), 1)
    allowed = key_pos < jnp.maximum(pos, 1)
    s = lax.dot_general(
        q_all[...], kv_all[:, 0:C_HEAD], (((1,), (1,)), ((), ())),
        preferred_element_type=jnp.float32,
    ) * scale
    s = jnp.where(allowed, s, NEG)
    top = jnp.max(s, -1, keepdims=True)
    p = jnp.where(allowed, jnp.exp(s - top), 0.0)
    total = jnp.sum(p, -1, keepdims=True)
    mixed = jnp.dot(
        p.astype(jnp.bfloat16), kv_all[:, C_HEAD : 2 * C_HEAD],
        preferred_element_type=jnp.float32,
    )
    some = total > 0.0
    safe = jnp.where(some, total, 1.0)
    mixed = jnp.where(some, mixed / safe, 0.0).astype(jnp.bfloat16)
    level = jnp.where(some, top + jnp.log(safe), NEG)
    a, b, d = split3(level)
    extra = jnp.where(lane == 0, a, jnp.where(lane == 1, b, jnp.where(lane == 2, d, 0.0)))
    extra = extra.astype(jnp.bfloat16)
    for piece in range(16):
        rows = slice(piece * CROWS, (piece + 1) * CROWS)
        out_ref[piece, :, 0:C_HEAD] = mixed[rows, :]
        out_ref[piece, :, C_HEAD : C_HEAD + 128] = extra[rows, :]


def coarse_attend(info, queries, pairs):
    whole = pl.BlockSpec(memory_space=pltpu.VMEM)
    return pl.pallas_call(
        coarse_kernel,
        grid=(1,),
        in_specs=[pl.BlockSpec(memory_space=pltpu.SMEM)]
        + [pl.BlockSpec((GROUP, C_HEAD), lambda i: (0, 0))]
        + [whole] * 3
        + [pl.BlockSpec((GROUP, 2 * C_HEAD), lambda i: (0, 0))]
        + [whole] * 7,
        out_specs=whole,
        out_shape=jax.ShapeDtypeStruct((16, CROWS, C_HEAD + 128), jnp.bfloat16),
        scratch_shapes=[
            pltpu.VMEM((8 * GROUP, 2 * C_HEAD), jnp.bfloat16),
            pltpu.VMEM((4 * GROUP, C_HEAD), jnp.bfloat16),
        ],
        compiler_params=limit(16),
        cost_estimate=pl.CostEstimate(
            flops=4 * 4 * GROUP * 8 * GROUP * C_HEAD,
            bytes_accessed=2 * MIB,
            transcendentals=4 * GROUP * 8 * GROUP,
        ),
        name="coarse_attend",
    )(info, *queries, *pairs)


def final_kernel(part_ref, fine_ref, out_ref, done_ref, sems):
    r = lax.broadcasted_iota(jnp.int32, (ROWS, CROWS), 0)
    j = lax.broadcasted_iota(jnp.int32, (ROWS, CROWS), 1)
    spread = jnp.where(r // SHORT == j, 1.0, 0.0).astype(jnp.bfloat16)
    coarse = []
    for head in range(4):
        parts = jnp.stack([part_ref[4 * i + head] for i in range(4)]).astype(jnp.float32)
        levels = jnp.sum(parts[:, :, C_HEAD : C_HEAD + 128], -1, keepdims=True)
        top = jnp.max(levels, 0, keepdims=True)
        weights = jnp.exp(levels - top)
        total = jnp.sum(weights, 0)
        mixed = jnp.sum(parts[:, :, 0:C_HEAD] * weights, 0) / total
        coarse.append(mixed.astype(jnp.bfloat16))
    coarse = jnp.concatenate(coarse, 1)
    stores = []
    for block in range(4):
        rows = slice(block * 128, (block + 1) * 128)
        up = jnp.dot(spread[rows, :], coarse, preferred_element_type=jnp.float32)
        done_ref[rows, :] = (fine_ref[rows, :].astype(jnp.float32) + up).astype(jnp.bfloat16)
        store = pltpu.make_async_copy(
            done_ref.at[pl.ds(block * 128, 128), :],
            out_ref.at[pl.ds(block * 128, 128), :],
            sems.at[block],
        )
        store.start()
        stores.append(store)
    for store in stores:
        store.wait()


def finish(parts, fine):
    whole = pl.BlockSpec(memory_space=pltpu.VMEM)
    return pl.pallas_call(
        final_kernel,
        in_specs=[whole] * 2,
        out_specs=pl.BlockSpec(memory_space=pl.ANY),
        out_shape=jax.ShapeDtypeStruct((ROWS, HALF), jnp.bfloat16),
        scratch_shapes=[
            pltpu.VMEM((ROWS, HALF), jnp.bfloat16),
            pltpu.SemaphoreType.DMA((4,)),
        ],
        compiler_params=limit(16),
        name="finish",
    )(parts, fine)


def per_device(fine_q, fine_k, fine_v, norm_gain, short_weight):
    x, y, z, c, m = (lax.axis_index(a) for a in CTX + ("m",))
    index = ((x * 4 + y) * 4 + z) * 2 + c
    info = jnp.stack([index, c, x, y, z, m]).astype(jnp.int32)

    k2 = shifted(fine_k, 2)
    v2 = shifted(fine_v, 2)
    ko = rolled(fine_k, "c", 1)
    vo = rolled(fine_v, "c", 1)
    part, own_columns, last_q, last_kv = pick_columns(
        info, short_weight, fine_q, fine_k, fine_v
    )
    k2 = lax.optimization_barrier((k2, last_q))[0]
    tail_q = shifted(last_q, 1)
    tail_kv = shifted(last_kv, 3)
    part = rolled(part, "m", 1)
    ks = [rolled(piece, "c", 1) for piece in halves(k2)]
    far, mid, near, l, acc = fine_probs(info, fine_q, k2, ks, ko, fine_k, vo, fine_v)
    v2, l, tail_q, tail_kv = lax.optimization_barrier((v2, l, tail_q, tail_kv))
    vs = rolled(v2, "c", 1)
    acc = far_mix(far, mid, acc, v2)
    pt, lt = tail_probs(info, v2, tail_q, tail_kv, k2, ko, ks)
    fine_out, pooled = fine_mix(
        info, near, l, acc, v2, vs, vo, pt, lt, tail_kv, norm_gain[None]
    )

    part, pooled = lax.optimization_barrier((part, pooled))
    eighths = [part] + [rolled(part, "x", k) for k in (1, 2, 3)]

    other = rolled(pooled, "m", 1)
    normed = normalise(pooled, other)
    normed, *eighths = lax.optimization_barrier((normed, *eighths))
    columns = []
    for piece in eighths:
        columns += [piece, rolled(piece, "c", 1)]
    rows = [normed] + [rolled(normed, "y", k) for k in (1, 2, 3)]
    kv, own_keys = project(info, rows, own_columns, columns)

    queries = [own_keys] + [rolled(own_keys, "x", k) for k in (1, 2, 3)]
    far = [paired(kv, "z", k) for k in (2, 3)]
    pieces = [kv, paired(kv, "z", 1)] + far
    held = lax.optimization_barrier((*queries, *pieces))
    queries, pieces = held[:4], held[4:]
    pairs = []
    for piece in pieces:
        pairs += [piece, rolled(piece, "c", 1)]
    parts = coarse_attend(info, queries, pairs)
    parts = lax.all_to_all(parts, ("x", "y"), split_axis=0, concat_axis=0, tiled=True)
    return finish(parts, fine_out)


def solution(mesh):
    grid = Mesh(mesh.devices.reshape(4, 4, 4, 2, 2), ("x", "y", "z", "c", "m"))
    rows = P(CTX, "m")
    return jax.shard_map(
        per_device,
        mesh=grid,
        in_specs=(rows, rows, rows, P("m"), P("m", None)),
        out_specs=rows,
        check_vma=False,
    )
```

```python
import functools
import math

import jax
import jax.numpy as jnp
from jax import lax
from jax.experimental import pallas as pl
from jax.experimental.pallas import tpu as pltpu
from jax.sharding import Mesh
from jax.sharding import PartitionSpec as P

D_FINE = 2048
HEADS = 16
HEAD = 128
C_HEADS = 8
C_HEAD = 256
WINDOW = 1024
SHORT = 16
EPS = 1e-05
NEG = -1e30
LOG2E = 1.4426950408889634

ROWS = 512
HALF = 1024
LOCAL_HEADS = HALF // HEAD
TILE = 256
CROWS = ROWS // SHORT
UNROLL = 1
TAIL = 128 + 2 * ROWS
GROUP = 4 * CROWS
SMALL = pl.CostEstimate(flops=1, bytes_accessed=1, transcendentals=0)
CTX = ("x", "y", "z", "c")
MIB = 1 << 20


def shifted(value, steps):
    count = 128
    return lax.ppermute(
        value, CTX, [(s, s + steps) for s in range(max(0, -steps), min(count, count - steps))]
    )


def rolled(value, axis, steps):
    count = lax.axis_size(axis)
    return lax.ppermute(value, axis, [(s, (s + steps) % count) for s in range(count)])


def paired(value, axis, distance):
    count = lax.axis_size(axis)
    return lax.ppermute(value, axis, [(s, s ^ distance) for s in range(count)])


def limit(mib):
    return pltpu.CompilerParams(vmem_limit_bytes=mib * MIB)


def halves_kernel(in_ref, low_ref, high_ref):
    low_ref[...] = in_ref[0:TILE, :]
    high_ref[...] = in_ref[TILE : 2 * TILE, :]


def halves(value):
    half = pl.BlockSpec((TILE, 512), lambda i: (0, i))
    return pl.pallas_call(
        halves_kernel,
        grid=(2,),
        in_specs=[pl.BlockSpec((ROWS, 512), lambda i: (0, i))],
        out_specs=[half] * 2,
        out_shape=[jax.ShapeDtypeStruct((TILE, HALF), jnp.bfloat16)] * 2,
        compiler_params=limit(8),
        cost_estimate=SMALL,
        name="halves",
    )(value)


def pick_kernel(
    info, part_ref, own_ref, q_ref, k_ref, v_ref, part_out, own_out, q_out, kv_out
):
    part_out[...] = part_ref[...]
    own_out[...] = own_ref[...]
    q_out[...] = q_ref[...]
    kv_out[0:SHORT, :] = k_ref[...]
    kv_out[SHORT : 2 * SHORT, :] = v_ref[...]


def pick_columns(info, weight, q, k, v):
    wide = 2 * C_HEAD
    size = HALF // 8
    part = pl.BlockSpec(
        (size, wide), lambda i, info: (info[2] * 2 + info[1], (1 - info[5]) * 4 + info[3])
    )
    own = pl.BlockSpec((HALF // 4, wide), lambda i, info: (i, info[5] * 4 + info[3]))
    end = pl.BlockSpec((SHORT, HALF), lambda i, info: (ROWS // SHORT - 1, 0))
    first = lambda rows, columns: pl.BlockSpec((rows, columns), lambda i, info: (0, 0))
    return pl.pallas_call(
        pick_kernel,
        grid_spec=pltpu.PrefetchScalarGridSpec(
            num_scalar_prefetch=1,
            grid=(4,),
            in_specs=[part, own, end, end, end],
            out_specs=[
                first(size, wide),
                pl.BlockSpec((HALF // 4, wide), lambda i, info: (i, 0)),
                first(SHORT, HALF),
                first(2 * SHORT, HALF),
            ],
        ),
        out_shape=[
            jax.ShapeDtypeStruct((size, wide), jnp.bfloat16),
            jax.ShapeDtypeStruct((HALF, wide), jnp.bfloat16),
            jax.ShapeDtypeStruct((SHORT, HALF), jnp.bfloat16),
            jax.ShapeDtypeStruct((2 * SHORT, HALF), jnp.bfloat16),
        ],
        compiler_params=limit(8),
        cost_estimate=pl.CostEstimate(flops=1 << 30, bytes_accessed=2 * MIB, transcendentals=0),
        name="pick_columns",
    )(info, weight, weight, q, k, v)


def attend(q, pieces, store):
    scale = LOG2E / math.sqrt(HEAD)

    def fold(combine, value):
        lanes = value[:, 0:128]
        for i in range(1, value.shape[1] // 128):
            lanes = combine(lanes, value[:, i * 128 : (i + 1) * 128])
        return lanes

    scores = []
    top = None
    for keys, okay, mask in pieces:
        s = lax.dot_general(
            q, keys, (((1,), (1,)), ((), ())), preferred_element_type=jnp.float32
        )
        if mask is not None:
            s = jnp.where(mask, s, NEG)
        scores.append(s)
        high = fold(jnp.maximum, s)
        if okay is not None:
            high = jnp.where(okay, high, NEG)
        top = high if top is None else jnp.maximum(top, high)
    top = jnp.max(top, -1, keepdims=True)
    total = None
    for step, (keys, okay, mask) in enumerate(pieces):
        base = top if okay is None else jnp.where(okay, top, -NEG)
        p = jnp.exp2((scores[step] - base) * scale)
        part = fold(jnp.add, p)
        total = part if total is None else total + part
        store(step, p.astype(jnp.bfloat16))
    return jnp.sum(total, -1, keepdims=True)


def probs_kernel(
    info, q_ref, ka_ref, ko_ref, kc_ref, vo_ref, vc_ref, kl_ref, kh_ref,
    far_ref, mid_ref, near_ref, l_ref, acc_ref,
):
    index = info[0]
    core = info[1]
    valid = [index >= 2, index >= 2, index >= 1, index >= 1, None, None]
    row = lax.broadcasted_iota(jnp.int32, (TILE, TILE), 0)
    col = lax.broadcasted_iota(jnp.int32, (TILE, TILE), 1)
    lane = lax.broadcasted_iota(jnp.int32, (TILE, 128), 1)
    low, high = slice(0, TILE), slice(TILE, 2 * TILE)
    l_ref[...] = jnp.ones_like(l_ref)

    def one_head(head, carry):
        columns = pl.ds(pl.multiple_of(head * HEAD, HEAD), HEAD)
        chunks = [
            ka_ref[low, columns],
            ka_ref[high, columns],
            jnp.where(core == 0, kl_ref[:, columns], ko_ref[low, columns]),
            jnp.where(core == 0, kh_ref[:, columns], ko_ref[high, columns]),
            kc_ref[low, columns],
            kc_ref[high, columns],
        ]
        for tile in range(ROWS // TILE):
            masks = [col > row, None, None, None, col <= row]
            keys = [(chunks[tile + j], valid[tile + j], masks[j]) for j in range(5)]
            rows = slice(tile * TILE, (tile + 1) * TILE)

            def store(step, p, tile=tile, rows=rows):
                chunk = tile + step
                if chunk == 0:
                    far_ref[head] = p
                elif chunk == 1:
                    mid_ref[head, rows, :] = p
                elif chunk < 4:
                    near_ref[head, rows, (chunk - 2) * TILE : (chunk - 1) * TILE] = p
                else:
                    values = vc_ref[low if chunk == 4 else high, columns]
                    part = jnp.dot(p, values, preferred_element_type=jnp.float32)
                    if chunk == 5:
                        part = part + acc_ref[rows, columns]
                    acc_ref[rows, columns] = part

            total = attend(q_ref[rows, columns], keys, store)
            l_ref[rows, :] = jnp.where(lane == head, total, l_ref[rows, :])

        @pl.when(core == 1)
        def _():
            acc_ref[:, columns] = acc_ref[:, columns] + jnp.dot(
                near_ref[head], vo_ref[:, columns], preferred_element_type=jnp.float32
            )

        return carry

    lax.fori_loop(0, LOCAL_HEADS, one_head, 0, unroll=UNROLL)


def fine_probs(info, q, ka, ks, ko, kc, vo, vc):
    whole = pl.BlockSpec(memory_space=pltpu.VMEM)
    return pl.pallas_call(
        probs_kernel,
        in_specs=[pl.BlockSpec(memory_space=pltpu.SMEM)] + [whole] * 8,
        out_specs=[whole] * 5,
        out_shape=[
            jax.ShapeDtypeStruct((LOCAL_HEADS, TILE, TILE), jnp.bfloat16),
            jax.ShapeDtypeStruct((LOCAL_HEADS, ROWS, TILE), jnp.bfloat16),
            jax.ShapeDtypeStruct((LOCAL_HEADS, ROWS, ROWS), jnp.bfloat16),
            jax.ShapeDtypeStruct((ROWS, 128), jnp.float32),
            jax.ShapeDtypeStruct((ROWS, HALF), jnp.float32),
        ],
        compiler_params=limit(20),
        cost_estimate=SMALL,
        name="fine_probs",
    )(info, q, ka, ko, kc, vo, vc, *ks)


def far_kernel(far_ref, mid_ref, acc_ref, va_ref, out_ref):
    for head in range(LOCAL_HEADS):
        columns = slice(head * HEAD, (head + 1) * HEAD)
        mixed = acc_ref[:, columns] + jnp.dot(
            mid_ref[head], va_ref[TILE : 2 * TILE, columns], preferred_element_type=jnp.float32
        )
        out_ref[0:TILE, columns] = mixed[0:TILE, :] + jnp.dot(
            far_ref[head], va_ref[0:TILE, columns], preferred_element_type=jnp.float32
        )
        out_ref[TILE : 2 * TILE, columns] = mixed[TILE : 2 * TILE, :]


def far_mix(far, mid, acc, va):
    whole = pl.BlockSpec(memory_space=pltpu.VMEM)
    return pl.pallas_call(
        far_kernel,
        in_specs=[whole] * 4,
        out_specs=whole,
        out_shape=jax.ShapeDtypeStruct((ROWS, HALF), jnp.float32),
        compiler_params=limit(16),
        cost_estimate=pl.CostEstimate(flops=1 << 30, bytes_accessed=8 * MIB, transcendentals=0),
        name="far_mix",
    )(far, mid, acc, va)


def tail_kernel(info, _, q_ref, kv_ref, ka_ref, ko_ref, kl_ref, kh_ref, pt_ref, lt_ref):
    index, core = info[0], info[1]
    r16 = lax.broadcasted_iota(jnp.int32, (SHORT, 128), 0)
    c16 = lax.broadcasted_iota(jnp.int32, (SHORT, 128), 1)
    r512 = lax.broadcasted_iota(jnp.int32, (SHORT, ROWS), 0)
    c512 = lax.broadcasted_iota(jnp.int32, (SHORT, ROWS), 1)
    blank = jnp.zeros((128 - SHORT, HALF), jnp.bfloat16)
    first = jnp.concatenate([kv_ref[0:SHORT, :], blank], 0)
    places = [0, 128, 128 + ROWS, TAIL]
    totals = jnp.zeros((SHORT, 128), jnp.float32)
    for head in range(LOCAL_HEADS):
        columns = slice(head * HEAD, (head + 1) * HEAD)
        swapped = jnp.concatenate([kl_ref[:, columns], kh_ref[:, columns]], 0)
        kb = jnp.where(core == 0, swapped, ko_ref[:, columns])
        pieces = [
            (first[:, columns], index >= 3, (c16 > r16) & (c16 < SHORT)),
            (ka_ref[:, columns], index >= 2, None),
            (kb, index >= 1, c512 <= r512 + (ROWS - SHORT)),
        ]

        def store(step, p, head=head):
            pt_ref[head, :, places[step] : places[step + 1]] = p

        total = attend(q_ref[:, columns], pieces, store)
        totals = jnp.where(c16 == head, total, totals)
    lt_ref[...] = totals


def tail_probs(info, after, q, kv, ka, ko, ks):
    whole = pl.BlockSpec(memory_space=pltpu.VMEM)
    return pl.pallas_call(
        tail_kernel,
        in_specs=[pl.BlockSpec(memory_space=pltpu.SMEM)]
        + [pl.BlockSpec(memory_space=pl.ANY)]
        + [whole] * 6,
        out_specs=[whole] * 2,
        out_shape=[
            jax.ShapeDtypeStruct((LOCAL_HEADS, SHORT, TAIL), jnp.bfloat16),
            jax.ShapeDtypeStruct((SHORT, 128), jnp.float32),
        ],
        compiler_params=limit(16),
        cost_estimate=pl.CostEstimate(flops=1 << 30, bytes_accessed=8 * MIB, transcendentals=0),
        name="tail_probs",
    )(info, after, q, kv, ka, ko, *ks)


def mix_kernel(
    info, near_ref, l_ref, acc_ref, va_ref, vs_ref, vo_ref, pt_ref, lt_ref, kv_ref, gain_ref,
    out_ref, sent_ref,
):
    core = info[1]

    def mix(with_near):
        j = lax.broadcasted_iota(jnp.int32, (CROWS, ROWS), 0)
        r = lax.broadcasted_iota(jnp.int32, (CROWS, ROWS), 1)
        pick = jnp.where((r > SHORT * j - SHORT) & (r <= SHORT * j), 1.0, 0.0)
        pick = pick.astype(jnp.bfloat16)
        j = lax.broadcasted_iota(jnp.int32, (CROWS, SHORT), 0)
        r = lax.broadcasted_iota(jnp.int32, (CROWS, SHORT), 1)
        pick_tail = jnp.where((j == 0) & (r > 0), 1.0, 0.0).astype(jnp.bfloat16)
        share = 1.0 / l_ref[...]
        some = lt_ref[...] > 0.0
        share_tail = jnp.where(some, 1.0 / jnp.where(some, lt_ref[...], 1.0), 0.0)
        blank = jnp.zeros((128 - SHORT, HALF), jnp.bfloat16)
        first = jnp.concatenate([kv_ref[SHORT : 2 * SHORT, :], blank], 0)
        squares = jnp.zeros((CROWS, HEAD), jnp.float32)
        before_ref = vs_ref if with_near else vo_ref
        for head in range(LOCAL_HEADS):
            columns = slice(head * HEAD, (head + 1) * HEAD)
            mixed = acc_ref[:, columns]
            if with_near:
                mixed = mixed + jnp.dot(
                    near_ref[head], vs_ref[:, columns], preferred_element_type=jnp.float32
                )
            out = (mixed * share[:, head : head + 1]).astype(jnp.bfloat16)
            out_ref[:, columns] = out
            tail = jnp.dot(
                pt_ref[head, :, 0:128], first[:, columns], preferred_element_type=jnp.float32
            )
            tail = tail + jnp.dot(
                pt_ref[head, :, 128 : 128 + ROWS], va_ref[:, columns],
                preferred_element_type=jnp.float32,
            )
            tail = tail + jnp.dot(
                pt_ref[head, :, 128 + ROWS : TAIL], before_ref[:, columns],
                preferred_element_type=jnp.float32,
            )
            tail = (tail * share_tail[:, head : head + 1]).astype(jnp.bfloat16)
            sums = jnp.dot(pick, out, preferred_element_type=jnp.float32)
            sums = sums + jnp.dot(pick_tail, tail, preferred_element_type=jnp.float32)
            pooled = sums * (1.0 / SHORT)
            squares = squares + pooled * pooled
            sent_ref[:, columns] = pooled * gain_ref[:, columns]
        sent_ref[:, HALF : HALF + 128] = jnp.broadcast_to(
            jnp.sum(squares, -1, keepdims=True), (CROWS, 128)
        )

    @pl.when(core == 0)
    def _():
        mix(True)

    @pl.when(core == 1)
    def _():
        mix(False)


def fine_mix(info, near, l, acc, va, vs, vo, pt, lt, kv, gain):
    whole = pl.BlockSpec(memory_space=pltpu.VMEM)
    return pl.pallas_call(
        mix_kernel,
        in_specs=[pl.BlockSpec(memory_space=pltpu.SMEM)] + [whole] * 10,
        out_specs=[whole] * 2,
        out_shape=[
            jax.ShapeDtypeStruct((ROWS, HALF), jnp.bfloat16),
            jax.ShapeDtypeStruct((CROWS, HALF + 128), jnp.float32),
        ],
        compiler_params=limit(20),
        cost_estimate=pl.CostEstimate(flops=1 << 30, bytes_accessed=8 * MIB, transcendentals=0),
        name="fine_mix",
    )(info, near, l, acc, va, vs, vo, pt, lt, kv, gain)


def norm_kernel(own_ref, other_ref, out_ref):
    squares = own_ref[:, HALF : HALF + 1] + other_ref[:, HALF : HALF + 1]
    factor = lax.rsqrt(squares / D_FINE + EPS)
    out_ref[:, 0:HALF] = (own_ref[:, 0:HALF] * factor).astype(jnp.bfloat16)
    out_ref[:, HALF : 2 * HALF] = (other_ref[:, 0:HALF] * factor).astype(jnp.bfloat16)


def normalise(own, other):
    whole = pl.BlockSpec(memory_space=pltpu.VMEM)
    return pl.pallas_call(
        norm_kernel,
        in_specs=[whole] * 2,
        out_specs=whole,
        out_shape=jax.ShapeDtypeStruct((CROWS, 2 * HALF), jnp.bfloat16),
        compiler_params=limit(4),
        cost_estimate=SMALL,
        name="normalise",
    )(own, other)


def project_kernel(info, *refs):
    row_refs, own_ref, far_refs, (kv_ref, key_ref, rows_ref, w_ref) = (
        refs[0:4], refs[4], refs[5:13], refs[13:],
    )
    c, x, y = info[1], info[2], info[3]
    for k in range(4):
        begin = pl.multiple_of((y - k + 4) % 4 * CROWS, CROWS)
        rows_ref[pl.ds(begin, CROWS), :] = row_refs[k][...]
    size = HALF // 8
    for piece in range(8):
        from_x = (x - piece // 2 + 4) % 4
        from_c = c if piece % 2 == 0 else 1 - c
        begin = pl.multiple_of((from_x * 2 + from_c) * size, size)
        w_ref[pl.ds(begin, size), :] = far_refs[piece][...]
    kv = jnp.dot(rows_ref[:, 0:HALF], own_ref[...], preferred_element_type=jnp.float32)
    kv = kv + jnp.dot(
        rows_ref[:, HALF : 2 * HALF], w_ref[...], preferred_element_type=jnp.float32
    )
    kv = kv.astype(jnp.bfloat16)
    kv_ref[...] = kv
    key_ref[...] = kv[:, 0:C_HEAD]


def project(info, rows, own, far):
    whole = pl.BlockSpec(memory_space=pltpu.VMEM)
    return pl.pallas_call(
        project_kernel,
        in_specs=[pl.BlockSpec(memory_space=pltpu.SMEM)] + [whole] * 13,
        out_specs=[whole, whole],
        out_shape=[
            jax.ShapeDtypeStruct((GROUP, 2 * C_HEAD), jnp.bfloat16),
            jax.ShapeDtypeStruct((GROUP, C_HEAD), jnp.bfloat16),
        ],
        scratch_shapes=[
            pltpu.VMEM((GROUP, 2 * HALF), jnp.bfloat16),
            pltpu.VMEM((HALF, 2 * C_HEAD), jnp.bfloat16),
        ],
        compiler_params=limit(20),
        cost_estimate=SMALL,
        name="project",
    )(info, *rows, own, *far)


def split3(value):
    first = value.astype(jnp.bfloat16).astype(jnp.float32)
    rest = value - first
    second = rest.astype(jnp.bfloat16).astype(jnp.float32)
    return first, second, rest - second


def coarse_kernel(info, *refs):
    q_refs, kv_refs, (out_ref, kv_all, q_all) = refs[0:4], refs[4:12], refs[12:]
    x, z, c = info[2], info[4], info[1]
    scale = 1.0 / math.sqrt(C_HEAD)
    keys = 8 * GROUP
    for piece in range(8):
        kv_all[piece * GROUP : (piece + 1) * GROUP, :] = kv_refs[piece][...]
    for k in range(4):
        begin = pl.multiple_of((x - k + 4) % 4 * GROUP, GROUP)
        q_all[pl.ds(begin, GROUP), :] = q_refs[k][...]
    slot = lax.broadcasted_iota(jnp.int32, (1, keys), 1)
    piece = slot // GROUP
    inside = slot % GROUP
    from_z = jnp.bitwise_xor(z, piece // 2)
    from_c = jnp.where(piece % 2 == 0, c, 1 - c)
    key_pos = (
        x * 1024 + (inside // CROWS) * 256 + from_z * 64 + from_c * 32 + inside % CROWS
    )
    place = lax.broadcasted_iota(jnp.int32, (4 * GROUP, 1), 0)
    inner = place % GROUP
    pos = (place // GROUP) * 1024 + (inner // CROWS) * 256 + z * 64 + c * 32 + inner % CROWS
    lane = lax.broadcasted_iota(jnp.int32, (4 * GROUP, 128), 1)
    allowed = key_pos < jnp.maximum(pos, 1)
    s = lax.dot_general(
        q_all[...], kv_all[:, 0:C_HEAD], (((1,), (1,)), ((), ())),
        preferred_element_type=jnp.float32,
    ) * scale
    s = jnp.where(allowed, s, NEG)
    top = jnp.max(s, -1, keepdims=True)
    p = jnp.where(allowed, jnp.exp(s - top), 0.0)
    total = jnp.sum(p, -1, keepdims=True)
    mixed = jnp.dot(
        p.astype(jnp.bfloat16), kv_all[:, C_HEAD : 2 * C_HEAD],
        preferred_element_type=jnp.float32,
    )
    some = total > 0.0
    safe = jnp.where(some, total, 1.0)
    mixed = jnp.where(some, mixed / safe, 0.0).astype(jnp.bfloat16)
    level = jnp.where(some, top + jnp.log(safe), NEG)
    a, b, d = split3(level)
    extra = jnp.where(lane == 0, a, jnp.where(lane == 1, b, jnp.where(lane == 2, d, 0.0)))
    extra = extra.astype(jnp.bfloat16)
    for piece in range(16):
        rows = slice(piece * CROWS, (piece + 1) * CROWS)
        out_ref[piece, :, 0:C_HEAD] = mixed[rows, :]
        out_ref[piece, :, C_HEAD : C_HEAD + 128] = extra[rows, :]


def coarse_attend(info, queries, pairs):
    whole = pl.BlockSpec(memory_space=pltpu.VMEM)
    return pl.pallas_call(
        coarse_kernel,
        grid=(1,),
        in_specs=[pl.BlockSpec(memory_space=pltpu.SMEM)]
        + [pl.BlockSpec((GROUP, C_HEAD), lambda i: (0, 0))]
        + [whole] * 3
        + [pl.BlockSpec((GROUP, 2 * C_HEAD), lambda i: (0, 0))]
        + [whole] * 7,
        out_specs=whole,
        out_shape=jax.ShapeDtypeStruct((16, CROWS, C_HEAD + 128), jnp.bfloat16),
        scratch_shapes=[
            pltpu.VMEM((8 * GROUP, 2 * C_HEAD), jnp.bfloat16),
            pltpu.VMEM((4 * GROUP, C_HEAD), jnp.bfloat16),
        ],
        compiler_params=limit(16),
        cost_estimate=pl.CostEstimate(
            flops=4 * 4 * GROUP * 8 * GROUP * C_HEAD,
            bytes_accessed=2 * MIB,
            transcendentals=4 * GROUP * 8 * GROUP,
        ),
        name="coarse_attend",
    )(info, *queries, *pairs)


def final_kernel(part_ref, fine_ref, out_ref, done_ref, sems):
    r = lax.broadcasted_iota(jnp.int32, (ROWS, CROWS), 0)
    j = lax.broadcasted_iota(jnp.int32, (ROWS, CROWS), 1)
    spread = jnp.where(r // SHORT == j, 1.0, 0.0).astype(jnp.bfloat16)
    coarse = []
    for head in range(4):
        parts = jnp.stack([part_ref[4 * i + head] for i in range(4)]).astype(jnp.float32)
        levels = jnp.sum(parts[:, :, C_HEAD : C_HEAD + 128], -1, keepdims=True)
        top = jnp.max(levels, 0, keepdims=True)
        weights = jnp.exp(levels - top)
        total = jnp.sum(weights, 0)
        mixed = jnp.sum(parts[:, :, 0:C_HEAD] * weights, 0) / total
        coarse.append(mixed.astype(jnp.bfloat16))
    coarse = jnp.concatenate(coarse, 1)
    stores = []
    for block in range(4):
        rows = slice(block * 128, (block + 1) * 128)
        up = jnp.dot(spread[rows, :], coarse, preferred_element_type=jnp.float32)
        done_ref[rows, :] = (fine_ref[rows, :].astype(jnp.float32) + up).astype(jnp.bfloat16)
        store = pltpu.make_async_copy(
            done_ref.at[pl.ds(block * 128, 128), :],
            out_ref.at[pl.ds(block * 128, 128), :],
            sems.at[block],
        )
        store.start()
        stores.append(store)
    for store in stores:
        store.wait()


def finish(parts, fine):
    whole = pl.BlockSpec(memory_space=pltpu.VMEM)
    return pl.pallas_call(
        final_kernel,
        in_specs=[whole] * 2,
        out_specs=pl.BlockSpec(memory_space=pl.ANY),
        out_shape=jax.ShapeDtypeStruct((ROWS, HALF), jnp.bfloat16),
        scratch_shapes=[
            pltpu.VMEM((ROWS, HALF), jnp.bfloat16),
            pltpu.SemaphoreType.DMA((4,)),
        ],
        compiler_params=limit(16),
        name="finish",
    )(parts, fine)


def per_device(fine_q, fine_k, fine_v, norm_gain, short_weight):
    x, y, z, c, m = (lax.axis_index(a) for a in CTX + ("m",))
    index = ((x * 4 + y) * 4 + z) * 2 + c
    info = jnp.stack([index, c, x, y, z, m]).astype(jnp.int32)

    k2 = shifted(fine_k, 2)
    v2 = shifted(fine_v, 2)
    ko = rolled(fine_k, "c", 1)
    vo = rolled(fine_v, "c", 1)
    part, own_columns, last_q, last_kv = pick_columns(
        info, short_weight, fine_q, fine_k, fine_v
    )
    k2 = lax.optimization_barrier((k2, last_q))[0]
    tail_q = shifted(last_q, 1)
    tail_kv = shifted(last_kv, 3)
    part = rolled(part, "m", 1)
    ks = [rolled(piece, "c", 1) for piece in halves(k2)]
    far, mid, near, l, acc = fine_probs(info, fine_q, k2, ks, ko, fine_k, vo, fine_v)
    v2, l, tail_q, tail_kv = lax.optimization_barrier((v2, l, tail_q, tail_kv))
    vs = rolled(v2, "c", 1)
    acc = far_mix(far, mid, acc, v2)
    pt, lt = tail_probs(info, v2, tail_q, tail_kv, k2, ko, ks)
    fine_out, pooled = fine_mix(
        info, near, l, acc, v2, vs, vo, pt, lt, tail_kv, norm_gain[None]
    )

    part, pooled = lax.optimization_barrier((part, pooled))
    eighths = [part] + [rolled(part, "x", k) for k in (1, 2, 3)]

    other = rolled(pooled, "m", 1)
    normed = normalise(pooled, other)
    normed, *eighths = lax.optimization_barrier((normed, *eighths))
    columns = []
    for piece in eighths:
        columns += [piece, rolled(piece, "c", 1)]
    rows = [normed] + [rolled(normed, "y", k) for k in (1, 2, 3)]
    kv, own_keys = project(info, rows, own_columns, columns)

    queries = [own_keys] + [rolled(own_keys, "x", k) for k in (1, 2, 3)]
    far = paired(kv, "z", 2)
    pieces = [kv, paired(kv, "z", 1), far]
    held = lax.optimization_barrier((*queries, *pieces))
    queries = held[:4]
    pairs = []
    for piece in held[4:] + (paired(held[6], "z", 1),):
        pairs += [piece, rolled(piece, "c", 1)]
    parts = coarse_attend(info, queries, pairs)
    parts = lax.all_to_all(parts, ("x", "y"), split_axis=0, concat_axis=0, tiled=True)
    return finish(parts, fine_out)


def solution(mesh):
    grid = Mesh(mesh.devices.reshape(4, 4, 4, 2, 2), ("x", "y", "z", "c", "m"))
    rows = P(CTX, "m")
    return jax.shard_map(
        per_device,
        mesh=grid,
        in_specs=(rows, rows, rows, P("m"), P("m", None)),
        out_specs=rows,
        check_vma=False,
    )
```

```python
import functools
import math

import jax
import jax.numpy as jnp
from jax import lax
from jax.experimental import pallas as pl
from jax.experimental.pallas import tpu as pltpu
from jax.sharding import Mesh
from jax.sharding import PartitionSpec as P

D_FINE = 2048
HEADS = 16
HEAD = 128
C_HEADS = 8
C_HEAD = 256
WINDOW = 1024
SHORT = 16
EPS = 1e-05
NEG = -1e30
LOG2E = 1.4426950408889634

ROWS = 512
HALF = 1024
LOCAL_HEADS = HALF // HEAD
TILE = 256
CROWS = ROWS // SHORT
UNROLL = 1
TAIL = 128 + 2 * ROWS
GROUP = 4 * CROWS
SMALL = pl.CostEstimate(flops=1, bytes_accessed=1, transcendentals=0)
CTX = ("x", "y", "z", "c")
MIB = 1 << 20


def shifted(value, steps):
    count = 128
    return lax.ppermute(
        value, CTX, [(s, s + steps) for s in range(max(0, -steps), min(count, count - steps))]
    )


def rolled(value, axis, steps):
    count = lax.axis_size(axis)
    return lax.ppermute(value, axis, [(s, (s + steps) % count) for s in range(count)])


def paired(value, axis, distance):
    count = lax.axis_size(axis)
    return lax.ppermute(value, axis, [(s, s ^ distance) for s in range(count)])


def limit(mib):
    return pltpu.CompilerParams(vmem_limit_bytes=mib * MIB)


def halves_kernel(in_ref, low_ref, high_ref):
    low_ref[...] = in_ref[0:TILE, :]
    high_ref[...] = in_ref[TILE : 2 * TILE, :]


def halves(value):
    half = pl.BlockSpec((TILE, 512), lambda i: (0, i))
    return pl.pallas_call(
        halves_kernel,
        grid=(2,),
        in_specs=[pl.BlockSpec((ROWS, 512), lambda i: (0, i))],
        out_specs=[half] * 2,
        out_shape=[jax.ShapeDtypeStruct((TILE, HALF), jnp.bfloat16)] * 2,
        compiler_params=limit(8),
        cost_estimate=SMALL,
        name="halves",
    )(value)


def pick_kernel(
    info, part_ref, own_ref, q_ref, k_ref, v_ref, part_out, own_out, q_out, kv_out
):
    part_out[...] = part_ref[...]
    own_out[...] = own_ref[...]
    q_out[...] = q_ref[...]
    kv_out[0:SHORT, :] = k_ref[...]
    kv_out[SHORT : 2 * SHORT, :] = v_ref[...]


def pick_columns(info, weight, q, k, v):
    wide = 2 * C_HEAD
    size = HALF // 8
    part = pl.BlockSpec(
        (size, wide), lambda i, info: (info[2] * 2 + info[1], (1 - info[5]) * 4 + info[3])
    )
    own = pl.BlockSpec((HALF // 4, wide), lambda i, info: (i, info[5] * 4 + info[3]))
    end = pl.BlockSpec((SHORT, HALF), lambda i, info: (ROWS // SHORT - 1, 0))
    first = lambda rows, columns: pl.BlockSpec((rows, columns), lambda i, info: (0, 0))
    return pl.pallas_call(
        pick_kernel,
        grid_spec=pltpu.PrefetchScalarGridSpec(
            num_scalar_prefetch=1,
            grid=(4,),
            in_specs=[part, own, end, end, end],
            out_specs=[
                first(size, wide),
                pl.BlockSpec((HALF // 4, wide), lambda i, info: (i, 0)),
                first(SHORT, HALF),
                first(2 * SHORT, HALF),
            ],
        ),
        out_shape=[
            jax.ShapeDtypeStruct((size, wide), jnp.bfloat16),
            jax.ShapeDtypeStruct((HALF, wide), jnp.bfloat16),
            jax.ShapeDtypeStruct((SHORT, HALF), jnp.bfloat16),
            jax.ShapeDtypeStruct((2 * SHORT, HALF), jnp.bfloat16),
        ],
        compiler_params=limit(8),
        cost_estimate=pl.CostEstimate(flops=1 << 30, bytes_accessed=2 * MIB, transcendentals=0),
        name="pick_columns",
    )(info, weight, weight, q, k, v)


def attend(q, pieces, store):
    scale = LOG2E / math.sqrt(HEAD)

    def fold(combine, value):
        lanes = value[:, 0:128]
        for i in range(1, value.shape[1] // 128):
            lanes = combine(lanes, value[:, i * 128 : (i + 1) * 128])
        return lanes

    scores = []
    top = None
    for keys, okay, mask in pieces:
        s = lax.dot_general(
            q, keys, (((1,), (1,)), ((), ())), preferred_element_type=jnp.float32
        )
        if mask is not None:
            s = jnp.where(mask, s, NEG)
        scores.append(s)
        high = fold(jnp.maximum, s)
        if okay is not None:
            high = jnp.where(okay, high, NEG)
        top = high if top is None else jnp.maximum(top, high)
    top = jnp.max(top, -1, keepdims=True)
    total = None
    for step, (keys, okay, mask) in enumerate(pieces):
        base = top if okay is None else jnp.where(okay, top, -NEG)
        p = jnp.exp2((scores[step] - base) * scale)
        part = fold(jnp.add, p)
        total = part if total is None else total + part
        store(step, p.astype(jnp.bfloat16))
    return jnp.sum(total, -1, keepdims=True)


def probs_kernel(
    info, q_ref, ka_ref, ko_ref, kc_ref, vo_ref, vc_ref, kl_ref, kh_ref,
    far_ref, mid_ref, near_ref, l_ref, acc_ref,
):
    index = info[0]
    core = info[1]
    valid = [index >= 2, index >= 2, index >= 1, index >= 1, None, None]
    row = lax.broadcasted_iota(jnp.int32, (TILE, TILE), 0)
    col = lax.broadcasted_iota(jnp.int32, (TILE, TILE), 1)
    lane = lax.broadcasted_iota(jnp.int32, (TILE, 128), 1)
    low, high = slice(0, TILE), slice(TILE, 2 * TILE)
    l_ref[...] = jnp.ones_like(l_ref)

    def one_head(head, carry):
        columns = pl.ds(pl.multiple_of(head * HEAD, HEAD), HEAD)
        chunks = [
            ka_ref[low, columns],
            ka_ref[high, columns],
            jnp.where(core == 0, kl_ref[:, columns], ko_ref[low, columns]),
            jnp.where(core == 0, kh_ref[:, columns], ko_ref[high, columns]),
            kc_ref[low, columns],
            kc_ref[high, columns],
        ]
        for tile in range(ROWS // TILE):
            masks = [col > row, None, None, None, col <= row]
            keys = [(chunks[tile + j], valid[tile + j], masks[j]) for j in range(5)]
            rows = slice(tile * TILE, (tile + 1) * TILE)

            def store(step, p, tile=tile, rows=rows):
                chunk = tile + step
                if chunk == 0:
                    far_ref[head] = p
                elif chunk == 1:
                    mid_ref[head, rows, :] = p
                elif chunk < 4:
                    near_ref[head, rows, (chunk - 2) * TILE : (chunk - 1) * TILE] = p
                else:
                    values = vc_ref[low if chunk == 4 else high, columns]
                    part = jnp.dot(p, values, preferred_element_type=jnp.float32)
                    if chunk == 5:
                        part = part + acc_ref[rows, columns]
                    acc_ref[rows, columns] = part

            total = attend(q_ref[rows, columns], keys, store)
            l_ref[rows, :] = jnp.where(lane == head, total, l_ref[rows, :])

        @pl.when(core == 1)
        def _():
            acc_ref[:, columns] = acc_ref[:, columns] + jnp.dot(
                near_ref[head], vo_ref[:, columns], preferred_element_type=jnp.float32
            )

        return carry

    lax.fori_loop(0, LOCAL_HEADS, one_head, 0, unroll=UNROLL)


def fine_probs(info, q, ka, ks, ko, kc, vo, vc):
    whole = pl.BlockSpec(memory_space=pltpu.VMEM)
    return pl.pallas_call(
        probs_kernel,
        in_specs=[pl.BlockSpec(memory_space=pltpu.SMEM)] + [whole] * 8,
        out_specs=[whole] * 5,
        out_shape=[
            jax.ShapeDtypeStruct((LOCAL_HEADS, TILE, TILE), jnp.bfloat16),
            jax.ShapeDtypeStruct((LOCAL_HEADS, ROWS, TILE), jnp.bfloat16),
            jax.ShapeDtypeStruct((LOCAL_HEADS, ROWS, ROWS), jnp.bfloat16),
            jax.ShapeDtypeStruct((ROWS, 128), jnp.float32),
            jax.ShapeDtypeStruct((ROWS, HALF), jnp.float32),
        ],
        compiler_params=limit(20),
        cost_estimate=SMALL,
        name="fine_probs",
    )(info, q, ka, ko, kc, vo, vc, *ks)


def far_kernel(far_ref, mid_ref, acc_ref, va_ref, out_ref):
    for head in range(LOCAL_HEADS):
        columns = slice(head * HEAD, (head + 1) * HEAD)
        mixed = acc_ref[:, columns] + jnp.dot(
            mid_ref[head], va_ref[TILE : 2 * TILE, columns], preferred_element_type=jnp.float32
        )
        out_ref[0:TILE, columns] = mixed[0:TILE, :] + jnp.dot(
            far_ref[head], va_ref[0:TILE, columns], preferred_element_type=jnp.float32
        )
        out_ref[TILE : 2 * TILE, columns] = mixed[TILE : 2 * TILE, :]


def far_mix(far, mid, acc, va):
    whole = pl.BlockSpec(memory_space=pltpu.VMEM)
    return pl.pallas_call(
        far_kernel,
        in_specs=[whole] * 4,
        out_specs=whole,
        out_shape=jax.ShapeDtypeStruct((ROWS, HALF), jnp.float32),
        compiler_params=limit(16),
        cost_estimate=pl.CostEstimate(flops=1 << 30, bytes_accessed=8 * MIB, transcendentals=0),
        name="far_mix",
    )(far, mid, acc, va)


def tail_kernel(info, _, q_ref, kv_ref, ka_ref, ko_ref, kl_ref, kh_ref, pt_ref, lt_ref):
    index, core = info[0], info[1]
    r16 = lax.broadcasted_iota(jnp.int32, (SHORT, 128), 0)
    c16 = lax.broadcasted_iota(jnp.int32, (SHORT, 128), 1)
    r512 = lax.broadcasted_iota(jnp.int32, (SHORT, ROWS), 0)
    c512 = lax.broadcasted_iota(jnp.int32, (SHORT, ROWS), 1)
    blank = jnp.zeros((128 - SHORT, HALF), jnp.bfloat16)
    first = jnp.concatenate([kv_ref[0:SHORT, :], blank], 0)
    places = [0, 128, 128 + ROWS, TAIL]
    totals = jnp.zeros((SHORT, 128), jnp.float32)
    for head in range(LOCAL_HEADS):
        columns = slice(head * HEAD, (head + 1) * HEAD)
        swapped = jnp.concatenate([kl_ref[:, columns], kh_ref[:, columns]], 0)
        kb = jnp.where(core == 0, swapped, ko_ref[:, columns])
        pieces = [
            (first[:, columns], index >= 3, (c16 > r16) & (c16 < SHORT)),
            (ka_ref[:, columns], index >= 2, None),
            (kb, index >= 1, c512 <= r512 + (ROWS - SHORT)),
        ]

        def store(step, p, head=head):
            pt_ref[head, :, places[step] : places[step + 1]] = p

        total = attend(q_ref[:, columns], pieces, store)
        totals = jnp.where(c16 == head, total, totals)
    lt_ref[...] = totals


def tail_probs(info, after, q, kv, ka, ko, ks):
    whole = pl.BlockSpec(memory_space=pltpu.VMEM)
    return pl.pallas_call(
        tail_kernel,
        in_specs=[pl.BlockSpec(memory_space=pltpu.SMEM)]
        + [pl.BlockSpec(memory_space=pl.ANY)]
        + [whole] * 6,
        out_specs=[whole] * 2,
        out_shape=[
            jax.ShapeDtypeStruct((LOCAL_HEADS, SHORT, TAIL), jnp.bfloat16),
            jax.ShapeDtypeStruct((SHORT, 128), jnp.float32),
        ],
        compiler_params=limit(16),
        cost_estimate=pl.CostEstimate(flops=1 << 30, bytes_accessed=8 * MIB, transcendentals=0),
        name="tail_probs",
    )(info, after, q, kv, ka, ko, *ks)


def mix_kernel(
    info, near_ref, l_ref, acc_ref, va_ref, vs_ref, vo_ref, pt_ref, lt_ref, kv_ref, gain_ref,
    out_ref, sent_ref,
):
    core = info[1]

    def mix(with_near):
        j = lax.broadcasted_iota(jnp.int32, (CROWS, ROWS), 0)
        r = lax.broadcasted_iota(jnp.int32, (CROWS, ROWS), 1)
        pick = jnp.where((r > SHORT * j - SHORT) & (r <= SHORT * j), 1.0, 0.0)
        pick = pick.astype(jnp.bfloat16)
        j = lax.broadcasted_iota(jnp.int32, (CROWS, SHORT), 0)
        r = lax.broadcasted_iota(jnp.int32, (CROWS, SHORT), 1)
        pick_tail = jnp.where((j == 0) & (r > 0), 1.0, 0.0).astype(jnp.bfloat16)
        share = 1.0 / l_ref[...]
        some = lt_ref[...] > 0.0
        share_tail = jnp.where(some, 1.0 / jnp.where(some, lt_ref[...], 1.0), 0.0)
        blank = jnp.zeros((128 - SHORT, HALF), jnp.bfloat16)
        first = jnp.concatenate([kv_ref[SHORT : 2 * SHORT, :], blank], 0)
        squares = jnp.zeros((CROWS, HEAD), jnp.float32)
        before_ref = vs_ref if with_near else vo_ref
        for head in range(LOCAL_HEADS):
            columns = slice(head * HEAD, (head + 1) * HEAD)
            mixed = acc_ref[:, columns]
            if with_near:
                mixed = mixed + jnp.dot(
                    near_ref[head], vs_ref[:, columns], preferred_element_type=jnp.float32
                )
            out = (mixed * share[:, head : head + 1]).astype(jnp.bfloat16)
            out_ref[:, columns] = out
            tail = jnp.dot(
                pt_ref[head, :, 0:128], first[:, columns], preferred_element_type=jnp.float32
            )
            tail = tail + jnp.dot(
                pt_ref[head, :, 128 : 128 + ROWS], va_ref[:, columns],
                preferred_element_type=jnp.float32,
            )
            tail = tail + jnp.dot(
                pt_ref[head, :, 128 + ROWS : TAIL], before_ref[:, columns],
                preferred_element_type=jnp.float32,
            )
            tail = (tail * share_tail[:, head : head + 1]).astype(jnp.bfloat16)
            sums = jnp.dot(pick, out, preferred_element_type=jnp.float32)
            sums = sums + jnp.dot(pick_tail, tail, preferred_element_type=jnp.float32)
            pooled = sums * (1.0 / SHORT)
            squares = squares + pooled * pooled
            sent_ref[:, columns] = pooled * gain_ref[:, columns]
        sent_ref[:, HALF : HALF + 128] = jnp.broadcast_to(
            jnp.sum(squares, -1, keepdims=True), (CROWS, 128)
        )

    @pl.when(core == 0)
    def _():
        mix(True)

    @pl.when(core == 1)
    def _():
        mix(False)


def fine_mix(info, near, l, acc, va, vs, vo, pt, lt, kv, gain):
    whole = pl.BlockSpec(memory_space=pltpu.VMEM)
    return pl.pallas_call(
        mix_kernel,
        in_specs=[pl.BlockSpec(memory_space=pltpu.SMEM)] + [whole] * 10,
        out_specs=[whole] * 2,
        out_shape=[
            jax.ShapeDtypeStruct((ROWS, HALF), jnp.bfloat16),
            jax.ShapeDtypeStruct((CROWS, HALF + 128), jnp.float32),
        ],
        compiler_params=limit(20),
        cost_estimate=pl.CostEstimate(flops=1 << 30, bytes_accessed=8 * MIB, transcendentals=0),
        name="fine_mix",
    )(info, near, l, acc, va, vs, vo, pt, lt, kv, gain)


def norm_kernel(own_ref, other_ref, out_ref):
    squares = own_ref[:, HALF : HALF + 1] + other_ref[:, HALF : HALF + 1]
    factor = lax.rsqrt(squares / D_FINE + EPS)
    out_ref[:, 0:HALF] = (own_ref[:, 0:HALF] * factor).astype(jnp.bfloat16)
    out_ref[:, HALF : 2 * HALF] = (other_ref[:, 0:HALF] * factor).astype(jnp.bfloat16)


def carry_kernel(_, in_ref, out_ref):
    out_ref[...] = in_ref[...]


def carried(value, after):
    whole = pl.BlockSpec(memory_space=pltpu.VMEM)
    return pl.pallas_call(
        carry_kernel,
        in_specs=[pl.BlockSpec(memory_space=pl.ANY), whole],
        out_specs=whole,
        out_shape=jax.ShapeDtypeStruct(value.shape, value.dtype),
        compiler_params=limit(4),
        cost_estimate=pl.CostEstimate(
            flops=1 << 34, bytes_accessed=32 * MIB, transcendentals=0
        ),
        name="carried",
    )(after, value)


def normalise(own, other):
    whole = pl.BlockSpec(memory_space=pltpu.VMEM)
    return pl.pallas_call(
        norm_kernel,
        in_specs=[whole] * 2,
        out_specs=whole,
        out_shape=jax.ShapeDtypeStruct((CROWS, 2 * HALF), jnp.bfloat16),
        compiler_params=limit(4),
        cost_estimate=SMALL,
        name="normalise",
    )(own, other)


def project_kernel(info, *refs):
    row_refs, own_ref, far_refs, (kv_ref, key_ref, rows_ref, w_ref) = (
        refs[0:4], refs[4], refs[5:13], refs[13:],
    )
    c, x, y = info[1], info[2], info[3]
    for k in range(4):
        begin = pl.multiple_of((y - k + 4) % 4 * CROWS, CROWS)
        rows_ref[pl.ds(begin, CROWS), :] = row_refs[k][...]
    size = HALF // 8
    for piece in range(8):
        from_x = (x - piece // 2 + 4) % 4
        from_c = c if piece % 2 == 0 else 1 - c
        begin = pl.multiple_of((from_x * 2 + from_c) * size, size)
        w_ref[pl.ds(begin, size), :] = far_refs[piece][...]
    kv = jnp.dot(rows_ref[:, 0:HALF], own_ref[...], preferred_element_type=jnp.float32)
    kv = kv + jnp.dot(
        rows_ref[:, HALF : 2 * HALF], w_ref[...], preferred_element_type=jnp.float32
    )
    kv = kv.astype(jnp.bfloat16)
    kv_ref[...] = kv
    key_ref[...] = kv[:, 0:C_HEAD]


def project(info, rows, own, far):
    whole = pl.BlockSpec(memory_space=pltpu.VMEM)
    return pl.pallas_call(
        project_kernel,
        in_specs=[pl.BlockSpec(memory_space=pltpu.SMEM)] + [whole] * 13,
        out_specs=[whole, whole],
        out_shape=[
            jax.ShapeDtypeStruct((GROUP, 2 * C_HEAD), jnp.bfloat16),
            jax.ShapeDtypeStruct((GROUP, C_HEAD), jnp.bfloat16),
        ],
        scratch_shapes=[
            pltpu.VMEM((GROUP, 2 * HALF), jnp.bfloat16),
            pltpu.VMEM((HALF, 2 * C_HEAD), jnp.bfloat16),
        ],
        compiler_params=limit(20),
        cost_estimate=SMALL,
        name="project",
    )(info, *rows, own, *far)


def split3(value):
    first = value.astype(jnp.bfloat16).astype(jnp.float32)
    rest = value - first
    second = rest.astype(jnp.bfloat16).astype(jnp.float32)
    return first, second, rest - second


def coarse_kernel(info, *refs):
    q_refs, kv_refs, (out_ref, kv_all, q_all) = refs[0:4], refs[4:12], refs[12:]
    x, z, c = info[2], info[4], info[1]
    scale = 1.0 / math.sqrt(C_HEAD)
    keys = 8 * GROUP
    for piece in range(8):
        kv_all[piece * GROUP : (piece + 1) * GROUP, :] = kv_refs[piece][...]
    for k in range(4):
        begin = pl.multiple_of((x - k + 4) % 4 * GROUP, GROUP)
        q_all[pl.ds(begin, GROUP), :] = q_refs[k][...]
    slot = lax.broadcasted_iota(jnp.int32, (1, keys), 1)
    piece = slot // GROUP
    inside = slot % GROUP
    from_z = jnp.bitwise_xor(z, piece // 2)
    from_c = jnp.where(piece % 2 == 0, c, 1 - c)
    key_pos = (
        x * 1024 + (inside // CROWS) * 256 + from_z * 64 + from_c * 32 + inside % CROWS
    )
    place = lax.broadcasted_iota(jnp.int32, (4 * GROUP, 1), 0)
    inner = place % GROUP
    pos = (place // GROUP) * 1024 + (inner // CROWS) * 256 + z * 64 + c * 32 + inner % CROWS
    lane = lax.broadcasted_iota(jnp.int32, (4 * GROUP, 128), 1)
    allowed = key_pos < jnp.maximum(pos, 1)
    s = lax.dot_general(
        q_all[...], kv_all[:, 0:C_HEAD], (((1,), (1,)), ((), ())),
        preferred_element_type=jnp.float32,
    ) * scale
    s = jnp.where(allowed, s, NEG)
    top = jnp.max(s, -1, keepdims=True)
    p = jnp.where(allowed, jnp.exp(s - top), 0.0)
    total = jnp.sum(p, -1, keepdims=True)
    mixed = jnp.dot(
        p.astype(jnp.bfloat16), kv_all[:, C_HEAD : 2 * C_HEAD],
        preferred_element_type=jnp.float32,
    )
    some = total > 0.0
    safe = jnp.where(some, total, 1.0)
    mixed = jnp.where(some, mixed / safe, 0.0).astype(jnp.bfloat16)
    level = jnp.where(some, top + jnp.log(safe), NEG)
    a, b, d = split3(level)
    extra = jnp.where(lane == 0, a, jnp.where(lane == 1, b, jnp.where(lane == 2, d, 0.0)))
    extra = extra.astype(jnp.bfloat16)
    for piece in range(16):
        rows = slice(piece * CROWS, (piece + 1) * CROWS)
        out_ref[piece, :, 0:C_HEAD] = mixed[rows, :]
        out_ref[piece, :, C_HEAD : C_HEAD + 128] = extra[rows, :]


def coarse_attend(info, queries, pairs):
    whole = pl.BlockSpec(memory_space=pltpu.VMEM)
    return pl.pallas_call(
        coarse_kernel,
        grid=(1,),
        in_specs=[pl.BlockSpec(memory_space=pltpu.SMEM)]
        + [pl.BlockSpec((GROUP, C_HEAD), lambda i: (0, 0))]
        + [whole] * 3
        + [pl.BlockSpec((GROUP, 2 * C_HEAD), lambda i: (0, 0))]
        + [whole] * 7,
        out_specs=whole,
        out_shape=jax.ShapeDtypeStruct((16, CROWS, C_HEAD + 128), jnp.bfloat16),
        scratch_shapes=[
            pltpu.VMEM((8 * GROUP, 2 * C_HEAD), jnp.bfloat16),
            pltpu.VMEM((4 * GROUP, C_HEAD), jnp.bfloat16),
        ],
        compiler_params=limit(16),
        cost_estimate=pl.CostEstimate(
            flops=4 * 4 * GROUP * 8 * GROUP * C_HEAD,
            bytes_accessed=2 * MIB,
            transcendentals=4 * GROUP * 8 * GROUP,
        ),
        name="coarse_attend",
    )(info, *queries, *pairs)


def final_kernel(part_ref, fine_ref, out_ref, done_ref, sems):
    r = lax.broadcasted_iota(jnp.int32, (ROWS, CROWS), 0)
    j = lax.broadcasted_iota(jnp.int32, (ROWS, CROWS), 1)
    spread = jnp.where(r // SHORT == j, 1.0, 0.0).astype(jnp.bfloat16)
    coarse = []
    for head in range(4):
        parts = jnp.stack([part_ref[4 * i + head] for i in range(4)]).astype(jnp.float32)
        levels = jnp.sum(parts[:, :, C_HEAD : C_HEAD + 128], -1, keepdims=True)
        top = jnp.max(levels, 0, keepdims=True)
        weights = jnp.exp(levels - top)
        total = jnp.sum(weights, 0)
        mixed = jnp.sum(parts[:, :, 0:C_HEAD] * weights, 0) / total
        coarse.append(mixed.astype(jnp.bfloat16))
    coarse = jnp.concatenate(coarse, 1)
    stores = []
    for block in range(4):
        rows = slice(block * 128, (block + 1) * 128)
        up = jnp.dot(spread[rows, :], coarse, preferred_element_type=jnp.float32)
        done_ref[rows, :] = (fine_ref[rows, :].astype(jnp.float32) + up).astype(jnp.bfloat16)
        store = pltpu.make_async_copy(
            done_ref.at[pl.ds(block * 128, 128), :],
            out_ref.at[pl.ds(block * 128, 128), :],
            sems.at[block],
        )
        store.start()
        stores.append(store)
    for store in stores:
        store.wait()


def finish(parts, fine):
    whole = pl.BlockSpec(memory_space=pltpu.VMEM)
    return pl.pallas_call(
        final_kernel,
        in_specs=[whole] * 2,
        out_specs=pl.BlockSpec(memory_space=pl.ANY),
        out_shape=jax.ShapeDtypeStruct((ROWS, HALF), jnp.bfloat16),
        scratch_shapes=[
            pltpu.VMEM((ROWS, HALF), jnp.bfloat16),
            pltpu.SemaphoreType.DMA((4,)),
        ],
        compiler_params=limit(16),
        name="finish",
    )(parts, fine)


def per_device(fine_q, fine_k, fine_v, norm_gain, short_weight):
    x, y, z, c, m = (lax.axis_index(a) for a in CTX + ("m",))
    index = ((x * 4 + y) * 4 + z) * 2 + c
    info = jnp.stack([index, c, x, y, z, m]).astype(jnp.int32)

    k2 = shifted(fine_k, 2)
    v2 = shifted(fine_v, 2)
    ko = rolled(fine_k, "c", 1)
    vo = rolled(fine_v, "c", 1)
    part, own_columns, last_q, last_kv = pick_columns(
        info, short_weight, fine_q, fine_k, fine_v
    )
    k2 = lax.optimization_barrier((k2, last_q))[0]
    tail_q = shifted(last_q, 1)
    tail_kv = shifted(last_kv, 3)
    part = rolled(part, "m", 1)
    ks = [rolled(piece, "c", 1) for piece in halves(k2)]
    far, mid, near, l, acc = fine_probs(info, fine_q, k2, ks, ko, fine_k, vo, fine_v)
    v2, l, tail_q, tail_kv = lax.optimization_barrier((v2, l, tail_q, tail_kv))
    vs = rolled(v2, "c", 1)
    acc = far_mix(far, mid, acc, v2)
    pt, lt = tail_probs(info, v2, tail_q, tail_kv, k2, ko, ks)
    fine_out, pooled = fine_mix(
        info, near, l, acc, v2, vs, vo, pt, lt, tail_kv, norm_gain[None]
    )

    part = carried(part, pooled)
    eighths = [part] + [rolled(part, "x", k) for k in (1, 2, 3)]

    other = rolled(pooled, "m", 1)
    normed = normalise(pooled, other)
    rows = [normed] + [rolled(normed, "y", k) for k in (1, 2, 3)]
    eighths = lax.optimization_barrier((*eighths, rows[1]))[:4]
    columns = []
    for piece in eighths:
        columns += [piece, rolled(piece, "c", 1)]
    kv, own_keys = project(info, rows, own_columns, columns)

    queries = [own_keys] + [rolled(own_keys, "x", k) for k in (1, 2, 3)]
    far = paired(kv, "z", 2)
    pieces = [kv, paired(kv, "z", 1), far]
    held = lax.optimization_barrier((*queries, *pieces))
    queries = held[:4]
    pairs = []
    for piece in held[4:] + (paired(held[6], "z", 1),):
        pairs += [piece, rolled(piece, "c", 1)]
    parts = coarse_attend(info, queries, pairs)
    parts = lax.all_to_all(parts, ("x", "y"), split_axis=0, concat_axis=0, tiled=True)
    return finish(parts, fine_out)


def solution(mesh):
    grid = Mesh(mesh.devices.reshape(4, 4, 4, 2, 2), ("x", "y", "z", "c", "m"))
    rows = P(CTX, "m")
    return jax.shard_map(
        per_device,
        mesh=grid,
        in_specs=(rows, rows, rows, P("m"), P("m", None)),
        out_specs=rows,
        check_vma=False,
    )
```

```python
import functools
import math

import jax
import jax.numpy as jnp
from jax import lax
from jax.experimental import pallas as pl
from jax.experimental.pallas import tpu as pltpu
from jax.sharding import Mesh
from jax.sharding import PartitionSpec as P

D_FINE = 2048
HEADS = 16
HEAD = 128
C_HEADS = 8
C_HEAD = 256
WINDOW = 1024
SHORT = 16
EPS = 1e-05
NEG = -1e30
LOG2E = 1.4426950408889634

ROWS = 512
HALF = 1024
LOCAL_HEADS = HALF // HEAD
TILE = 256
CROWS = ROWS // SHORT
UNROLL = 1
TAIL = 128 + 2 * ROWS
GROUP = 4 * CROWS
SMALL = pl.CostEstimate(flops=1, bytes_accessed=1, transcendentals=0)
CTX = ("x", "y", "z", "c")
MIB = 1 << 20


def shifted(value, steps):
    count = 128
    return lax.ppermute(
        value, CTX, [(s, s + steps) for s in range(max(0, -steps), min(count, count - steps))]
    )


def rolled(value, axis, steps):
    count = lax.axis_size(axis)
    return lax.ppermute(value, axis, [(s, (s + steps) % count) for s in range(count)])


def paired(value, axis, distance):
    count = lax.axis_size(axis)
    return lax.ppermute(value, axis, [(s, s ^ distance) for s in range(count)])


def limit(mib):
    return pltpu.CompilerParams(vmem_limit_bytes=mib * MIB)


def halves_kernel(in_ref, low_ref, high_ref):
    low_ref[...] = in_ref[0:TILE, :]
    high_ref[...] = in_ref[TILE : 2 * TILE, :]


def halves(value):
    half = pl.BlockSpec((TILE, 512), lambda i: (0, i))
    return pl.pallas_call(
        halves_kernel,
        grid=(2,),
        in_specs=[pl.BlockSpec((ROWS, 512), lambda i: (0, i))],
        out_specs=[half] * 2,
        out_shape=[jax.ShapeDtypeStruct((TILE, HALF), jnp.bfloat16)] * 2,
        compiler_params=limit(8),
        cost_estimate=SMALL,
        name="halves",
    )(value)


def pick_kernel(
    info, part_ref, own_ref, q_ref, k_ref, v_ref, part_out, own_out, q_out, kv_out
):
    part_out[...] = part_ref[...]
    own_out[...] = own_ref[...]
    q_out[...] = q_ref[...]
    kv_out[0:SHORT, :] = k_ref[...]
    kv_out[SHORT : 2 * SHORT, :] = v_ref[...]


def pick_columns(info, weight, q, k, v):
    wide = 2 * C_HEAD
    size = HALF // 8
    part = pl.BlockSpec(
        (size, wide), lambda i, info: (info[2] * 2 + info[1], (1 - info[5]) * 4 + info[3])
    )
    own = pl.BlockSpec((HALF // 4, wide), lambda i, info: (i, info[5] * 4 + info[3]))
    end = pl.BlockSpec((SHORT, HALF), lambda i, info: (ROWS // SHORT - 1, 0))
    first = lambda rows, columns: pl.BlockSpec((rows, columns), lambda i, info: (0, 0))
    return pl.pallas_call(
        pick_kernel,
        grid_spec=pltpu.PrefetchScalarGridSpec(
            num_scalar_prefetch=1,
            grid=(4,),
            in_specs=[part, own, end, end, end],
            out_specs=[
                first(size, wide),
                pl.BlockSpec((HALF // 4, wide), lambda i, info: (i, 0)),
                first(SHORT, HALF),
                first(2 * SHORT, HALF),
            ],
        ),
        out_shape=[
            jax.ShapeDtypeStruct((size, wide), jnp.bfloat16),
            jax.ShapeDtypeStruct((HALF, wide), jnp.bfloat16),
            jax.ShapeDtypeStruct((SHORT, HALF), jnp.bfloat16),
            jax.ShapeDtypeStruct((2 * SHORT, HALF), jnp.bfloat16),
        ],
        compiler_params=limit(8),
        cost_estimate=pl.CostEstimate(flops=1 << 30, bytes_accessed=2 * MIB, transcendentals=0),
        name="pick_columns",
    )(info, weight, weight, q, k, v)


def attend(q, pieces, store):
    scale = LOG2E / math.sqrt(HEAD)

    def fold(combine, value):
        lanes = value[:, 0:128]
        for i in range(1, value.shape[1] // 128):
            lanes = combine(lanes, value[:, i * 128 : (i + 1) * 128])
        return lanes

    scores = []
    top = None
    for keys, okay, mask in pieces:
        s = lax.dot_general(
            q, keys, (((1,), (1,)), ((), ())), preferred_element_type=jnp.float32
        )
        if mask is not None:
            s = jnp.where(mask, s, NEG)
        scores.append(s)
        high = fold(jnp.maximum, s)
        if okay is not None:
            high = jnp.where(okay, high, NEG)
        top = high if top is None else jnp.maximum(top, high)
    top = jnp.max(top, -1, keepdims=True)
    total = None
    for step, (keys, okay, mask) in enumerate(pieces):
        base = top if okay is None else jnp.where(okay, top, -NEG)
        p = jnp.exp2((scores[step] - base) * scale)
        part = fold(jnp.add, p)
        total = part if total is None else total + part
        store(step, p.astype(jnp.bfloat16))
    return jnp.sum(total, -1, keepdims=True)


def probs_kernel(
    info, q_ref, ka_ref, ko_ref, kc_ref, vo_ref, vc_ref, kl_ref, kh_ref,
    far_ref, mid_ref, near_ref, l_ref, acc_ref,
):
    index = info[0]
    core = info[1]
    valid = [index >= 2, index >= 2, index >= 1, index >= 1, None, None]
    row = lax.broadcasted_iota(jnp.int32, (TILE, TILE), 0)
    col = lax.broadcasted_iota(jnp.int32, (TILE, TILE), 1)
    lane = lax.broadcasted_iota(jnp.int32, (TILE, 128), 1)
    low, high = slice(0, TILE), slice(TILE, 2 * TILE)
    l_ref[...] = jnp.ones_like(l_ref)

    def one_head(head, carry):
        columns = pl.ds(pl.multiple_of(head * HEAD, HEAD), HEAD)
        chunks = [
            ka_ref[low, columns],
            ka_ref[high, columns],
            jnp.where(core == 0, kl_ref[:, columns], ko_ref[low, columns]),
            jnp.where(core == 0, kh_ref[:, columns], ko_ref[high, columns]),
            kc_ref[low, columns],
            kc_ref[high, columns],
        ]
        for tile in range(ROWS // TILE):
            masks = [col > row, None, None, None, col <= row]
            keys = [(chunks[tile + j], valid[tile + j], masks[j]) for j in range(5)]
            rows = slice(tile * TILE, (tile + 1) * TILE)

            def store(step, p, tile=tile, rows=rows):
                chunk = tile + step
                if chunk == 0:
                    far_ref[head] = p
                elif chunk == 1:
                    mid_ref[head, rows, :] = p
                elif chunk < 4:
                    near_ref[head, rows, (chunk - 2) * TILE : (chunk - 1) * TILE] = p
                else:
                    values = vc_ref[low if chunk == 4 else high, columns]
                    part = jnp.dot(p, values, preferred_element_type=jnp.float32)
                    if chunk == 5:
                        part = part + acc_ref[rows, columns]
                    acc_ref[rows, columns] = part

            total = attend(q_ref[rows, columns], keys, store)
            l_ref[rows, :] = jnp.where(lane == head, total, l_ref[rows, :])

        @pl.when(core == 1)
        def _():
            acc_ref[:, columns] = acc_ref[:, columns] + jnp.dot(
                near_ref[head], vo_ref[:, columns], preferred_element_type=jnp.float32
            )

        return carry

    lax.fori_loop(0, LOCAL_HEADS, one_head, 0, unroll=UNROLL)


def fine_probs(info, q, ka, ks, ko, kc, vo, vc):
    whole = pl.BlockSpec(memory_space=pltpu.VMEM)
    return pl.pallas_call(
        probs_kernel,
        in_specs=[pl.BlockSpec(memory_space=pltpu.SMEM)] + [whole] * 8,
        out_specs=[whole] * 5,
        out_shape=[
            jax.ShapeDtypeStruct((LOCAL_HEADS, TILE, TILE), jnp.bfloat16),
            jax.ShapeDtypeStruct((LOCAL_HEADS, ROWS, TILE), jnp.bfloat16),
            jax.ShapeDtypeStruct((LOCAL_HEADS, ROWS, ROWS), jnp.bfloat16),
            jax.ShapeDtypeStruct((ROWS, 128), jnp.float32),
            jax.ShapeDtypeStruct((ROWS, HALF), jnp.float32),
        ],
        compiler_params=limit(20),
        cost_estimate=SMALL,
        name="fine_probs",
    )(info, q, ka, ko, kc, vo, vc, *ks)


def far_kernel(far_ref, mid_ref, acc_ref, va_ref, out_ref):
    for head in range(LOCAL_HEADS):
        columns = slice(head * HEAD, (head + 1) * HEAD)
        mixed = acc_ref[:, columns] + jnp.dot(
            mid_ref[head], va_ref[TILE : 2 * TILE, columns], preferred_element_type=jnp.float32
        )
        out_ref[0:TILE, columns] = mixed[0:TILE, :] + jnp.dot(
            far_ref[head], va_ref[0:TILE, columns], preferred_element_type=jnp.float32
        )
        out_ref[TILE : 2 * TILE, columns] = mixed[TILE : 2 * TILE, :]


def far_mix(far, mid, acc, va):
    whole = pl.BlockSpec(memory_space=pltpu.VMEM)
    return pl.pallas_call(
        far_kernel,
        in_specs=[whole] * 4,
        out_specs=whole,
        out_shape=jax.ShapeDtypeStruct((ROWS, HALF), jnp.float32),
        compiler_params=limit(16),
        cost_estimate=pl.CostEstimate(flops=1 << 30, bytes_accessed=8 * MIB, transcendentals=0),
        name="far_mix",
    )(far, mid, acc, va)


def tail_kernel(info, _, q_ref, kv_ref, ka_ref, ko_ref, kl_ref, kh_ref, pt_ref, lt_ref):
    index, core = info[0], info[1]
    r16 = lax.broadcasted_iota(jnp.int32, (SHORT, 128), 0)
    c16 = lax.broadcasted_iota(jnp.int32, (SHORT, 128), 1)
    r512 = lax.broadcasted_iota(jnp.int32, (SHORT, ROWS), 0)
    c512 = lax.broadcasted_iota(jnp.int32, (SHORT, ROWS), 1)
    blank = jnp.zeros((128 - SHORT, HALF), jnp.bfloat16)
    first = jnp.concatenate([kv_ref[0:SHORT, :], blank], 0)
    places = [0, 128, 128 + ROWS, TAIL]
    totals = jnp.zeros((SHORT, 128), jnp.float32)
    for head in range(LOCAL_HEADS):
        columns = slice(head * HEAD, (head + 1) * HEAD)
        swapped = jnp.concatenate([kl_ref[:, columns], kh_ref[:, columns]], 0)
        kb = jnp.where(core == 0, swapped, ko_ref[:, columns])
        pieces = [
            (first[:, columns], index >= 3, (c16 > r16) & (c16 < SHORT)),
            (ka_ref[:, columns], index >= 2, None),
            (kb, index >= 1, c512 <= r512 + (ROWS - SHORT)),
        ]

        def store(step, p, head=head):
            pt_ref[head, :, places[step] : places[step + 1]] = p

        total = attend(q_ref[:, columns], pieces, store)
        totals = jnp.where(c16 == head, total, totals)
    lt_ref[...] = totals


def tail_probs(info, after, q, kv, ka, ko, ks):
    whole = pl.BlockSpec(memory_space=pltpu.VMEM)
    return pl.pallas_call(
        tail_kernel,
        in_specs=[pl.BlockSpec(memory_space=pltpu.SMEM)]
        + [pl.BlockSpec(memory_space=pl.ANY)]
        + [whole] * 6,
        out_specs=[whole] * 2,
        out_shape=[
            jax.ShapeDtypeStruct((LOCAL_HEADS, SHORT, TAIL), jnp.bfloat16),
            jax.ShapeDtypeStruct((SHORT, 128), jnp.float32),
        ],
        compiler_params=limit(16),
        cost_estimate=pl.CostEstimate(flops=1 << 30, bytes_accessed=8 * MIB, transcendentals=0),
        name="tail_probs",
    )(info, after, q, kv, ka, ko, *ks)


def mix_kernel(
    info, near_ref, l_ref, acc_ref, va_ref, vs_ref, vo_ref, pt_ref, lt_ref, kv_ref, gain_ref,
    out_ref, sent_ref,
):
    core = info[1]

    def mix(with_near):
        j = lax.broadcasted_iota(jnp.int32, (CROWS, ROWS), 0)
        r = lax.broadcasted_iota(jnp.int32, (CROWS, ROWS), 1)
        pick = jnp.where((r > SHORT * j - SHORT) & (r <= SHORT * j), 1.0, 0.0)
        pick = pick.astype(jnp.bfloat16)
        j = lax.broadcasted_iota(jnp.int32, (CROWS, SHORT), 0)
        r = lax.broadcasted_iota(jnp.int32, (CROWS, SHORT), 1)
        pick_tail = jnp.where((j == 0) & (r > 0), 1.0, 0.0).astype(jnp.bfloat16)
        share = 1.0 / l_ref[...]
        some = lt_ref[...] > 0.0
        share_tail = jnp.where(some, 1.0 / jnp.where(some, lt_ref[...], 1.0), 0.0)
        blank = jnp.zeros((128 - SHORT, HALF), jnp.bfloat16)
        first = jnp.concatenate([kv_ref[SHORT : 2 * SHORT, :], blank], 0)
        squares = jnp.zeros((CROWS, HEAD), jnp.float32)
        before_ref = vs_ref if with_near else vo_ref
        for head in range(LOCAL_HEADS):
            columns = slice(head * HEAD, (head + 1) * HEAD)
            mixed = acc_ref[:, columns]
            if with_near:
                mixed = mixed + jnp.dot(
                    near_ref[head], vs_ref[:, columns], preferred_element_type=jnp.float32
                )
            out = (mixed * share[:, head : head + 1]).astype(jnp.bfloat16)
            out_ref[:, columns] = out
            tail = jnp.dot(
                pt_ref[head, :, 0:128], first[:, columns], preferred_element_type=jnp.float32
            )
            tail = tail + jnp.dot(
                pt_ref[head, :, 128 : 128 + ROWS], va_ref[:, columns],
                preferred_element_type=jnp.float32,
            )
            tail = tail + jnp.dot(
                pt_ref[head, :, 128 + ROWS : TAIL], before_ref[:, columns],
                preferred_element_type=jnp.float32,
            )
            tail = (tail * share_tail[:, head : head + 1]).astype(jnp.bfloat16)
            sums = jnp.dot(pick, out, preferred_element_type=jnp.float32)
            sums = sums + jnp.dot(pick_tail, tail, preferred_element_type=jnp.float32)
            pooled = sums * (1.0 / SHORT)
            squares = squares + pooled * pooled
            sent_ref[:, columns] = pooled * gain_ref[:, columns]
        sent_ref[:, HALF : HALF + 128] = jnp.broadcast_to(
            jnp.sum(squares, -1, keepdims=True), (CROWS, 128)
        )

    @pl.when(core == 0)
    def _():
        mix(True)

    @pl.when(core == 1)
    def _():
        mix(False)


def fine_mix(info, near, l, acc, va, vs, vo, pt, lt, kv, gain):
    whole = pl.BlockSpec(memory_space=pltpu.VMEM)
    return pl.pallas_call(
        mix_kernel,
        in_specs=[pl.BlockSpec(memory_space=pltpu.SMEM)] + [whole] * 10,
        out_specs=[whole] * 2,
        out_shape=[
            jax.ShapeDtypeStruct((ROWS, HALF), jnp.bfloat16),
            jax.ShapeDtypeStruct((CROWS, HALF + 128), jnp.float32),
        ],
        compiler_params=limit(20),
        cost_estimate=pl.CostEstimate(flops=1 << 30, bytes_accessed=8 * MIB, transcendentals=0),
        name="fine_mix",
    )(info, near, l, acc, va, vs, vo, pt, lt, kv, gain)


def norm_kernel(own_ref, other_ref, out_ref):
    squares = own_ref[:, HALF : HALF + 1] + other_ref[:, HALF : HALF + 1]
    factor = lax.rsqrt(squares / D_FINE + EPS)
    out_ref[:, 0:HALF] = (own_ref[:, 0:HALF] * factor).astype(jnp.bfloat16)
    out_ref[:, HALF : 2 * HALF] = (other_ref[:, 0:HALF] * factor).astype(jnp.bfloat16)


def carry_kernel(_, in_ref, out_ref):
    out_ref[...] = in_ref[...]


def carried(value, after):
    whole = pl.BlockSpec(memory_space=pltpu.VMEM)
    return pl.pallas_call(
        carry_kernel,
        in_specs=[pl.BlockSpec(memory_space=pl.ANY), whole],
        out_specs=whole,
        out_shape=jax.ShapeDtypeStruct(value.shape, value.dtype),
        compiler_params=limit(4),
        cost_estimate=pl.CostEstimate(
            flops=1 << 34, bytes_accessed=32 * MIB, transcendentals=0
        ),
        name="carried",
    )(after, value)


def normalise(own, other):
    whole = pl.BlockSpec(memory_space=pltpu.VMEM)
    return pl.pallas_call(
        norm_kernel,
        in_specs=[whole] * 2,
        out_specs=whole,
        out_shape=jax.ShapeDtypeStruct((CROWS, 2 * HALF), jnp.bfloat16),
        compiler_params=limit(4),
        cost_estimate=SMALL,
        name="normalise",
    )(own, other)


def project_kernel(info, *refs):
    row_refs, own_ref, far_refs, (kv_ref, key_ref, rows_ref, w_ref) = (
        refs[0:4], refs[4], refs[5:13], refs[13:],
    )
    c, x, y = info[1], info[2], info[3]
    for k in range(4):
        begin = pl.multiple_of((y - k + 4) % 4 * CROWS, CROWS)
        rows_ref[pl.ds(begin, CROWS), :] = row_refs[k][...]
    size = HALF // 8
    for piece in range(8):
        from_x = (x - piece // 2 + 4) % 4
        from_c = c if piece % 2 == 0 else 1 - c
        begin = pl.multiple_of((from_x * 2 + from_c) * size, size)
        w_ref[pl.ds(begin, size), :] = far_refs[piece][...]
    kv = jnp.dot(rows_ref[:, 0:HALF], own_ref[...], preferred_element_type=jnp.float32)
    kv = kv + jnp.dot(
        rows_ref[:, HALF : 2 * HALF], w_ref[...], preferred_element_type=jnp.float32
    )
    kv = kv.astype(jnp.bfloat16)
    kv_ref[...] = kv
    key_ref[...] = kv[:, 0:C_HEAD]


def project(info, rows, own, far):
    whole = pl.BlockSpec(memory_space=pltpu.VMEM)
    return pl.pallas_call(
        project_kernel,
        in_specs=[pl.BlockSpec(memory_space=pltpu.SMEM)] + [whole] * 13,
        out_specs=[whole, whole],
        out_shape=[
            jax.ShapeDtypeStruct((GROUP, 2 * C_HEAD), jnp.bfloat16),
            jax.ShapeDtypeStruct((GROUP, C_HEAD), jnp.bfloat16),
        ],
        scratch_shapes=[
            pltpu.VMEM((GROUP, 2 * HALF), jnp.bfloat16),
            pltpu.VMEM((HALF, 2 * C_HEAD), jnp.bfloat16),
        ],
        compiler_params=limit(20),
        cost_estimate=SMALL,
        name="project",
    )(info, *rows, own, *far)


def split3(value):
    first = value.astype(jnp.bfloat16).astype(jnp.float32)
    rest = value - first
    second = rest.astype(jnp.bfloat16).astype(jnp.float32)
    return first, second, rest - second


def coarse_kernel(info, *refs):
    q_refs, kv_refs, (out_ref, kv_all, q_all) = refs[0:4], refs[4:12], refs[12:]
    x, z, c = info[2], info[4], info[1]
    scale = 1.0 / math.sqrt(C_HEAD)
    keys = 8 * GROUP
    for piece in range(8):
        kv_all[piece * GROUP : (piece + 1) * GROUP, :] = kv_refs[piece][...]
    for k in range(4):
        begin = pl.multiple_of((x - k + 4) % 4 * GROUP, GROUP)
        q_all[pl.ds(begin, GROUP), :] = q_refs[k][...]
    slot = lax.broadcasted_iota(jnp.int32, (1, keys), 1)
    piece = slot // GROUP
    inside = slot % GROUP
    from_z = jnp.bitwise_xor(z, piece // 2)
    from_c = jnp.where(piece % 2 == 0, c, 1 - c)
    key_pos = (
        x * 1024 + (inside // CROWS) * 256 + from_z * 64 + from_c * 32 + inside % CROWS
    )
    place = lax.broadcasted_iota(jnp.int32, (4 * GROUP, 1), 0)
    inner = place % GROUP
    pos = (place // GROUP) * 1024 + (inner // CROWS) * 256 + z * 64 + c * 32 + inner % CROWS
    lane = lax.broadcasted_iota(jnp.int32, (4 * GROUP, 128), 1)
    allowed = key_pos < jnp.maximum(pos, 1)
    s = lax.dot_general(
        q_all[...], kv_all[:, 0:C_HEAD], (((1,), (1,)), ((), ())),
        preferred_element_type=jnp.float32,
    ) * scale
    s = jnp.where(allowed, s, NEG)
    top = jnp.max(s, -1, keepdims=True)
    p = jnp.where(allowed, jnp.exp(s - top), 0.0)
    total = jnp.sum(p, -1, keepdims=True)
    mixed = jnp.dot(
        p.astype(jnp.bfloat16), kv_all[:, C_HEAD : 2 * C_HEAD],
        preferred_element_type=jnp.float32,
    )
    some = total > 0.0
    safe = jnp.where(some, total, 1.0)
    mixed = jnp.where(some, mixed / safe, 0.0).astype(jnp.bfloat16)
    level = jnp.where(some, top + jnp.log(safe), NEG)
    a, b, d = split3(level)
    extra = jnp.where(lane == 0, a, jnp.where(lane == 1, b, jnp.where(lane == 2, d, 0.0)))
    extra = extra.astype(jnp.bfloat16)
    for piece in range(16):
        rows = slice(piece * CROWS, (piece + 1) * CROWS)
        out_ref[piece, :, 0:C_HEAD] = mixed[rows, :]
        out_ref[piece, :, C_HEAD : C_HEAD + 128] = extra[rows, :]


def coarse_attend(info, queries, pairs):
    whole = pl.BlockSpec(memory_space=pltpu.VMEM)
    return pl.pallas_call(
        coarse_kernel,
        grid=(1,),
        in_specs=[pl.BlockSpec(memory_space=pltpu.SMEM)]
        + [pl.BlockSpec((GROUP, C_HEAD), lambda i: (0, 0))]
        + [whole] * 3
        + [pl.BlockSpec((GROUP, 2 * C_HEAD), lambda i: (0, 0))]
        + [whole] * 7,
        out_specs=whole,
        out_shape=jax.ShapeDtypeStruct((16, CROWS, C_HEAD + 128), jnp.bfloat16),
        scratch_shapes=[
            pltpu.VMEM((8 * GROUP, 2 * C_HEAD), jnp.bfloat16),
            pltpu.VMEM((4 * GROUP, C_HEAD), jnp.bfloat16),
        ],
        compiler_params=limit(16),
        cost_estimate=pl.CostEstimate(
            flops=4 * 4 * GROUP * 8 * GROUP * C_HEAD,
            bytes_accessed=2 * MIB,
            transcendentals=4 * GROUP * 8 * GROUP,
        ),
        name="coarse_attend",
    )(info, *queries, *pairs)


def final_kernel(part_ref, fine_ref, out_ref, done_ref, sems):
    r = lax.broadcasted_iota(jnp.int32, (ROWS, CROWS), 0)
    j = lax.broadcasted_iota(jnp.int32, (ROWS, CROWS), 1)
    spread = jnp.where(r // SHORT == j, 1.0, 0.0).astype(jnp.bfloat16)
    coarse = []
    for head in range(4):
        parts = jnp.stack([part_ref[4 * i + head] for i in range(4)]).astype(jnp.float32)
        levels = jnp.sum(parts[:, :, C_HEAD : C_HEAD + 128], -1, keepdims=True)
        top = jnp.max(levels, 0, keepdims=True)
        weights = jnp.exp(levels - top)
        total = jnp.sum(weights, 0)
        mixed = jnp.sum(parts[:, :, 0:C_HEAD] * weights, 0) / total
        coarse.append(mixed.astype(jnp.bfloat16))
    coarse = jnp.concatenate(coarse, 1)
    stores = []
    for block in range(4):
        rows = slice(block * 128, (block + 1) * 128)
        up = jnp.dot(spread[rows, :], coarse, preferred_element_type=jnp.float32)
        done_ref[rows, :] = (fine_ref[rows, :].astype(jnp.float32) + up).astype(jnp.bfloat16)
        store = pltpu.make_async_copy(
            done_ref.at[pl.ds(block * 128, 128), :],
            out_ref.at[pl.ds(block * 128, 128), :],
            sems.at[block],
        )
        store.start()
        stores.append(store)
    for store in stores:
        store.wait()


def finish(parts, fine):
    whole = pl.BlockSpec(memory_space=pltpu.VMEM)
    return pl.pallas_call(
        final_kernel,
        in_specs=[whole] * 2,
        out_specs=pl.BlockSpec(memory_space=pl.ANY),
        out_shape=jax.ShapeDtypeStruct((ROWS, HALF), jnp.bfloat16),
        scratch_shapes=[
            pltpu.VMEM((ROWS, HALF), jnp.bfloat16),
            pltpu.SemaphoreType.DMA((4,)),
        ],
        compiler_params=limit(16),
        name="finish",
    )(parts, fine)


def per_device(fine_q, fine_k, fine_v, norm_gain, short_weight):
    x, y, z, c, m = (lax.axis_index(a) for a in CTX + ("m",))
    index = ((x * 4 + y) * 4 + z) * 2 + c
    info = jnp.stack([index, c, x, y, z, m]).astype(jnp.int32)

    k2 = shifted(fine_k, 2)
    v2 = shifted(fine_v, 2)
    ko = rolled(fine_k, "c", 1)
    vo = rolled(fine_v, "c", 1)
    part, own_columns, last_q, last_kv = pick_columns(
        info, short_weight, fine_q, fine_k, fine_v
    )
    k2 = lax.optimization_barrier((k2, last_q))[0]
    tail_q = shifted(last_q, 1)
    tail_kv = shifted(last_kv, 3)
    part = rolled(part, "m", 1)
    ks = [rolled(piece, "c", 1) for piece in halves(k2)]
    far, mid, near, l, acc = fine_probs(info, fine_q, k2, ks, ko, fine_k, vo, fine_v)
    v2, l, tail_q, tail_kv = lax.optimization_barrier((v2, l, tail_q, tail_kv))
    vs = rolled(v2, "c", 1)
    acc = far_mix(far, mid, acc, v2)
    pt, lt = tail_probs(info, v2, tail_q, tail_kv, k2, ko, ks)
    fine_out, pooled = fine_mix(
        info, near, l, acc, v2, vs, vo, pt, lt, tail_kv, norm_gain[None]
    )

    part = carried(part, pooled)
    eighths = [part] + [rolled(part, "x", k) for k in (1, 2, 3)]

    other = rolled(pooled, "m", 1)
    normed = normalise(pooled, other)
    rows = [normed] + [rolled(normed, "y", k) for k in (1, 2, 3)]
    eighths = lax.optimization_barrier((*eighths, rows[1]))[:4]
    columns = []
    for piece in eighths:
        columns += [piece, rolled(piece, "c", 1)]
    kv, own_keys = project(info, rows, own_columns, columns)

    queries = [own_keys] + [rolled(own_keys, "x", k) for k in (1, 2, 3)]
    far = paired(kv, "z", 2)
    pieces = [kv, paired(kv, "z", 1), far]
    far = lax.optimization_barrier((far, queries[1], queries[2]))[0]
    pieces.append(paired(far, "z", 1))
    held = lax.optimization_barrier((*queries, *pieces[:3]))
    pairs = []
    for piece in held[4:] + (pieces[3],):
        pairs += [piece, rolled(piece, "c", 1)]
    parts = coarse_attend(info, queries, pairs)
    parts = lax.all_to_all(parts, ("x", "y"), split_axis=0, concat_axis=0, tiled=True)
    return finish(parts, fine_out)


def solution(mesh):
    grid = Mesh(mesh.devices.reshape(4, 4, 4, 2, 2), ("x", "y", "z", "c", "m"))
    rows = P(CTX, "m")
    return jax.shard_map(
        per_device,
        mesh=grid,
        in_specs=(rows, rows, rows, P("m"), P("m", None)),
        out_specs=rows,
        check_vma=False,
    )
```
